128 devices in a mesh: wide: 32 (over y, x_lo, z), narrow: 4 (over x_hi, core).
Axes of the slice: x: 4 (x_hi: 2, x_lo: 2; x = x_hi * 2 + x_lo), y: 4, z: 4, core: 2. Of those that a mesh axis runs over, the one named last changes fastest.
Arguments:
- inputs: bfloat16 [16384, 1536], P(('wide', 'narrow')), may hold values from -6 to 6
- norm_one: bfloat16 [1536], P(('wide', 'narrow')), may hold values from 0.5 to 1.5
- qkv_weight: bfloat16 [1536, 2048], P(('wide', 'narrow')), may hold values from -0.15625 to 0.15625
- qkv_bias: bfloat16 [2048], P(('wide', 'narrow')), may hold values from -3 to 3
- out_weight: bfloat16 [1536, 1536], P(('wide', 'narrow')), may hold values from -1.25 to 1.25
- norm_two: bfloat16 [1536], P(('wide', 'narrow')), may hold values from 0.5 to 1.5
- gate_weight: bfloat16 [1536, 8960], P('wide', 'narrow'), may hold values from -0.15625 to 0.15625
- up_weight: bfloat16 [1536, 8960], P('wide', 'narrow'), may hold values from -0.15625 to 0.15625
- down_weight: bfloat16 [8960, 1536], P('narrow', 'wide'), may hold values from -0.0625 to 0.0625
- lengths: int32 [32, 2], P('wide'), may hold values from 200 to 312, as said below
- offsets: int32 [32, 2], P('wide'), may hold values from 0 to 312, as said below
- cotangent: bfloat16 [16384, 1536], P(('wide', 'narrow')), may hold values from -6 to 6
Outputs:
- output: bfloat16 [16384, 1536], P(('wide', 'narrow'))
- input_grad: float32 [16384, 1536], P(('wide', 'narrow'))
- norm_one_grad: float32 [1536], P(('wide', 'narrow'))
- qkv_grad: float32 [1536, 2048], P(('wide', 'narrow'))
- qkv_bias_grad: float32 [2048], P(('wide', 'narrow'))
- out_grad: float32 [1536, 1536], P(('wide', 'narrow'))
- norm_two_grad: float32 [1536], P(('wide', 'narrow'))
- gate_grad: float32 [1536, 8960], P('wide', 'narrow')
- up_grad: float32 [1536, 8960], P('wide', 'narrow')
- down_grad: float32 [8960, 1536], P('narrow', 'wide')
The draws below stay inside these ranges and needn't reach their ends.
Inputs may be any that keep to these rules, and one draw needn't show every extreme that they name: Each shard of 512 slots holds 2 sequences in the order of their offsets, without intersection and inside the shard; one of them has 200 to 248 tokens, and at most 64 slots of a shard are padding; in some shard the two lengths are exactly 200 and 312. `offsets`: padding may stand before, between and after the sequences; in some shard the first sequence starts at slot 0, the second at slot 312, and the last ends at slot 511.
All inputs are finite; a program needn't handle non-finite values.
Results may differ from the reference program's by a relative error of at most 0.025.
Values may be sent and summed in bfloat16 or wider, within the bound.
No kernel may reach another device: no remote copies, remote signals or barrier semaphores. Data moves between devices by JAX's collectives and lax.ppermute only.
A program may use at most 192 MiB of HBM per device.

```python
import jax
import jax.numpy as jnp
from jax import lax

D = 1536
QH = 12
KVH = 2
HD = 128
FF = 8960
SHARD = 512
SHARDS = 32
TOKENS = 16384
KVD = 256


def packing(key):
    capacity = SHARD
    streams = jax.random.split(key, 6)
    least = capacity * 25 // 64
    first = jax.random.randint(streams[0], (SHARDS,), least, capacity * 31 // 64 + 1)
    spare = jax.random.randint(streams[1], (SHARDS,), 0, capacity // 8 + 1)
    chosen = jax.random.randint(streams[2], (), 0, SHARDS)
    is_chosen = jnp.arange(SHARDS) == chosen
    first = jnp.where(is_chosen, least, first)
    spare = jnp.where(is_chosen, 0, spare)
    second = capacity - first - spare
    swapped = jax.random.randint(streams[3], (SHARDS,), 0, 2) == 1
    swapped = swapped | is_chosen
    leading = jnp.where(swapped, second, first)
    trailing = jnp.where(swapped, first, second)
    before = jax.random.randint(streams[4], (SHARDS,), 0, spare + 1)
    between = jax.random.randint(streams[5], (SHARDS,), 0, spare - before + 1)
    lengths = jnp.stack([leading, trailing], axis=1).astype(jnp.int32)
    offsets = jnp.stack([before, before + leading + between], axis=1).astype(jnp.int32)
    return (lengths, offsets)


def draw_lengths(key, part):
    shared = packing(key)
    return shared[0]


def draw_offsets(key, part):
    shared = packing(key)
    return shared[1]


def block_scale(key, dims, cuts, low, top_value):
    loudness, own = 1.0, jax.random.fold_in(key, 6)
    for dim, blocks in cuts:
        draws = jnp.exp(jax.random.uniform(jax.random.fold_in(own, dim), (blocks,), jnp.float32, low / len(cuts), top_value / len(cuts)))
        loudness = loudness * jnp.repeat(draws, dims[dim] // blocks).reshape([-1 if axis == dim else 1 for axis in range(len(dims))])
    return loudness


def noise(key, shape, spread, bound, pieces=(), kind=jnp.bfloat16):
    drawn = spread * jax.random.normal(key, shape, jnp.float32)
    if pieces:
        drawn = drawn * block_scale(key, shape, pieces, -0.22, 0.18)
    return jnp.clip(drawn, -bound, bound).astype(kind)


def setup_inputs(seed: int = 0) -> dict:
    arg_keys = jax.random.split(jax.random.key(seed), 13)
    inputs = noise(arg_keys[0], (TOKENS, D), 1.0, 6.0, ((0, 128),))
    norm_one = jnp.clip(1.0 + 0.1 * jax.random.normal(arg_keys[1], (D,), jnp.float32), 0.5, 1.5).astype(jnp.bfloat16)
    qkv_weight = noise(arg_keys[2], (D, D + 2 * KVD), D ** -0.5, 0.15625, ((0, 128),))
    qkv_bias = noise(arg_keys[3], (D + 2 * KVD,), 0.5, 3.0, ((0, 128),))
    out_weight = noise(arg_keys[4], (D, D), (D // 64) ** -0.5, 1.25, ((0, 128),))
    norm_two = jnp.clip(1.0 + 0.1 * jax.random.normal(arg_keys[5], (D,), jnp.float32), 0.5, 1.5).astype(jnp.bfloat16)
    gate_weight = noise(arg_keys[6], (D, FF), D ** -0.5, 0.15625, ((0, 32), (1, 4)))
    up_weight = noise(arg_keys[7], (D, FF), D ** -0.5, 0.15625, ((0, 32), (1, 4)))
    down_weight = noise(arg_keys[8], (FF, D), FF ** -0.5, 0.0625, ((0, 4), (1, 32)))
    lengths = draw_lengths(jax.random.fold_in(arg_keys[12], 71), 0)
    offsets = draw_offsets(jax.random.fold_in(arg_keys[12], 71), 0)
    cotangent = noise(arg_keys[11], (TOKENS, D), 1.0, 6.0, ((0, 128),))
    return {"inputs": inputs, "norm_one": norm_one, "qkv_weight": qkv_weight, "qkv_bias": qkv_bias, "out_weight": out_weight, "norm_two": norm_two, "gate_weight": gate_weight, "up_weight": up_weight, "down_weight": down_weight, "lengths": lengths, "offsets": offsets, "cotangent": cotangent}


@jax.custom_vjp
def low(v):
    return lax.optimization_barrier(v.astype(jnp.bfloat16)).astype(jnp.float32)

@jax.custom_vjp
def low_back(v):
    return v

def low_keep(v):
    return (low(v), None)

def low_pass(kept, grad):
    return (grad,)

def back_keep(v):
    return (v, None)

def back_low(kept, grad):
    return (low(grad),)
low.defvjp(low_keep, low_pass)
low_back.defvjp(back_keep, back_low)
epsilon = 1e-06
rope_base = 10000.0

def matmul(left_side, right_side):
    return jnp.dot(left_side, right_side, precision=lax.Precision.HIGHEST, preferred_element_type=jnp.float32)

def layout(lengths, offsets, capacity):
    slot_index = jnp.arange(capacity, dtype=jnp.int32)[:, None]
    inside = (slot_index >= offsets[None, :]) & (slot_index < offsets[None, :] + lengths[None, :])
    labels = jnp.arange(offsets.shape[0], dtype=jnp.int32)[None, :] + 1
    number = lax.optimization_barrier(jnp.sum(jnp.where(inside, labels, 0), axis=1)).astype(jnp.int32) - 1
    position = lax.optimization_barrier(jnp.sum(jnp.where(inside, slot_index - offsets[None, :], 0), axis=1)).astype(jnp.int32)
    return (number, position)

def rope_tables(position, width):
    halfway = width // 2
    inverse = rope_base ** (-jnp.arange(halfway, dtype=jnp.float32) * 2.0 / width)
    angles = position.astype(jnp.float32)[:, None] * inverse[None, :]
    angles = jnp.concatenate([angles, angles], axis=1)
    return (jnp.cos(angles), jnp.sin(angles))

def rotate(values, cosine, sine_table):
    halfway = values.shape[-1] // 2
    turned = jnp.concatenate([-values[..., halfway:], values[..., :halfway]], axis=-1)
    return values * cosine[:, None, :] + turned * sine_table[:, None, :]

def shard_layer(rows, number, position, weights):
    norm_one, qkv_weight, qkv_bias, out_weight, norm_two, gate_weight, up_weight, down_weight = weights
    capacity = rows.shape[0]
    inverse_one = lax.rsqrt(lax.optimization_barrier(jnp.mean(rows * rows, axis=1, keepdims=True)) + epsilon)
    normed_one = low(rows * inverse_one * norm_one)
    mixed = low_back(matmul(normed_one, qkv_weight) + qkv_bias)
    cosine, sine_table = rope_tables(position, HD)
    query_heads = low(rotate(mixed[:, :D].reshape(capacity, QH, HD), cosine, sine_table))
    grouped = query_heads.reshape(capacity, KVH, QH // KVH, HD)
    key_heads = low(rotate(mixed[:, D:D + KVD].reshape(capacity, KVH, HD), cosine, sine_table))
    value_heads = low(mixed[:, D + KVD:]).reshape(capacity, KVH, HD)
    scores = jnp.einsum('qkgd,tkd->kgqt', grouped, key_heads, precision=lax.Precision.HIGHEST)
    scores = low_back(scores * HD ** (-0.5))
    slot_index = jnp.arange(capacity, dtype=jnp.int32)
    allowed = (number[:, None] == number[None, :]) & (number[:, None] >= 0) & (slot_index[None, :] <= slot_index[:, None]) | (slot_index[:, None] == slot_index[None, :])
    scores = jnp.where(allowed[None, None], scores, -1e+30)
    probs = low(jax.nn.softmax(scores, axis=-1))
    attended = jnp.einsum('kgqt,tkd->qkgd', probs, value_heads, precision=lax.Precision.HIGHEST).reshape(capacity, D)
    attended = low(low_back(attended))
    middle = rows + low_back(matmul(attended, out_weight))
    inverse_two = lax.rsqrt(lax.optimization_barrier(jnp.mean(middle * middle, axis=1, keepdims=True)) + epsilon)
    normed_two = low(middle * inverse_two * norm_two)
    gate = low_back(matmul(normed_two, gate_weight))
    upward = low_back(matmul(normed_two, up_weight))
    hidden = low(jax.nn.silu(gate) * upward)
    return middle + low_back(matmul(hidden, down_weight))

def reference(inputs, norm_one, qkv_weight, qkv_bias, out_weight, norm_two, gate_weight, up_weight, down_weight, lengths, offsets, cotangent):
    weights = tuple((weight_arg.astype(jnp.float32) for weight_arg in (norm_one, qkv_weight, qkv_bias, out_weight, norm_two, gate_weight, up_weight, down_weight)))
    source = inputs.astype(jnp.float32)

    def forward(rows_all, weight_set):
        blocks = rows_all.reshape(SHARDS, SHARD, D)

        def one_shard(shard_data):
            number, position = layout(shard_data[1], shard_data[2], SHARD)
            return shard_layer(shard_data[0], number, position, weight_set)
        return lax.map(jax.checkpoint(one_shard), (blocks, lengths, offsets)).reshape(TOKENS, D)
    result, pullback = jax.vjp(forward, source, weights)
    input_grad, weight_grads = pullback(cotangent.astype(jnp.float32))
    return (result.astype(jnp.bfloat16), input_grad, weight_grads[0], weight_grads[1], weight_grads[2], weight_grads[3], weight_grads[4], weight_grads[5], weight_grads[6], weight_grads[7])
```

```python
import jax
import jax.numpy as jnp
from jax import lax
from jax.experimental import pallas as pl
from jax.experimental.pallas import tpu as pltpu
from jax.sharding import PartitionSpec as P

D = 1536
QH = 12
KVH = 2
HD = 128
FF = 8960
GROUP = QH // KVH
HEADS = GROUP * HD
QKV = HEADS + 2 * HD
HALF = 1152
SPARE = FF // 4 - HALF
EXTRA = 128
WIDE = 32
ROWS = 48
BOTH = ("wide", "narrow")
epsilon = 1e-06
rope_base = 10000.0
bf16 = jnp.bfloat16
f32 = jnp.float32


def coords(index):
    wide, narrow = divmod(index, 4)
    y, rest = divmod(wide, 8)
    x_lo, z = divmod(rest, 4)
    x_hi, core = divmod(narrow, 2)
    return x_hi * 2 + x_lo, y, z, core


def number_of(x, y, z, core):
    x_hi, x_lo = divmod(x % 4, 2)
    return (((y % 4) * 2 + x_lo) * 4 + z % 4) * 4 + x_hi * 2 + core


def send(value, move):
    pairs = [(i, number_of(*move(*coords(i)))) for i in range(128)]
    return lax.ppermute(value, BOTH, pairs)


def other_core(value):
    return send(value, lambda x, y, z, c: (x, y, z, 1 - c))


def along_x(value, step):
    return send(value, lambda x, y, z, c: (x + step, y, z, c))


def partner_x(value):
    return send(value, lambda x, y, z, c: (x ^ 1, y, z, c))


def along_a(value, step):
    return send(value, lambda x, y, z, c: (x, y, z + step, c) if c == 0 else (x, y + step, z, c))


def along_b(value, step):
    return send(value, lambda x, y, z, c: (x, y + step, z, c) if c == 0 else (x, y, z + step, c))


def relocate(name, indices, inputs, outs, plan):
    lanes_all = max(n + at for _, reads, _ in plan for _, _, _, at, n in reads)
    dtype = inputs[0].dtype
    count_in = sum(len(r) for _, r, _ in plan)
    count_out = sum(len(w) for _, _, w in plan)

    def kernel(idx, *refs):
        ins, results = refs[: len(inputs)], refs[len(inputs) : len(inputs) + len(outs)]
        held, in_sems, out_sems = refs[len(inputs) + len(outs) :]

        def copies(k, place, rows, refs_of, sems, first, into):
            made = []
            for n, (array, slot, lane, at, lanes) in enumerate(rows):
                ref = refs_of[array]
                far = ref.at[idx[place] if slot is None else slot]
                if lanes != ref.shape[-1]:
                    far = far.at[:, pl.ds(lane, lanes)]
                near = held.at[k]
                if lanes != lanes_all:
                    near = near.at[:, pl.ds(at, lanes)]
                pair = (far, near) if into else (near, far)
                made.append(pltpu.make_async_copy(*pair, sems.at[first + n]))
            return made

        loads, first = [], 0
        for k, (place, reads, _) in enumerate(plan):
            loads.append(copies(k, place, reads, ins, in_sems, first, True))
            first += len(reads)
            for copy in loads[-1]:
                copy.start()
        stores, first = [], 0
        for k, (place, _, writes) in enumerate(plan):
            for copy in loads[k]:
                copy.wait()
            made = copies(k, place, writes, results, out_sems, first, False)
            first += len(writes)
            for copy in made:
                copy.start()
            stores += made
        for copy in stores:
            copy.wait()

    moved = sum(2 * o.size * o.dtype.itemsize for o in outs)
    held_bytes = len(plan) * ROWS * lanes_all * 2
    return pl.pallas_call(
        kernel,
        out_shape=tuple(outs),
        in_specs=[pl.BlockSpec(memory_space=pltpu.SMEM)] + [pl.BlockSpec(memory_space=pl.ANY)] * len(inputs),
        out_specs=tuple(pl.BlockSpec(memory_space=pl.ANY) for _ in outs),
        scratch_shapes=[
            pltpu.VMEM((len(plan), ROWS, lanes_all), dtype),
            pltpu.SemaphoreType.DMA((count_in,)),
            pltpu.SemaphoreType.DMA((count_out,)),
        ],
        compiler_params=pltpu.CompilerParams(vmem_limit_bytes=held_bytes + (1 << 21)),
        cost_estimate=pl.CostEstimate(flops=0, bytes_accessed=moved, transcendentals=0),
        name=name,
    )(jnp.stack(indices).astype(jnp.int32), *inputs)


class Place:
    def __init__(self):
        wide, narrow = lax.axis_index("wide"), lax.axis_index("narrow")
        self.y, rest = wide // 8, wide % 8
        self.x_lo, self.z = rest // 4, rest % 4
        self.x_hi, self.core = narrow // 2, narrow % 2
        self.narrow = narrow
        first = self.core == 0
        self.a = jnp.where(first, self.z, self.y)
        self.b = jnp.where(first, self.y, self.z)
        self.first = first

    def slot_a(self, x_lo, step):
        at = (self.a + step) % 4
        return jnp.where(self.first, x_lo * 4 + at, at * 2 + x_lo)

    def slot_b(self, j, step):
        at = (self.b + step) % 4
        return jnp.where(self.first, at * 8 + j, j * 4 + at)


STEPS = (0, -1, 1, 2)


def gather(place, name, block, widths):
    total = block.shape[-1]
    got = [block, along_a(block, 1), along_a(block, -1), along_a(block, 2)]
    plan, indices = [], []
    for k, step in enumerate(STEPS):
        for x_lo in range(2):
            plan.append((len(indices), [(k, x_lo, 0, 0, total)], [(0, None, 0, 0, total)]))
            indices.append(place.slot_a(x_lo, step))
    (piece,) = relocate(name + "_a", indices, got, [jax.ShapeDtypeStruct((8, ROWS, total), block.dtype)], plan)
    left, right = along_b(piece, 1), along_b(piece, -1)
    top, bottom = along_b(left[:4], 1), along_b(right[4:], -1)
    got = [piece, left, right, top, bottom]
    plan, indices = [], []
    for k, step in enumerate(STEPS):
        for j in range(8):
            source, slot = (k, j) if k < 3 else ((3, j) if j < 4 else (4, j - 4))
            writes, lane = [], 0
            for o, width in enumerate(widths):
                writes.append((o, None, 0, lane, width))
                lane += width
            plan.append((len(indices), [(source, slot, 0, 0, total)], writes))
            indices.append(place.slot_b(j, step))
    outs = [jax.ShapeDtypeStruct((WIDE, ROWS, w), block.dtype) for w in widths]
    return relocate(name + "_b", indices, got, outs, plan)


def add(*terms):
    return sum(t.astype(f32) for t in terms)


def scatter(place, name, parts):
    widths = [p.shape[-1] for p in parts]
    total = sum(widths)
    plan, indices = [], []
    for k, step in enumerate(STEPS):
        for j in range(8):
            target, slot = (k, j) if k < 3 else ((3, j) if j < 4 else (4, j - 4))
            reads, lane = [], 0
            for i, width in enumerate(widths):
                reads.append((i, None, 0, lane, width))
                lane += width
            plan.append((len(indices), reads, [(target, slot, 0, 0, total)]))
            indices.append(place.slot_b(j, step))
    outs = [jax.ShapeDtypeStruct((n, ROWS, total), bf16) for n in (8, 8, 8, 4, 4)]
    own, left, right, far_top, far_bottom = relocate(name + "_b", indices, parts, outs, plan)
    from_right = along_b(far_top, -1)
    from_left = along_b(far_bottom, 1)
    left = jnp.concatenate([add(left[:4], from_right).astype(bf16), left[4:]])
    right = jnp.concatenate([right[:4], add(right[4:], from_left).astype(bf16)])
    piece = add(own, along_b(left, -1), along_b(right, 1)).astype(bf16)
    plan, indices = [], []
    for k, step in enumerate(STEPS):
        for x_lo in range(2):
            plan.append((len(indices), [(0, None, 0, 0, total)], [(k, x_lo, 0, 0, total)]))
            indices.append(place.slot_a(x_lo, step))
    outs = [jax.ShapeDtypeStruct((2, ROWS, total), bf16)] * 4
    own, left, right, far = relocate(name + "_a", indices, [piece], outs, plan)
    return add(own, along_a(left, -1), along_a(right, 1), along_a(far, 2))


def gather_tokens(rows):
    mine = jnp.concatenate([rows, along_x(rows, 1), along_x(rows, -1), along_x(rows, 2)])
    return jnp.concatenate([mine, other_core(mine)])


def scatter_tokens(parts):
    count = parts.shape[0] // 2
    mine = add(parts[:count], other_core(parts[count:].astype(bf16)))
    n = count // 4
    low = mine[n:].astype(bf16)
    return add(mine[:n], along_x(low[:n], -1), along_x(low[n : 2 * n], 1), along_x(low[2 * n :], 2))


def split(place, array):
    half = array.shape[-1] // 2
    low, high = array[..., :half], array[..., half:]
    return jnp.where(place.first, low, high), jnp.where(place.first, high, low)


def join(place, mine, other):
    low, high = jnp.where(place.first, mine, other), jnp.where(place.first, other, mine)
    return jnp.concatenate([low, high], axis=-1)


def rope_tables(position):
    halfway = HD // 2
    inverse = rope_base ** (-jnp.arange(halfway, dtype=f32) * 2.0 / HD)
    angles = position.astype(f32)[:, None] * inverse[None, :]
    angles = jnp.concatenate([angles, angles], axis=1)
    return jnp.cos(angles), jnp.sin(angles)


def rotate(values, cosine, sine):
    halfway = HD // 2
    turned = jnp.concatenate([-values[..., halfway:], values[..., :halfway]], axis=-1)
    return values * cosine[:, None, :] + turned * sine[:, None, :]


def unrotate(grads, cosine, sine):
    halfway = HD // 2
    scaled = grads * sine[:, None, :]
    turned = jnp.concatenate([scaled[..., halfway:], -scaled[..., :halfway]], axis=-1)
    return grads * cosine[:, None, :] + turned


def dot(left, right, dims):
    return lax.dot_general(left, right, (dims, ((), ())), preferred_element_type=f32)


def pair_columns(place, weight):
    mine, other = split(place, weight)
    return mine, other


def attention_blocks(place, qkv_weight, out_weight, norm_one, norm_two, qkv_bias):
    q = split(place, qkv_weight[:, :D])
    k = split(place, qkv_weight[:, D : D + 256])
    v = split(place, qkv_weight[:, D + 256 :])
    o = split(place, out_weight)
    lanes = jnp.zeros((12, EXTRA), bf16)
    lanes = lanes.at[:, 0].set(norm_one).at[:, 1].set(norm_two)
    lanes = lax.dynamic_update_slice(lanes, qkv_bias[None, :], (0, 2 + 16 * place.narrow))
    mine = jnp.concatenate([q[0], k[0], v[0], lanes, o[0]], axis=1)
    other = other_core(jnp.concatenate([q[1], k[1], v[1], lanes, o[1]], axis=1))
    chip = jnp.concatenate([jnp.where(place.first, mine, other), jnp.where(place.first, other, mine)])
    width = chip.shape[-1]
    every = jnp.zeros((4, 24, width), bf16)
    x = place.x_hi * 2 + place.x_lo
    for step, value in ((0, chip), (-1, along_x(chip, 1)), (1, along_x(chip, -1)), (2, along_x(chip, 2))):
        at = (x + step) % 4
        every = lax.dynamic_update_slice(every, value[None], ((at % 2) * 2 + at // 2, 0, 0))
    return every.reshape(2, ROWS, width)


def ffn_blocks(place, gate_weight, up_weight, down_weight):
    both = []
    for weight in (gate_weight, up_weight, down_weight.T):
        low = weight[:, :HALF]
        high = jnp.pad(weight[:, HALF:], ((0, 0), (0, HALF - SPARE)))
        both.append((low, high))
    zero = place.x_lo == 0
    mine = jnp.concatenate([jnp.where(zero, low, high) for low, high in both], axis=1)
    other = partner_x(jnp.concatenate([jnp.where(zero, high, low) for low, high in both], axis=1))
    return jnp.stack([jnp.where(zero, mine, other), jnp.where(zero, other, mine)])


def per_device(
    inputs,
    norm_one,
    qkv_weight,
    qkv_bias,
    out_weight,
    norm_two,
    gate_weight,
    up_weight,
    down_weight,
    lengths,
    offsets,
    cotangent,
):
    place = Place()
    own = inputs.shape[0]
    with jax.named_scope("weights"):
        projections, lanes, out_mine = gather(
            place,
            "attn",
            attention_blocks(place, qkv_weight, out_weight, norm_one, norm_two, qkv_bias),
            (QKV, EXTRA, HEADS),
        )
        gate_full, up_full, down_full = (
            w.reshape(D, HALF)
            for w in gather(place, "ffn", ffn_blocks(place, gate_weight, up_weight, down_weight), (HALF,) * 3)
        )
        gains = lanes.reshape(D, EXTRA)[:, :2].T.astype(f32)
        gain_one, gain_two = gains[:1], gains[1:]
        bias = jnp.sum(lanes[:, :, 2:66].astype(f32), axis=1).reshape(2 * (QKV))
        bias_mine = jnp.concatenate(
            [
                lax.dynamic_slice_in_dim(bias, place.core * HEADS, HEADS),
                lax.dynamic_slice_in_dim(bias, D + place.core * HD, HD),
                lax.dynamic_slice_in_dim(bias, D + 256 + place.core * HD, HD),
            ]
        )
        projections = projections.reshape(D, QKV)
        out_mine = out_mine.reshape(D, HEADS)
        out_other = other_core(out_mine)
    with jax.named_scope("layout"):
        start = place.x_hi * 2 * own
        ramp = jnp.arange(own, dtype=jnp.int32)
        slots = jnp.concatenate([start + place.core * own + ramp, start + (1 - place.core) * own + ramp])
        away = 2 * own - start
        key_slots = jnp.concatenate([slots, slots - start + away])

        def find(at):
            inside = (at[:, None] >= offsets[0][None, :]) & (at[:, None] < (offsets[0] + lengths[0])[None, :])
            labels = jnp.arange(2, dtype=jnp.int32)[None, :] + 1
            which = jnp.sum(jnp.where(inside, labels, 0), axis=1) - 1
            return which, jnp.sum(jnp.where(inside, at[:, None] - offsets[0][None, :], 0), axis=1)

        which, position = find(slots)
        key_which, _ = find(key_slots)
        allowed = (which[:, None] == key_which[None, :]) & (which[:, None] >= 0) & (
            key_slots[None, :] <= slots[:, None]
        ) | (slots[:, None] == key_slots[None, :])
        cosine, sine = rope_tables(position)
    with jax.named_scope("projections"):
        source = inputs.astype(f32)
        inverse_one = lax.rsqrt(jnp.mean(source * source, axis=1, keepdims=True) + epsilon)
        both = jnp.concatenate([inputs, other_core(inputs)]).astype(f32)
        inverse_both = lax.rsqrt(jnp.mean(both * both, axis=1, keepdims=True) + epsilon)
        normed_one = (both * inverse_both * gain_one).astype(bf16)
        mixed = dot(normed_one, projections, ((1,), (0,))) + bias_mine[None, :]
        tokens = 2 * own
        query = rotate(mixed[:, :HEADS].reshape(tokens, GROUP, HD), cosine, sine).astype(bf16)
        key = rotate(mixed[:, HEADS : HEADS + HD].reshape(tokens, 1, HD), cosine, sine).astype(bf16)
        pair = jnp.concatenate([key.reshape(tokens, HD), mixed[:, HEADS + HD :].astype(bf16)], axis=1)
        pairs = jnp.concatenate([pair, along_x(pair, 2)])
        keys, values = pairs[:, :HD], pairs[:, HD:]
        heads = query.transpose(1, 0, 2)
    with jax.named_scope("attention"):
        scale = HD**-0.5
        scores = jnp.einsum("hqd,td->hqt", heads, keys, preferred_element_type=f32) * scale
        scores = jnp.where(allowed[None], scores, -1e30)
        raised = jnp.exp(scores - jnp.max(scores, axis=-1, keepdims=True))
        probs = raised / jnp.sum(raised, axis=-1, keepdims=True)
        probs_low = probs.astype(bf16)
        attended = (
            jnp.einsum("hqt,td->qhd", probs_low, values, preferred_element_type=f32)
            .reshape(tokens, HEADS)
            .astype(bf16)
        )
        attended_away = other_core(attended)
        attended_own = join(place, attended[:own], attended_away[own:])
        attended_next = join(place, attended[own:], attended_away[:own])
        branch = join(
            place,
            dot(attended_own, out_mine, ((1,), (0,))),
            dot(attended_own, out_other, ((1,), (0,))),
        )
        middle = source + branch
        inverse_two = lax.rsqrt(jnp.mean(middle * middle, axis=1, keepdims=True) + epsilon)
        normed_two = (middle * inverse_two * gain_two).astype(bf16)
    with jax.named_scope("ffn"):
        cotangent_all = gather_tokens(cotangent)
        normed_all = gather_tokens(normed_two)
        gate = dot(normed_all, gate_full, ((1,), (0,)))
        upward = dot(normed_all, up_full, ((1,), (0,)))
        sigmoid = jax.nn.sigmoid(gate)
        silu = gate * sigmoid
        hidden = (silu * upward).astype(bf16)
        hidden_grad = dot(cotangent_all, down_full, ((1,), (0,)))
        up_rows_grad = (hidden_grad * silu).astype(bf16)
        gate_rows_grad = (hidden_grad * upward * (sigmoid * (1.0 + gate * (1.0 - sigmoid)))).astype(bf16)
        normed_two_grad = scatter_tokens(
            dot(gate_rows_grad, gate_full, ((1,), (1,))) + dot(up_rows_grad, up_full, ((1,), (1,)))
        )
        down_wgrad = dot(cotangent_all, hidden, ((0,), (0,))).astype(bf16)
        gate_wgrad = dot(normed_all, gate_rows_grad, ((0,), (0,))).astype(bf16)
        up_wgrad = dot(normed_all, up_rows_grad, ((0,), (0,))).astype(bf16)
        ffn = scatter_tokens(dot(hidden, down_full, ((1,), (1,))))
        output = (middle + ffn).astype(bf16)
        summed = scatter(place, "ffn_grad", [w.reshape(WIDE, ROWS, HALF) for w in (gate_wgrad, up_wgrad, down_wgrad)])
        zero = place.x_lo == 0
        keep = jnp.where(zero, summed[0], summed[1])
        away = partner_x(jnp.where(zero, summed[1], summed[0]).astype(bf16)).astype(f32)
        low, high = jnp.where(zero, keep, away), jnp.where(zero, away, keep)
        ffn_grads = [
            jnp.concatenate([low[:, i * HALF : (i + 1) * HALF], high[:, i * HALF : i * HALF + SPARE]], axis=1)
            for i in range(3)
        ]
    with jax.named_scope("attention_back"):
        scaled_two = normed_two_grad * gain_two
        gain_two_grad = jnp.sum(normed_two_grad * middle * inverse_two, axis=0)
        middle_grad = (
            cotangent.astype(f32)
            + inverse_two * scaled_two
            - middle * inverse_two**3 * jnp.mean(scaled_two * middle, axis=1, keepdims=True)
        )
        branch_grad = middle_grad.astype(bf16)
        branch_mine, branch_other = split(place, branch_grad)
        branch_next = other_core(branch_other)
        attended_grad = (
            dot(branch_mine, out_mine, ((1,), (1,))) + dot(branch_other, out_other, ((1,), (1,)))
        ).astype(bf16)
        grad_mine, grad_other = split(place, attended_grad)
        attended_grads = (
            jnp.concatenate([grad_mine, other_core(grad_other)]).reshape(tokens, GROUP, HD).transpose(1, 0, 2)
        )
        out_wgrad = dot(
            jnp.concatenate([attended_own, attended_next]),
            jnp.concatenate([branch_mine, branch_next]),
            ((0,), (0,)),
        ).astype(bf16)
        prob_grad = jnp.einsum("hqd,td->hqt", attended_grads, values, preferred_element_type=f32)
        row_dot = jnp.sum(probs * prob_grad, axis=-1, keepdims=True)
        score_grad = (probs * (prob_grad - row_dot)).astype(bf16)
        query_grad = jnp.einsum("hqt,td->qhd", score_grad, keys, preferred_element_type=f32) * scale
        key_grad = jnp.einsum("hqt,hqd->td", score_grad, heads, preferred_element_type=f32) * scale
        value_grad = jnp.einsum("hqt,hqd->td", probs_low, attended_grads, preferred_element_type=f32)
        pair_grad = jnp.concatenate([key_grad, value_grad], axis=1)
        pair_grad = add(pair_grad[:tokens], along_x(pair_grad[tokens:].astype(bf16), 2))
        mixed_grad = jnp.concatenate(
            [
                unrotate(query_grad, cosine, sine).reshape(tokens, HEADS),
                unrotate(pair_grad[:, None, :HD], cosine, sine).reshape(tokens, HD),
                pair_grad[:, HD:],
            ],
            axis=1,
        ).astype(bf16)
    with jax.named_scope("projections_back"):
        bias_sum = jnp.sum(mixed_grad.astype(f32), axis=0)
        normed_one_grad = dot(mixed_grad, projections, ((1,), (1,)))
        normed_one_grad = add(normed_one_grad[:own], other_core(normed_one_grad[own:]))
        qkv_wgrad = dot(normed_one, mixed_grad, ((0,), (0,))).astype(bf16)
        scaled_one = normed_one_grad * gain_one
        gain_one_grad = jnp.sum(normed_one_grad * source * inverse_one, axis=0)
        input_grad = (
            middle_grad
            + inverse_one * scaled_one
            - source * inverse_one**3 * jnp.mean(scaled_one * source, axis=1, keepdims=True)
        )
        bias_all = jnp.zeros((2 * QKV,), f32)
        bias_all = lax.dynamic_update_slice(bias_all, bias_sum[:HEADS], (place.core * HEADS,))
        bias_all = lax.dynamic_update_slice(bias_all, bias_sum[HEADS : HEADS + HD], (D + place.core * HD,))
        bias_all = lax.dynamic_update_slice(bias_all, bias_sum[HEADS + HD :], (D + 256 + place.core * HD,))
        columns = jnp.stack([gain_one_grad, gain_two_grad], axis=1).reshape(128, 12, 2)
        spread = jnp.pad(bias_all.reshape(128, 1, 16), ((0, 0), (0, 11), (0, 0)))
        lanes_grad = jnp.pad(jnp.concatenate([columns, spread], axis=2), ((0, 0), (0, 0), (0, EXTRA - 18)))
        lanes_grad = lanes_grad.astype(bf16).reshape(WIDE, ROWS, EXTRA)
        parts = [qkv_wgrad.reshape(WIDE, ROWS, QKV), lanes_grad, out_wgrad.reshape(WIDE, ROWS, HEADS)]
        every = scatter(place, "attn_grad", parts).reshape(4, 24, QKV + EXTRA + HEADS)
        x = place.x_hi * 2 + place.x_lo

        def of(step):
            at = (x + step) % 4
            return lax.dynamic_index_in_dim(every, (at % 2) * 2 + at // 2, 0, keepdims=False)

        chip = add(
            of(0),
            along_x(of(-1).astype(bf16), -1),
            along_x(of(1).astype(bf16), 1),
            along_x(of(2).astype(bf16), 2),
        )
        keep = jnp.where(place.first, chip[:12], chip[12:])
        away = other_core(jnp.where(place.first, chip[12:], chip[:12]))
        extra = keep[:, QKV : QKV + EXTRA] + away[:, QKV : QKV + EXTRA]

        def columns_of(lo, hi):
            return join(place, keep[:, lo:hi], away[:, lo:hi])

        qkv_grad = jnp.concatenate(
            [columns_of(0, HEADS), columns_of(HEADS, HEADS + HD), columns_of(HEADS + HD, QKV)], axis=1
        )
        out_grad = columns_of(QKV + EXTRA, QKV + EXTRA + HEADS)
    return (
        output,
        input_grad,
        extra[:, 0],
        qkv_grad,
        extra[0, 2:18],
        out_grad,
        extra[:, 1],
        ffn_grads[0],
        ffn_grads[1],
        ffn_grads[2].T,
    )


def solution(mesh):
    return jax.shard_map(
        per_device,
        mesh=mesh,
        in_specs=(
            P(("wide", "narrow"), None),
            P(("wide", "narrow")),
            P(("wide", "narrow"), None),
            P(("wide", "narrow")),
            P(("wide", "narrow"), None),
            P(("wide", "narrow")),
            P("wide", "narrow"),
            P("wide", "narrow"),
            P("narrow", "wide"),
            P("wide", None),
            P("wide", None),
            P(("wide", "narrow"), None),
        ),
        out_specs=(
            P(("wide", "narrow"), None),
            P(("wide", "narrow"), None),
            P(("wide", "narrow")),
            P(("wide", "narrow"), None),
            P(("wide", "narrow")),
            P(("wide", "narrow"), None),
            P(("wide", "narrow")),
            P("wide", "narrow"),
            P("wide", "narrow"),
            P("narrow", "wide"),
        ),
        check_vma=False,
    )
```

```python
import math

import jax
import jax.numpy as jnp
from jax import lax
from jax.experimental import pallas as pl
from jax.experimental.pallas import tpu as pltpu
from jax.sharding import Mesh
from jax.sharding import PartitionSpec as P

D = 1536
QH = 12
KVH = 2
HD = 128
FF = 8960
GROUP = QH // KVH
HEADS = GROUP * HD
QKV = HEADS + 2 * HD
HALF = 1152
SPARE = FF // 4 - HALF
EXTRA = 128
WIDE = 32
ROWS = 48
WIDE_AXES = ("y", "x_lo", "z")
NARROW_AXES = ("x_hi", "core")
BOTH = WIDE_AXES + NARROW_AXES
RING = ("x_lo", "x_hi", "core")
epsilon = 1e-06
rope_base = 10000.0
bf16 = jnp.bfloat16
f32 = jnp.float32


def coords(index):
    wide, narrow = divmod(index, 4)
    y, rest = divmod(wide, 8)
    x_lo, z = divmod(rest, 4)
    x_hi, core = divmod(narrow, 2)
    return x_hi * 2 + x_lo, y, z, core


def number_of(x, y, z, core):
    x_hi, x_lo = divmod(x % 4, 2)
    return (((y % 4) * 2 + x_lo) * 4 + z % 4) * 4 + x_hi * 2 + core


def send(value, move):
    pairs = [(i, number_of(*move(*coords(i)))) for i in range(128)]
    return lax.ppermute(value, BOTH, pairs)


def other_core(value):
    return send(value, lambda x, y, z, c: (x, y, z, 1 - c))


def along_x(value, step):
    return send(value, lambda x, y, z, c: (x + step, y, z, c))


def partner_x(value):
    return send(value, lambda x, y, z, c: (x ^ 1, y, z, c))


def along_a(value, step):
    return send(value, lambda x, y, z, c: (x, y, z + step, c) if c == 0 else (x, y + step, z, c))


def along_b(value, step):
    return send(value, lambda x, y, z, c: (x, y + step, z, c) if c == 0 else (x, y, z + step, c))


class Place:
    def __init__(self):
        self.y, self.x_lo, self.z, self.x_hi, self.core = (lax.axis_index(axis) for axis in BOTH)
        self.narrow = self.x_hi * 2 + self.core
        self.x = self.x_hi * 2 + self.x_lo
        first = self.core == 0
        self.a = jnp.where(first, self.z, self.y)
        self.b = jnp.where(first, self.y, self.z)
        self.first = first

    def slot_a(self, x_lo, step):
        at = (self.a + step) % 4
        return jnp.where(self.first, x_lo * 4 + at, at * 2 + x_lo)

    def slot_b(self, j, step):
        at = (self.b + step) % 4
        return jnp.where(self.first, at * 8 + j, j * 4 + at)


STEPS = (0, -1, 1, 2)


def after(value, *others):
    return lax.optimization_barrier((value, *others))[0]


def whole(shape, dtype=bf16):
    return jax.ShapeDtypeStruct(shape, dtype)


def size(*arrays):
    return sum(math.prod(a.shape) * jnp.dtype(a.dtype).itemsize for a in arrays)


def cost(flops, *arrays):
    return pl.CostEstimate(flops=int(flops), bytes_accessed=int(size(*arrays)), transcendentals=0)


SCALARS = pl.BlockSpec(memory_space=pltpu.SMEM)
IN_VMEM = pl.BlockSpec(memory_space=pltpu.VMEM)
TOTAL = QKV + EXTRA + HEADS


def local(name, kernel, scalars, inputs, outs, scratch=(), extra=0, flops=0, wait_for=(), tables=()):
    outs = tuple(outs)
    held = sum(size(s) for s in scratch)
    n, m = len(tables) + len(inputs), len(wait_for)

    def body(at, *refs):
        kernel(at, *refs[:n], *refs[n + m :])

    return pl.pallas_call(
        body,
        out_shape=outs,
        in_specs=[SCALARS] * (1 + len(tables)) + [IN_VMEM] * len(inputs) + [pl.BlockSpec(memory_space=pl.ANY)] * m,
        out_specs=(IN_VMEM,) * len(outs),
        scratch_shapes=list(scratch),
        compiler_params=pltpu.CompilerParams(vmem_limit_bytes=int(size(*inputs, *outs) + held + extra + (2 << 20))),
        cost_estimate=cost(flops, *inputs, *outs),
        name=name,
    )(jnp.stack(scalars).astype(jnp.int32), *tables, *inputs, *wait_for)


def in_hbm(array):
    return pltpu.with_memory_space_constraint(array, pltpu.HBM)


def nothing():
    return [jnp.int32(0)]


def gather_a(place, block, wait_for):
    got = [block, *(in_hbm(along_a(block, step)) for step in (1, -1, 2))]
    slots = [place.slot_a(x_lo, step) for step in STEPS for x_lo in range(2)]
    width = QKV + EXTRA

    def kernel(at, *refs):
        out, quarter, held = refs[4:]
        for k in range(4):
            for x_lo in range(2):
                slot = at[2 * k + x_lo]
                out[slot] = refs[k][x_lo, :, :width]
                held[slot] = refs[k][x_lo, :, width:]
        for i in range(2):
            quarter[i] = held[2 * at[8] + i]

    outs = [whole((8, ROWS, width)), whole((2, ROWS, HEADS))]
    scratch = [pltpu.VMEM((8, ROWS, HEADS), bf16)]
    return local("gather_a", kernel, slots + [place.x], got, outs, scratch, 1 << 20, wait_for=wait_for)


def gather_b(place, piece, quarter):
    left, right = in_hbm(along_b(piece, 1)), in_hbm(along_b(piece, -1))
    got = [quarter, *(in_hbm(along_b(quarter, step)) for step in (1, -1, 2))]

    def forward(at, *refs):
        for k in range(4):
            for i in range(2):
                refs[6][2 * k + i] = refs[k][i]
        refs[7][...], refs[8][...] = refs[4][:4], refs[5][4:]

    outs = [whole((8, ROWS, HEADS)), whole((4, *piece.shape[1:])), whole((4, *piece.shape[1:]))]
    quarter, top, bottom = local("forward", forward, nothing(), [*got, left, right], outs)
    quarters = [quarter, in_hbm(along_x(quarter, 1)), in_hbm(along_x(quarter, -1))]
    top, bottom = in_hbm(along_b(top, 1)), in_hbm(along_b(bottom, -1))

    def kernel(at, *refs):
        main, extra = refs[5:]
        for k in range(4):
            for j in range(8):
                source, spot = (k, j) if k < 3 else (3 + j // 4, j % 4)
                main[at[8 * k + j]] = refs[source][spot, :, :QKV]
                extra[at[8 * k + j]] = refs[source][spot, :, QKV:]

    inputs = [piece, left, right, top, bottom]
    outs = [whole((WIDE, ROWS, QKV)), whole((WIDE, ROWS, EXTRA))]
    main, extra = local("gather_b", kernel, slots_b(place), inputs, outs, (), 1 << 20, wait_for=quarters[1:])
    return main, extra, quarters


def gather_x(place, quarters, wait_for):
    slots = []
    for back in (0, 1, 3, 2):
        x = (place.x - back) % 4
        slots += [place.slot_b(2 * x + i, step) for step in STEPS for i in range(2)]

    def kernel(at, *refs):
        for n in range(4):
            for k in range(8):
                refs[4][at[8 * n + k]] = refs[n][k]

    return local("gather_x", kernel, slots, quarters, [whole((WIDE, ROWS, HEADS))], wait_for=wait_for)[0]


def add(*terms):
    return sum(t.astype(f32) for t in terms)


def slots_b(place):
    return [place.slot_b(j, step) for step in STEPS for j in range(8)]


def send_b(shares):
    own, left, right, opposite = shares
    return [own, in_hbm(along_b(left, -1)), in_hbm(along_b(right, 1)), in_hbm(along_b(opposite, 2))]


def scatter_a(place, name, groups, wait_for=()):
    widths = [g[0].shape[-1] for g in groups]
    slots = [place.slot_a(x_lo, step) for step in STEPS for x_lo in range(2)]

    def kernel(at, *refs):
        outs = refs[-4:]
        for k in range(4):
            for x_lo in range(2):
                lane = 0
                for i, width in enumerate(widths):
                    total = sum(refs[4 * i + n][at[2 * k + x_lo]].astype(f32) for n in range(4))
                    outs[k][x_lo, :, lane : lane + width] = total.astype(bf16)
                    lane += width

    outs = [whole((2, ROWS, sum(widths)))] * 4
    inputs = [share for group in groups for share in group]
    own, left, right, opposite = local(name, kernel, slots, inputs, outs, wait_for=wait_for)
    return [own, along_a(left, -1), along_a(right, 1), along_a(opposite, 2)]


def deal(shares, wait_for):
    width = shares[0].shape[2]

    def kernel(at, *refs):
        for x_lo in range(2):
            rows = sum(refs[n][x_lo].astype(f32) for n in range(4))
            for k in range(4):
                refs[4][x_lo * 4 + k] = rows[12 * k : 12 * k + 12].astype(bf16)

    return local("deal", kernel, nothing(), shares, [whole((8, 12, width))], wait_for=wait_for)[0]


def arrange(got, wait_for):
    width = got.shape[2]

    def kernel(at, source, out, rows):
        for x_lo in range(2):
            for k in range(4):
                rows[x_lo, 12 * k : 12 * k + 12, :] = source[x_lo * 4 + k].astype(f32)
        out[...] = rows[...].astype(bf16)

    scratch = [pltpu.VMEM((2, ROWS, width), f32)]
    return local("arrange", kernel, nothing(), [got], [whole((2, ROWS, width))], scratch, wait_for=wait_for)[0]


def finish(place, got):
    def kernel(at, source, qkv, out, extra):
        low = sum(source[k].astype(f32) for k in range(0, 8, 2))
        high = sum(source[k].astype(f32) for k in range(1, 8, 2))
        qkv[:, :HEADS], qkv[:, HEADS:D] = low[:, :HEADS], high[:, :HEADS]
        for i in range(2):
            cut = slice(HEADS + i * HD, HEADS + (i + 1) * HD)
            at_lane = D + 2 * i * HD
            qkv[:, at_lane : at_lane + HD], qkv[:, at_lane + HD : at_lane + 2 * HD] = low[:, cut], high[:, cut]
        extra[...] = (low + high)[:, QKV : QKV + EXTRA]
        out[:, :HEADS], out[:, HEADS:] = low[:, QKV + EXTRA :], high[:, QKV + EXTRA :]

    outs = (whole((12, 2 * QKV), f32), whole((12, D), f32), whole((12, EXTRA), f32))
    return local("finish", kernel, nothing(), [got], outs)


def send_ring(rows):
    return [rows, along_x(rows, 1), along_x(rows, -1), along_x(rows, 2)]


def ring(name, got, wait_for=()):
    def kernel(at, *refs):
        for k in range(4):
            refs[4][128 * k : 128 * (k + 1)] = refs[k][...]

    return local(name, kernel, nothing(), got, [whole((512, D))], wait_for=wait_for)[0]


def scatter_ring(name, mine, other, wait_for=()):
    def kernel(at, mine_ref, other_ref, own, *rest):
        for k in range(4):
            rows = slice(128 * k, 128 * (k + 1))
            total = mine_ref[rows].astype(f32) + other_ref[rows].astype(f32)
            if k == 0:
                own[...] = total
            else:
                rest[k - 1][...] = total.astype(bf16)

    outs = [whole((128, D), f32)] + [whole((128, D))] * 3
    own, left, right, opposite = local(name, kernel, nothing(), [mine, other], outs, wait_for=wait_for)
    return [own, along_x(left, -1), along_x(right, 1), along_x(opposite, 2)]


def select(first, low, high):
    return jnp.where(first, low.astype(f32), high.astype(f32))


def turn(values, cosine, sine):
    return values * cosine + pltpu.roll(values, HD // 2, 1) * sine


def project(place, inputs, inputs_away, projections, lanes, cosine, sine, wait_for):
    tokens = 256

    def kernel(at, own, away, weight, lane_ref, cos_ref, sin_ref, normed, query, pair, gains):
        first = at[0] == 0
        table = lane_ref[...].astype(f32)
        gains_all = jnp.transpose(table.reshape(D, EXTRA))
        gains[...] = gains_all[:8]
        sums = jnp.sum(table, axis=1)
        left, right = pltpu.roll(sums, EXTRA - 2, 1), pltpu.roll(sums, 62, 1)
        lane = lax.broadcasted_iota(jnp.int32, (1, EXTRA), 1)

        def bias_at(low, high):
            def tile(j):
                return jnp.where(lane < 64, left[2 * j : 2 * j + 1], right[2 * j + 1 : 2 * j + 2])

            return jnp.where(first, tile(low), tile(high))

        for half, ref in enumerate((own, away)):
            rows = slice(128 * half, 128 * (half + 1))
            x = ref[...].astype(f32)
            inverse = lax.rsqrt(jnp.mean(x * x, axis=1, keepdims=True) + epsilon)
            normed[rows] = (x * inverse * gains_all[:1]).astype(bf16)
        cos, sin = cos_ref[...], sin_ref[...]
        mixed = jnp.dot(normed[...], weight[...], preferred_element_type=f32)
        for h in range(GROUP):
            values = mixed[:, h * HD : (h + 1) * HD] + bias_at(h, GROUP + h)
            query[h] = turn(values, cos, sin).astype(bf16)
        key = mixed[:, HEADS : HEADS + HD] + bias_at(12, 13)
        pair[:, :HD] = turn(key, cos, sin).astype(bf16)
        pair[:, HD:] = (mixed[:, HEADS + HD :] + bias_at(14, 15)).astype(bf16)

    outs = [whole((tokens, D)), whole((GROUP, tokens, HD)), whole((tokens, 2 * HD)), whole((8, D), f32)]
    inputs = [inputs, inputs_away, projections, lanes, cosine, sine]
    flops = 2 * tokens * D * QKV
    return local("project", kernel, [place.core], inputs, outs, extra=8 << 20, flops=flops, wait_for=wait_for)


def attend(place, query, pair, pair_away, lengths, offsets, wait_for):
    tokens = 256
    scale = HD**-0.5

    def kernel(at, offset, length, query_ref, own, away, probs, attended):
        core, start = at[0], at[1]
        off_a, off_b, len_a, len_b = offset[0, 0], offset[0, 1], length[0, 0], length[0, 1]

        def slot_of(index, base):
            other = index >= 128
            return base + jnp.where(other, (1 - core) * 128 - 128, core * 128) + index

        def which(slot):
            in_a = (slot >= off_a) & (slot < off_a + len_a)
            in_b = (slot >= off_b) & (slot < off_b + len_b)
            return jnp.where(in_a, 0, jnp.where(in_b, 1, -1))

        rows = slot_of(lax.broadcasted_iota(jnp.int32, (tokens, 1), 0), start)
        lane = lax.broadcasted_iota(jnp.int32, (1, 2 * tokens), 1)
        columns = jnp.where(lane < tokens, slot_of(lane, start), slot_of(lane - tokens, tokens - start))
        number, key_number = which(rows), which(columns)
        allowed = ((number == key_number) & (number >= 0) & (columns <= rows)) | (columns == rows)
        keys = jnp.concatenate([own[:, :HD], away[:, :HD]], axis=0)
        values = jnp.concatenate([own[:, HD:], away[:, HD:]], axis=0)
        for h in range(GROUP):
            scores = lax.dot_general(query_ref[h], keys, (((1,), (1,)), ((), ())), preferred_element_type=f32) * scale
            scores = jnp.where(allowed, scores, -1e30)
            raised = jnp.exp(scores - jnp.max(scores, axis=1, keepdims=True))
            result = raised * (1.0 / jnp.sum(raised, axis=1, keepdims=True))
            probs[h] = result
            attended[:, h * HD : (h + 1) * HD] = jnp.dot(
                result.astype(bf16), values, preferred_element_type=f32
            ).astype(bf16)

    scalars, tables = [place.core, place.x_hi * tokens], [offsets, lengths]
    outs = [whole((GROUP, tokens, 2 * tokens), f32), whole((tokens, HEADS))]
    flops = 8 * GROUP * tokens * tokens * HD
    return local(
        "attend", kernel, scalars, [query, pair, pair_away], outs, (), 6 << 20, flops, wait_for, tables
    )


def branch(place, attended, attended_away, out_mine, out_other, inputs, gains, wait_for):
    def kernel(at, mine, away, weight, weight_away, x_ref, gain, middle, normed, every):
        first = at[0] == 0
        for half, (a, b) in enumerate(((mine[:128], away[128:]), (mine[128:], away[:128]))):
            rows = slice(128 * half, 128 * (half + 1))
            every[rows, :HEADS] = select(first, a, b).astype(bf16)
            every[rows, HEADS:] = select(first, b, a).astype(bf16)
        left = every[:128]
        a = jnp.dot(left, weight[...], preferred_element_type=f32)
        b = jnp.dot(left, weight_away[...], preferred_element_type=f32)
        x = x_ref[...].astype(f32)
        low = x[:, :HEADS] + jnp.where(first, a, b)
        high = x[:, HEADS:] + jnp.where(first, b, a)
        middle[:, :HEADS], middle[:, HEADS:] = low, high
        squares = jnp.sum(low * low, axis=1, keepdims=True) + jnp.sum(high * high, axis=1, keepdims=True)
        inverse = lax.rsqrt(squares * (1.0 / D) + epsilon)
        normed[:, :HEADS] = (low * inverse * gain[1:2, :HEADS]).astype(bf16)
        normed[:, HEADS:] = (high * inverse * gain[1:2, HEADS:]).astype(bf16)

    outs = [whole((128, D), f32), whole((128, D)), whole((256, D))]
    inputs = [attended, attended_away, out_mine, out_other, inputs, gains]
    return local(
        "branch", kernel, [place.core], inputs, outs, extra=6 << 20, flops=2 * 128 * D * D, wait_for=wait_for
    )


def branch_back(place, shares, middle, gains, cotangent, out_mine, out_other, wait_for):
    def kernel(at, own, left, right, opposite, mid_ref, gain, cot, weight, weight_away, grad, gain_grad, mine, heads, away):
        first = at[0] == 0
        total = own[...] + left[...].astype(f32) + right[...].astype(f32) + opposite[...].astype(f32)
        mid = mid_ref[...]
        inverse = lax.rsqrt(jnp.mean(mid * mid, axis=1, keepdims=True) + epsilon)
        scaled = total * gain[1:2]
        mean = jnp.mean(scaled * mid, axis=1, keepdims=True)
        result = cot[...].astype(f32) + inverse * scaled - mid * (inverse * inverse * inverse * mean)
        grad[...] = result
        gain_grad[...] = jnp.sum(total * mid * inverse, axis=0, keepdims=True)
        low, high = result[:, :HEADS], result[:, HEADS:]
        mine[...] = jnp.where(first, low, high).astype(bf16)
        away[:, :HEADS] = jnp.where(first, high, low).astype(bf16)
        back = lax.dot_general(mine[...], weight[...], (((1,), (1,)), ((), ())), preferred_element_type=f32)
        back += lax.dot_general(
            away[:, :HEADS], weight_away[...], (((1,), (1,)), ((), ())), preferred_element_type=f32
        )
        low, high = back[:, :HEADS], back[:, HEADS:]
        heads[...] = jnp.where(first, low, high).astype(bf16)
        away[:, HEADS:] = jnp.where(first, high, low).astype(bf16)

    outs = [whole((128, D), f32), whole((1, D), f32), whole((128, HEADS)), whole((128, HEADS)), whole((128, D))]
    inputs = [*shares, middle, gains, cotangent, out_mine, out_other]
    return local(
        "branch_back", kernel, [place.core], inputs, outs, extra=8 << 20, flops=2 * 128 * D * D, wait_for=wait_for
    )


def attend_back(probs, query, pair, pair_away, heads, received, cosine, sine):
    tokens = 256
    scale = HD**-0.5

    def kernel(at, probs_ref, query_ref, own, away, mine, others, cos_ref, sin_ref, mixed, pair_own, pair_send, total):
        keys = jnp.concatenate([own[:, :HD], away[:, :HD]], axis=0)
        values = jnp.concatenate([own[:, HD:], away[:, HD:]], axis=0)
        cos, sin = cos_ref[...], sin_ref[...]
        for h in range(GROUP):
            cut = slice(h * HD, (h + 1) * HD)
            grad = jnp.concatenate([mine[:, cut], others[:, HEADS + h * HD : HEADS + (h + 1) * HD]], axis=0)
            p = probs_ref[h]
            by_prob = lax.dot_general(grad, values, (((1,), (1,)), ((), ())), preferred_element_type=f32)
            row = jnp.sum(p * by_prob, axis=1, keepdims=True)
            by_score = (p * (by_prob - row)).astype(bf16)
            by_query = jnp.dot(by_score, keys, preferred_element_type=f32) * scale
            mixed[:, cut] = turn(by_query, cos, -sin).astype(bf16)
            by_key = lax.dot_general(by_score, query_ref[h], (((0,), (0,)), ((), ())), preferred_element_type=f32)
            by_value = lax.dot_general(p.astype(bf16), grad, (((0,), (0,)), ((), ())), preferred_element_type=f32)
            if h == 0:
                total[:, :HD], total[:, HD:] = by_key * scale, by_value
            else:
                total[:, :HD] += by_key * scale
                total[:, HD:] += by_value
        pair_own[...] = total[:tokens]
        pair_send[...] = total[tokens:].astype(bf16)

    outs = [whole((tokens, HEADS)), whole((tokens, 2 * HD), f32), whole((tokens, 2 * HD))]
    inputs = [probs, query, pair, pair_away, heads, received, cosine, sine]
    scratch = [pltpu.VMEM((2 * tokens, 2 * HD), f32)]
    flops = 20 * GROUP * tokens * tokens * HD
    return local("attend_back", kernel, nothing(), inputs, outs, scratch, extra=8 << 20, flops=flops)


def out_back(every, mine, received, wait_for):
    def kernel(at, every_ref, mine_ref, others, out):
        both = jnp.concatenate([mine_ref[...], others[:, :HEADS]], axis=0)
        for r in range(0, D, 384):
            out[r : r + 384] = lax.dot_general(
                every_ref[:, r : r + 384], both, (((0,), (0,)), ((), ())), preferred_element_type=f32
            ).astype(bf16)

    flops = 2 * 256 * D * HEADS
    inputs = [every, mine, received]
    return local("out_back", kernel, nothing(), inputs, [whole((D, HEADS))], (), 6 << 20, flops, wait_for)[0]


def project_back(place, mixed, pair_own, pair_received, cosine, sine, projections, normed, inputs, inputs_away, two, out):
    width = QKV + EXTRA

    def kernel(at, mix, own_ref, got, cos_ref, sin_ref, weight, norm_ref, x_ref, x_away, two_ref, out_ref, mine, away, *rest):
        shares, (held, grads, rows) = rest[:4], rest[4:]
        core = at[32]
        total = own_ref[...] + got[...].astype(f32)
        grads[:, :HEADS] = mix[...]
        grads[:, HEADS : HEADS + HD] = turn(total[:, :HD], cos_ref[...], -sin_ref[...]).astype(bf16)
        grads[:, HEADS + HD :] = total[:, HD:].astype(bf16)
        one = jnp.zeros((1, D), f32)
        for half, (x_from, ref) in enumerate(((x_ref, mine), (x_away, away))):
            part = lax.dot_general(
                grads[128 * half : 128 * (half + 1)],
                weight[...],
                (((1,), (1,)), ((), ())),
                preferred_element_type=f32,
            )
            ref[...] = part
            x = x_from[...].astype(f32)
            inverse = lax.rsqrt(jnp.mean(x * x, axis=1, keepdims=True) + epsilon)
            one += jnp.sum(part * x * inverse, axis=0, keepdims=True)
        for r in range(0, D, 384):
            part = lax.dot_general(
                norm_ref[:, r : r + 384], grads[...], (((0,), (0,)), ((), ())), preferred_element_type=f32
            ).astype(bf16)
            held[r // ROWS : r // ROWS + 8, :, :QKV] = part.reshape(8, ROWS, QKV)
        rows[...] = jnp.zeros((EXTRA, D), f32)
        rows[0:1], rows[1:2] = one, two_ref[...]
        held[:, :, QKV:] = jnp.transpose(rows[...]).reshape(WIDE, ROWS, EXTRA).astype(bf16)
        bias = jnp.sum(grads[...].astype(f32), axis=0, keepdims=True)
        lane = lax.broadcasted_iota(jnp.int32, (ROWS, EXTRA), 1)
        row = lax.broadcasted_iota(jnp.int32, (ROWS, EXTRA), 0)
        spot = (lane >= 2) & (lane < 66) & (lax.rem(row, 12) == 0)
        for i in range(8):
            tile = bias[:, i * HD : (i + 1) * HD]
            base = 12 * core + 2 * i if i < GROUP else 24 + 4 * (i - GROUP) + 2 * core
            for odd, shift in ((0, 2), (1, 66)):
                moved = pltpu.roll(tile, shift, 1)
                before = held[base + odd, :, QKV:].astype(f32)
                held[base + odd, :, QKV:] = jnp.where(spot, moved, before).astype(bf16)
        for k in range(4):
            for j in range(8):
                shares[k][j, :, :width] = held[at[8 * k + j]]
                shares[k][j, :, width:] = out_ref[at[8 * k + j]]

    outs = [whole((128, D), f32)] * 2 + [whole((8, ROWS, TOTAL))] * 4
    scratch = [pltpu.VMEM((WIDE, ROWS, width), bf16), pltpu.VMEM((256, QKV), bf16), pltpu.VMEM((EXTRA, D), f32)]
    inputs = [mixed, pair_own, pair_received, cosine, sine, projections, normed, inputs, inputs_away, two, out]
    scalars = slots_b(place) + [place.core]
    flops = 4 * 256 * D * QKV
    mine, away, *shares = local("project_back", kernel, scalars, inputs, outs, scratch, 10 << 20, flops)
    return mine, away, shares


def prepare_attention(place, qkv_weight, out_weight, norm_one, norm_two, qkv_bias):
    def kernel(at, qkv, out, one, two, bias, result):
        narrow = at[0]
        lane = lax.broadcasted_iota(jnp.int32, (12, EXTRA), 1)
        row = lax.broadcasted_iota(jnp.int32, (12, EXTRA), 0)
        diagonal = lax.broadcasted_iota(jnp.int32, (12, 12), 0) == lax.broadcasted_iota(jnp.int32, (12, 12), 1)

        def column(gain):
            return jnp.sum(jnp.where(diagonal, gain[...].astype(f32), 0.0), axis=1, keepdims=True)

        extra = jnp.where(lane == 0, column(one), 0.0) + jnp.where(lane == 1, column(two), 0.0)
        spread = jnp.concatenate([bias[...].astype(f32)] * 8, axis=1)
        base = 2 + 16 * narrow
        shifted = pltpu.roll(spread, 2, 1)
        extra = extra + jnp.where((row == 0) & (lane >= base) & (lane < base + 16), shifted, 0.0)
        extra = extra.astype(bf16)
        for k in range(8):
            c = k % 2
            result[k, :, :HEADS] = qkv[:, c * HEADS : (c + 1) * HEADS]
            for i in range(2):
                at_lane = D + (2 * i + c) * HD
                result[k, :, HEADS + i * HD : HEADS + (i + 1) * HD] = qkv[:, at_lane : at_lane + HD]
            result[k, :, QKV : QKV + EXTRA] = extra
            result[k, :, QKV + EXTRA :] = out[:, c * HEADS : (c + 1) * HEADS]

    inputs = [
        in_hbm(a)
        for a in (qkv_weight, out_weight, norm_one.reshape(1, 12), norm_two.reshape(1, 12), qkv_bias.reshape(1, 16))
    ]
    return local("prepare_attention", kernel, [place.narrow], inputs, [whole((8, 12, TOTAL))])[0]


def prepare_ffn(place, weights):
    def kernel(at, gate, up, down, mine, other):
        zero = at[0] == 0
        for i, weight in enumerate((gate, up, down)):
            low = weight[:, :HALF].astype(f32)
            high = jnp.concatenate([weight[:, HALF:].astype(f32), jnp.zeros((ROWS, HALF - SPARE), f32)], axis=1)
            mine[:, i * HALF : (i + 1) * HALF] = jnp.where(zero, low, high).astype(bf16)
            other[:, i * HALF : (i + 1) * HALF] = jnp.where(zero, high, low).astype(bf16)

    outs = (whole((ROWS, 3 * HALF)),) * 2
    return local("prepare_ffn", kernel, [place.x_lo], [in_hbm(w) for w in weights], outs)


def by_x_lo(place, mine, other, wait_for):
    def kernel(at, mine_ref, other_ref, out):
        out[at[0]] = mine_ref[...]
        out[1 - at[0]] = other_ref[...]

    return local("by_x_lo", kernel, [place.x_lo], [mine, other], [whole((2, *mine.shape))], wait_for=wait_for)[0]


def part_x_lo(place, both):
    def kernel(at, source, mine, other):
        mine[...] = source[at[0]]
        other[...] = source[1 - at[0]]

    return local("part_x_lo", kernel, [place.x_lo], [both], [whole(both.shape[1:])] * 2)


def finish_ffn(place, keep, gone):
    def kernel(at, keep_ref, gone_ref, *outs):
        zero = at[0] == 0
        for i, out in zip((1, 0, 2), outs):
            a = keep_ref[:, i * HALF : (i + 1) * HALF].astype(f32)
            b = gone_ref[:, i * HALF : (i + 1) * HALF].astype(f32)
            out[:, :HALF] = jnp.where(zero, a, b)
            out[:, HALF:] = jnp.where(zero, b, a)[:, :SPARE]

    return local("finish_ffn", kernel, [place.x_lo], [keep, gone], [whole((ROWS, HALF + SPARE), f32)] * 3)


def ffn_rows(x_mine, x_other, c_mine, c_other, gathered):
    half, step = x_mine.shape[0], 256
    chunks = 2 * half // step
    tokens = (x_mine, x_other, c_mine, c_other)

    def kernel(*refs):
        far_tokens, source, rows, mine, other, down = refs[:4], *refs[4:9]
        weights, held, near, grads, sems, token_sems, out_sems, row_sems, grad_sems = refs[9:]
        loads = [[] for _ in range(3)]
        token_loads = [pltpu.make_async_copy(far_tokens[i], near.at[i], token_sems.at[i]) for i in range(4)]

        def load_weight(m):
            for y in range(4):
                for x_lo in range(2):
                    load = pltpu.make_async_copy(
                        source.at[y, :, x_lo, :, pl.ds(m * HALF, HALF)],
                        weights.at[m, pl.ds(y * 8 + x_lo * 4, 4)],
                        sems.at[(m * 4 + y) * 2 + x_lo],
                    )
                    load.start()
                    loads[m].append(load)

        token_loads[0].start()
        load_weight(0)
        load_weight(1)
        token_loads[2].start()
        load_weight(2)
        token_loads[1].start()
        token_loads[3].start()
        stores = []

        def store(*copy):
            stores.append(pltpu.make_async_copy(*copy))
            stores[-1].start()

        for n in range(chunks):
            side = n * step // half
            here = slice(n * step % half, n * step % half + step)
            there = slice(n * step, n * step + step)
            products = []
            for m, i in ((0, side), (1, side), (2, 2 + side)):
                if n * step % half == 0 and m != 1:
                    token_loads[i].wait()
                if n == 0:
                    for load in loads[m]:
                        load.wait()
                products.append(jnp.dot(near[i, here], weights[m].reshape(D, HALF), preferred_element_type=f32))
            if n == 0:
                store(weights.at[2], down, out_sems.at[0])
            gate, upward, grad = products
            sigmoid = 1.0 / (1.0 + jnp.exp(-gate))
            silu = gate * sigmoid
            held[0, there] = (grad * upward * (sigmoid * (1.0 + gate * (1.0 - sigmoid)))).astype(bf16)
            held[1, there] = (grad * silu).astype(bf16)
            held[2, there] = (silu * upward).astype(bf16)
            for i in range(3):
                store(held.at[i, there], rows.at[i, there], row_sems.at[3 * n + i])
            back = sum(
                lax.dot_general(
                    held[m, there], weights[m].reshape(D, HALF), (((1,), (1,)), ((), ())), preferred_element_type=f32
                )
                for m in range(2)
            )
            grads[there] = back.astype(bf16)
            store(grads.at[there], (mine, other)[side].at[here], grad_sems.at[n])
        for copy in stores:
            copy.wait()

    outs = (
        pltpu.HBM((3, 2 * half, HALF), bf16),
        pltpu.HBM((half, D), bf16),
        pltpu.HBM((half, D), bf16),
        pltpu.HBM((WIDE, ROWS, HALF), bf16),
    )
    return pl.pallas_call(
        kernel,
        out_shape=outs,
        in_specs=[pl.BlockSpec(memory_space=pl.ANY)] * 5,
        out_specs=(pl.BlockSpec(memory_space=pl.ANY),) * 4,
        scratch_shapes=[
            pltpu.VMEM((3, WIDE, ROWS, HALF), bf16),
            pltpu.VMEM((3, 2 * half, HALF), bf16),
            pltpu.VMEM((4, half, D), bf16),
            pltpu.VMEM((2 * half, D), bf16),
            pltpu.SemaphoreType.DMA((24,)),
            pltpu.SemaphoreType.DMA((4,)),
            pltpu.SemaphoreType.DMA((1,)),
            pltpu.SemaphoreType.DMA((3 * chunks,)),
            pltpu.SemaphoreType.DMA((chunks,)),
        ],
        compiler_params=pltpu.CompilerParams(vmem_limit_bytes=40 << 20),
        cost_estimate=cost(20 * half * D * HALF, *tokens, gathered),
        name="ffn_rows",
    )(*(in_hbm(t) for t in tokens), gathered)


def ffn_back(name, rows, parts, weights, half, wait_for=()):
    count, pairs = rows.shape[1] // 2, len(parts)
    n, cut = 3, D // 3

    def kernel(*refs):
        out = refs[-1]
        for r in range(0, count, 256):
            out[r : r + 256] = sum(
                lax.dot_general(
                    refs[i][0, r : r + 256], refs[pairs + i][...], (((1,), (1,)), ((), ())), preferred_element_type=f32
                )
                for i in range(pairs)
            ).astype(bf16)

    out = whole((count, D))
    return pl.pallas_call(
        kernel,
        grid=(n,),
        out_shape=out,
        in_specs=[pl.BlockSpec((1, count, HALF), lambda j, m=m: (m, half, 0)) for m in parts]
        + [pl.BlockSpec((cut, HALF), lambda j: (j, 0))] * pairs
        + [pl.BlockSpec(memory_space=pl.ANY)] * len(wait_for),
        out_specs=pl.BlockSpec((count, cut), lambda j: (0, j)),
        compiler_params=pltpu.CompilerParams(vmem_limit_bytes=20 << 20),
        cost_estimate=cost(2 * pairs * count * D * HALF, out, out, out),
        name=name,
    )(*([in_hbm(rows)] * pairs), *(in_hbm(w) for w in weights), *wait_for)


def weight_grads(name, x_mine, x_other, rows, m, start, lanes, at, before=(), wait_for=()):
    assert start % lanes == 0 and at % lanes == 0
    count = x_mine.shape[0]

    def kernel(a, b, r, *refs):
        out, mark = refs[-2:]
        left = jnp.concatenate([a[...], b[...]], axis=0)
        part = lax.dot_general(left, r[0], (((0,), (0,)), ((), ())), preferred_element_type=f32).astype(bf16)
        for w in range(WIDE):
            y, rest = divmod(w, 8)
            x_lo, z = divmod(rest, 4)
            out[y * 8 + z * 2 + x_lo] = part[w * ROWS : (w + 1) * ROWS]
        mark[...] = jnp.zeros((8, 128), f32)

    x_spec = pl.BlockSpec((count, D), lambda i: (0, 0))
    more = [*before, *wait_for]
    return pl.pallas_call(
        kernel,
        grid=(1,),
        out_shape=(pltpu.HBM((WIDE, ROWS, 3 * HALF), bf16), whole((8, 128), f32)),
        in_specs=[x_spec, x_spec, pl.BlockSpec((1, 2 * count, lanes), lambda i: (m, 0, start // lanes))]
        + [pl.BlockSpec(memory_space=pl.ANY)] * len(more),
        out_specs=(
            pl.BlockSpec((WIDE, ROWS, lanes), lambda i: (0, 0, at // lanes)),
            pl.BlockSpec((8, 128), lambda i: (0, 0)),
        ),
        input_output_aliases={3: 0} if before else {},
        compiler_params=pltpu.CompilerParams(vmem_limit_bytes=40 << 20),
        cost_estimate=cost(4 * count * D * lanes, rows),
        name=name,
    )(*(in_hbm(v) for v in (x_mine, x_other, rows)), *before, *wait_for)


def rope_tables(position):
    halfway = HD // 2
    inverse = rope_base ** (-jnp.arange(halfway, dtype=f32) * 2.0 / HD)
    angles = position.astype(f32)[:, None] * inverse[None, :]
    angles = jnp.concatenate([angles, angles], axis=1)
    return jnp.cos(angles), jnp.sin(angles)


def dot(left, right, dims):
    return lax.dot_general(left, right, (dims, ((), ())), preferred_element_type=f32)


def per_device(
    inputs,
    norm_one,
    qkv_weight,
    qkv_bias,
    out_weight,
    norm_two,
    gate_weight,
    up_weight,
    down_weight,
    lengths,
    offsets,
    cotangent,
):
    place = Place()
    own = inputs.shape[0]
    zero = place.x_lo == 0
    with jax.named_scope("weights"):
        mine, other = prepare_ffn(place, (gate_weight, up_weight, down_weight.T))
        other = partner_x(other)
        blocks = prepare_attention(place, qkv_weight, out_weight, norm_one, norm_two, qkv_bias)
        blocks = lax.all_to_all(blocks, RING, 0, 0, tiled=True)
        inputs_away = other_core(inputs)
        got = send_ring(cotangent)
        piece, quarter = gather_a(place, arrange(blocks, [inputs_away]), got[1:3])
        block = by_x_lo(place, mine, other, [piece])
        gathered = lax.all_gather(block.reshape(2 * ROWS, 3 * HALF), ("y", "z"), axis=0, tiled=True)
        projections, lanes, quarters = gather_b(place, piece, quarter)
        projections = projections.reshape(D, QKV)
    with jax.named_scope("layout"):
        start = place.x_hi * 2 * own
        ramp = jnp.arange(own, dtype=jnp.int32)
        slots = jnp.concatenate([start + place.core * own + ramp, start + (1 - place.core) * own + ramp])
        inside = (slots[:, None] >= offsets[0][None, :]) & (slots[:, None] < (offsets[0] + lengths[0])[None, :])
        position = jnp.sum(jnp.where(inside, slots[:, None] - offsets[0][None, :], 0), axis=1)
        cosine, sine = rope_tables(position)
        sine = jnp.where(jnp.arange(HD)[None, :] < HD // 2, -sine, sine)
    with jax.named_scope("attention"):
        normed_one, query, pair, gains = project(
            place, inputs, inputs_away, projections, lanes, cosine, sine, []
        )
        cotangent_mine = ring("ring_cotangent", [in_hbm(v) for v in got], [pair])
        cotangent_other = other_core(cotangent_mine)
        pair_away = along_x(pair, 2)
        quarters.append(in_hbm(along_x(quarters[0], 2)))
        probs, attended = attend(place, query, pair, pair_away, lengths, offsets, quarters[3:])
        out_mine = gather_x(place, quarters, [pair]).reshape(D, HEADS)
        out_other = other_core(out_mine)
        middle, normed_two, every = branch(
            place, attended, other_core(attended), out_mine, out_other, inputs, gains, got[3:]
        )
    with jax.named_scope("ffn"):
        normed_mine = ring("ring_normed", [in_hbm(v) for v in send_ring(normed_two)])
        normed_other = other_core(normed_mine)
        gathered = in_hbm(gathered.reshape(4, 4, 2, ROWS, 3 * HALF))
        rows, grad_mine, grad_other, down_full = ffn_rows(
            normed_mine, normed_other, cotangent_mine, cotangent_other, gathered
        )
        down_full = down_full.reshape(D, HALF)
        wgrad, mark = weight_grads("gate_grad", normed_mine, normed_other, rows, 0, 0, HALF, HALF)
        shares = scatter_ring("ring_grad", in_hbm(grad_mine), in_hbm(other_core(grad_other)), [mark])
        wgrad, _ = weight_grads("down_grad", cotangent_mine, cotangent_other, rows, 2, 0, HALF, 2 * HALF, [wgrad], [shares[0]])
        wgrad, _ = weight_grads("up_grad_low", normed_mine, normed_other, rows, 1, 0, 768, 0, [wgrad])
        wgrad, _ = weight_grads("up_grad_high", normed_mine, normed_other, rows, 1, 768, 384, 768, [wgrad], shares[1:])
        summed = lax.psum_scatter(wgrad.reshape(D, 3 * HALF), ("y", "z"), scatter_dimension=0, tiled=True)
    with jax.named_scope("attention_back"):
        middle_grad, two_grad, branch_mine, heads, away = branch_back(
            place, [in_hbm(v) for v in shares], in_hbm(middle), gains, cotangent, in_hbm(out_mine), in_hbm(out_other), []
        )
        received = other_core(away)
        mixed, pair_own, pair_send = attend_back(
            in_hbm(probs), in_hbm(query), in_hbm(pair), in_hbm(pair_away), heads, received, in_hbm(cosine), in_hbm(sine)
        )
        out_grad = out_back(in_hbm(every), branch_mine, received, [mixed]).reshape(WIDE, ROWS, HEADS)
        one_mine, one_away, attn_shares = project_back(
            place,
            mixed,
            pair_own,
            along_x(pair_send, 2),
            in_hbm(cosine),
            in_hbm(sine),
            in_hbm(projections),
            in_hbm(normed_one),
            inputs,
            inputs_away,
            two_grad,
            out_grad,
        )
    with jax.named_scope("results"):
        attn_sent = send_b(attn_shares)
        part_other = ffn_back("ffn_out", rows, (2,), [down_full], 1, [one_mine])
        part_mine = ffn_back("ffn_out", rows, (2,), [down_full], 0, [part_other])
        output_shares = scatter_ring("ring_output", part_mine, other_core(part_other))
        output = (middle + add(*output_shares)).astype(bf16)
        source = inputs.astype(f32)
        inverse_one = lax.rsqrt(jnp.mean(source * source, axis=1, keepdims=True) + epsilon)
        scaled_one = (one_mine + other_core(one_away)) * gains[:1]
        input_grad = (
            middle_grad
            + inverse_one * scaled_one
            - source * inverse_one**3 * jnp.mean(scaled_one * source, axis=1, keepdims=True)
        )
        keep, gone = part_x_lo(place, summed.reshape(2, ROWS, 3 * HALF))
        ffn_grads = finish_ffn(place, keep, partner_x(gone))
        sums = deal(scatter_a(place, "attn_grad_a", [attn_sent], [output_shares[0]]), [ffn_grads[0]])
        qkv_grad, out_grad, extra = finish(place, lax.all_to_all(sums, RING, 0, 0, tiled=True))
        bias_grad = lax.dynamic_slice(extra, (0, 2 + 16 * place.narrow), (1, 16))[0]
    return (
        output,
        input_grad,
        extra[:, 0],
        qkv_grad,
        bias_grad,
        out_grad,
        extra[:, 1],
        ffn_grads[0],
        ffn_grads[1],
        ffn_grads[2].T,
    )


def solution(mesh):
    split_mesh = Mesh(mesh.devices.reshape(4, 2, 4, 2, 2), BOTH)
    return jax.shard_map(
        per_device,
        mesh=split_mesh,
        in_specs=(
            P(BOTH, None),
            P(BOTH),
            P(BOTH, None),
            P(BOTH),
            P(BOTH, None),
            P(BOTH),
            P(WIDE_AXES, NARROW_AXES),
            P(WIDE_AXES, NARROW_AXES),
            P(NARROW_AXES, WIDE_AXES),
            P(WIDE_AXES, None),
            P(WIDE_AXES, None),
            P(BOTH, None),
        ),
        out_specs=(
            P(BOTH, None),
            P(BOTH, None),
            P(BOTH),
            P(BOTH, None),
            P(BOTH),
            P(BOTH, None),
            P(BOTH),
            P(WIDE_AXES, NARROW_AXES),
            P(WIDE_AXES, NARROW_AXES),
            P(NARROW_AXES, WIDE_AXES),
        ),
        check_vma=False,
    )
```

```python
import math

import jax
import jax.numpy as jnp
from jax import lax
from jax.experimental import pallas as pl
from jax.experimental.pallas import tpu as pltpu
from jax.sharding import Mesh
from jax.sharding import PartitionSpec as P

D = 1536
QH = 12
KVH = 2
HD = 128
FF = 8960
GROUP = QH // KVH
HEADS = GROUP * HD
QKV = HEADS + 2 * HD
HALF = 1152
SPARE = FF // 4 - HALF
EXTRA = 128
WIDE = 32
ROWS = 48
WIDE_AXES = ("y", "x_lo", "z")
NARROW_AXES = ("x_hi", "core")
BOTH = WIDE_AXES + NARROW_AXES
RING = ("x_lo", "x_hi", "core")
epsilon = 1e-06
rope_base = 10000.0
bf16 = jnp.bfloat16
f32 = jnp.float32


def coords(index):
    wide, narrow = divmod(index, 4)
    y, rest = divmod(wide, 8)
    x_lo, z = divmod(rest, 4)
    x_hi, core = divmod(narrow, 2)
    return x_hi * 2 + x_lo, y, z, core


def number_of(x, y, z, core):
    x_hi, x_lo = divmod(x % 4, 2)
    return (((y % 4) * 2 + x_lo) * 4 + z % 4) * 4 + x_hi * 2 + core


def send(value, move):
    pairs = [(i, number_of(*move(*coords(i)))) for i in range(128)]
    return lax.ppermute(value, BOTH, pairs)


def other_core(value):
    return send(value, lambda x, y, z, c: (x, y, z, 1 - c))


def along_x(value, step):
    return send(value, lambda x, y, z, c: (x + step, y, z, c))


def partner_x(value):
    return send(value, lambda x, y, z, c: (x ^ 1, y, z, c))


def along_a(value, step):
    return send(value, lambda x, y, z, c: (x, y, z + step, c) if c == 0 else (x, y + step, z, c))


def along_b(value, step):
    return send(value, lambda x, y, z, c: (x, y + step, z, c) if c == 0 else (x, y, z + step, c))


class Place:
    def __init__(self):
        self.y, self.x_lo, self.z, self.x_hi, self.core = (lax.axis_index(axis) for axis in BOTH)
        self.narrow = self.x_hi * 2 + self.core
        self.x = self.x_hi * 2 + self.x_lo
        first = self.core == 0
        self.a = jnp.where(first, self.z, self.y)
        self.b = jnp.where(first, self.y, self.z)
        self.first = first

    def slot_a(self, x_lo, step):
        at = (self.a + step) % 4
        return jnp.where(self.first, x_lo * 4 + at, at * 2 + x_lo)

    def slot_b(self, j, step):
        at = (self.b + step) % 4
        return jnp.where(self.first, at * 8 + j, j * 4 + at)


STEPS = (0, -1, 1, 2)


def after(value, *others):
    return lax.optimization_barrier((value, *others))[0]


def whole(shape, dtype=bf16):
    return jax.ShapeDtypeStruct(shape, dtype)


def size(*arrays):
    return sum(math.prod(a.shape) * jnp.dtype(a.dtype).itemsize for a in arrays)


def cost(flops, *arrays):
    return pl.CostEstimate(flops=int(flops), bytes_accessed=int(size(*arrays)), transcendentals=0)


SCALARS = pl.BlockSpec(memory_space=pltpu.SMEM)
IN_VMEM = pl.BlockSpec(memory_space=pltpu.VMEM)
TOTAL = QKV + EXTRA + HEADS


def local(name, kernel, scalars, inputs, outs, scratch=(), extra=0, flops=0, wait_for=(), tables=()):
    outs = tuple(outs)
    held = sum(size(s) for s in scratch)
    n, m = len(tables) + len(inputs), len(wait_for)

    def body(at, *refs):
        kernel(at, *refs[:n], *refs[n + m :])

    return pl.pallas_call(
        body,
        out_shape=outs,
        in_specs=[SCALARS] * (1 + len(tables)) + [IN_VMEM] * len(inputs) + [pl.BlockSpec(memory_space=pl.ANY)] * m,
        out_specs=(IN_VMEM,) * len(outs),
        scratch_shapes=list(scratch),
        compiler_params=pltpu.CompilerParams(vmem_limit_bytes=int(size(*inputs, *outs) + held + extra + (2 << 20))),
        cost_estimate=cost(flops, *inputs, *outs),
        name=name,
    )(jnp.stack(scalars).astype(jnp.int32), *tables, *inputs, *wait_for)


def in_hbm(array):
    return pltpu.with_memory_space_constraint(array, pltpu.HBM)


def nothing():
    return [jnp.int32(0)]


PACKED = 2 * ROWS * HEADS // (QKV + EXTRA)


def pack(first, second):
    rows = jnp.concatenate([first, second], axis=0)
    tiles = jnp.concatenate([rows[:, i : i + 128] for i in range(0, HEADS, 128)], axis=0)
    return jnp.concatenate([tiles[i : i + PACKED] for i in range(0, tiles.shape[0], PACKED)], axis=1)


def unpack(packed):
    tiles = jnp.concatenate([packed[:, i : i + 128] for i in range(0, QKV + EXTRA, 128)], axis=0)
    rows = jnp.concatenate([tiles[i : i + 2 * ROWS] for i in range(0, tiles.shape[0], 2 * ROWS)], axis=1)
    return rows[:ROWS], rows[ROWS:]


def gather_a(place, block, wait_for):
    got = [block, *(along_a(block, step) for step in (1, -1, 2))]
    slots = [place.slot_a(x_lo, step) for step in STEPS for x_lo in range(2)]
    width = QKV + EXTRA

    def kernel(at, *refs):
        out, quarter, held = refs[4:]
        for k in range(4):
            for x_lo in range(2):
                slot = at[2 * k + x_lo]
                out[pl.ds(pl.multiple_of(slot * ROWS, ROWS), ROWS), :] = refs[k][x_lo, :, :width]
                held[slot] = refs[k][x_lo, :, width:]
        first, second = held[2 * at[8]], held[2 * at[8] + 1]
        out[8 * ROWS :] = pack(first, second)
        quarter[0], quarter[1] = first, second

    outs = [whole((8 * ROWS + PACKED, width)), whole((2, ROWS, HEADS))]
    scratch = [pltpu.VMEM((8, ROWS, HEADS), bf16)]
    return local("gather_a", kernel, slots + [place.x], got, outs, scratch, 2 << 20, wait_for=wait_for)


def gather_b(place, message, quarter):
    left, right = along_b(message, 1), along_b(message, -1)
    far = along_b(quarter, 2)
    half = 4 * ROWS

    def forward(at, near_ref, left_ref, right_ref, far_ref, out, top, bottom):
        for k, ref in enumerate((left_ref, right_ref)):
            out[2 * k + 2], out[2 * k + 3] = unpack(ref[2 * half :])
        for i in range(2):
            out[i], out[6 + i] = near_ref[i], far_ref[i]
        top[...], bottom[...] = left_ref[:half], right_ref[half : 2 * half]

    outs = [whole((8, ROWS, HEADS))] + [whole((half, QKV + EXTRA))] * 2
    inputs = [quarter, left, right, far]
    quarter, top, bottom = local("forward", forward, nothing(), inputs, outs, (), 2 << 20)
    quarters = [quarter, along_x(quarter, 1), along_x(quarter, -1)]
    top, bottom = along_b(top, 1), along_b(bottom, -1)

    def kernel(at, *refs):
        main, extra = refs[5:]
        for k in range(4):
            for j in range(8):
                source, spot = (k, j) if k < 3 else (3 + j // 4, j % 4)
                rows = slice(spot * ROWS, (spot + 1) * ROWS)
                main[at[8 * k + j]] = refs[source][rows, :QKV]
                extra[at[8 * k + j]] = refs[source][rows, QKV:]

    inputs = [message, left, right, top, bottom]
    outs = [whole((WIDE, ROWS, QKV)), whole((WIDE, ROWS, EXTRA))]
    main, extra = local("gather_b", kernel, slots_b(place), inputs, outs, (), 1 << 20, wait_for=quarters[1:])
    return main, extra, quarters


def gather_x(place, quarters, wait_for):
    slots = []
    for back in (0, 1, 3, 2):
        x = (place.x - back) % 4
        slots += [place.slot_b(2 * x + i, step) for step in STEPS for i in range(2)]

    def kernel(at, *refs):
        for n in range(4):
            for k in range(8):
                refs[4][at[8 * n + k]] = refs[n][k]

    return local("gather_x", kernel, slots, quarters, [whole((WIDE, ROWS, HEADS))], wait_for=wait_for)[0]


def add(*terms):
    return sum(t.astype(f32) for t in terms)


def slots_b(place):
    return [place.slot_b(j, step) for step in STEPS for j in range(8)]


def send_b(shares):
    own, left, right, opposite = shares
    return [own, along_b(left, -1), along_b(right, 1), along_b(opposite, 2)]


def scatter_a(place, name, groups, wait_for=()):
    widths = [g[0].shape[-1] for g in groups]
    slots = [place.slot_a(x_lo, step) for step in STEPS for x_lo in range(2)]

    def kernel(at, *refs):
        outs = refs[-4:]
        for k in range(4):
            for x_lo in range(2):
                lane = 0
                for i, width in enumerate(widths):
                    total = sum(refs[4 * i + n][at[2 * k + x_lo]].astype(f32) for n in range(4))
                    outs[k][x_lo, :, lane : lane + width] = total.astype(bf16)
                    lane += width

    outs = [whole((2, ROWS, sum(widths)))] * 4
    inputs = [share for group in groups for share in group]
    own, left, right, opposite = local(name, kernel, slots, inputs, outs, wait_for=wait_for)
    return [own, along_a(left, -1), along_a(right, 1), along_a(opposite, 2)]


def deal(shares, wait_for):
    width = shares[0].shape[2]

    def kernel(at, *refs):
        for x_lo in range(2):
            rows = sum(refs[n][x_lo].astype(f32) for n in range(4))
            for k in range(4):
                refs[4][x_lo * 4 + k] = rows[12 * k : 12 * k + 12].astype(bf16)

    return local("deal", kernel, nothing(), shares, [whole((8, 12, width))], wait_for=wait_for)[0]


def arrange(got, wait_for):
    width = got.shape[2]

    def kernel(at, source, out, rows):
        for x_lo in range(2):
            for k in range(4):
                rows[x_lo, 12 * k : 12 * k + 12, :] = source[x_lo * 4 + k].astype(f32)
        out[...] = rows[...].astype(bf16)

    scratch = [pltpu.VMEM((2, ROWS, width), f32)]
    return local("arrange", kernel, nothing(), [got], [whole((2, ROWS, width))], scratch, wait_for=wait_for)[0]


def finish(place, got):
    def kernel(at, source, qkv, out, extra):
        low = sum(source[k].astype(f32) for k in range(0, 8, 2))
        high = sum(source[k].astype(f32) for k in range(1, 8, 2))
        qkv[:, :HEADS], qkv[:, HEADS:D] = low[:, :HEADS], high[:, :HEADS]
        for i in range(2):
            cut = slice(HEADS + i * HD, HEADS + (i + 1) * HD)
            at_lane = D + 2 * i * HD
            qkv[:, at_lane : at_lane + HD], qkv[:, at_lane + HD : at_lane + 2 * HD] = low[:, cut], high[:, cut]
        extra[...] = (low + high)[:, QKV : QKV + EXTRA]
        out[:, :HEADS], out[:, HEADS:] = low[:, QKV + EXTRA :], high[:, QKV + EXTRA :]

    outs = (whole((12, 2 * QKV), f32), whole((12, D), f32), whole((12, EXTRA), f32))
    return local("finish", kernel, nothing(), [got], outs)


def send_ring(rows):
    return [rows, along_x(rows, 1), along_x(rows, -1), along_x(rows, 2)]


def ring(name, got, wait_for=()):
    def kernel(at, *refs):
        for k in range(4):
            refs[4][128 * k : 128 * (k + 1)] = refs[k][...]

    return local(name, kernel, nothing(), got, [whole((512, D))], wait_for=wait_for)[0]


def scatter_ring(name, mine, other, wait_for=()):
    def kernel(at, mine_ref, other_ref, own, *rest):
        for k in range(4):
            rows = slice(128 * k, 128 * (k + 1))
            total = mine_ref[rows].astype(f32) + other_ref[rows].astype(f32)
            if k == 0:
                own[...] = total
            else:
                rest[k - 1][...] = total.astype(bf16)

    outs = [whole((128, D), f32)] + [whole((128, D))] * 3
    own, left, right, opposite = local(name, kernel, nothing(), [mine, other], outs, wait_for=wait_for)
    return [own, along_x(left, -1), along_x(right, 1), along_x(opposite, 2)]


def select(first, low, high):
    return jnp.where(first, low.astype(f32), high.astype(f32))


def turn(values, cosine, sine):
    return values * cosine + pltpu.roll(values, HD // 2, 1) * sine


def project(place, inputs, inputs_away, projections, lanes, cosine, sine, wait_for):
    tokens = 256

    def kernel(at, own, away, weight, lane_ref, cos_ref, sin_ref, normed, query, pair, gains):
        first = at[0] == 0
        table = lane_ref[...].astype(f32)
        gains_all = jnp.transpose(table.reshape(D, EXTRA))
        gains[...] = gains_all[:8]
        sums = jnp.sum(table, axis=1)
        left, right = pltpu.roll(sums, EXTRA - 2, 1), pltpu.roll(sums, 62, 1)
        lane = lax.broadcasted_iota(jnp.int32, (1, EXTRA), 1)

        def bias_at(low, high):
            def tile(j):
                return jnp.where(lane < 64, left[2 * j : 2 * j + 1], right[2 * j + 1 : 2 * j + 2])

            return jnp.where(first, tile(low), tile(high))

        for half, ref in enumerate((own, away)):
            rows = slice(128 * half, 128 * (half + 1))
            x = ref[...].astype(f32)
            inverse = lax.rsqrt(jnp.mean(x * x, axis=1, keepdims=True) + epsilon)
            normed[rows] = (x * inverse * gains_all[:1]).astype(bf16)
        cos, sin = cos_ref[...], sin_ref[...]
        mixed = jnp.dot(normed[...], weight[...], preferred_element_type=f32)
        for h in range(GROUP):
            values = mixed[:, h * HD : (h + 1) * HD] + bias_at(h, GROUP + h)
            query[h] = turn(values, cos, sin).astype(bf16)
        key = mixed[:, HEADS : HEADS + HD] + bias_at(12, 13)
        pair[:, :HD] = turn(key, cos, sin).astype(bf16)
        pair[:, HD:] = (mixed[:, HEADS + HD :] + bias_at(14, 15)).astype(bf16)

    outs = [whole((tokens, D)), whole((GROUP, tokens, HD)), whole((tokens, 2 * HD)), whole((8, D), f32)]
    inputs = [inputs, inputs_away, projections, lanes, cosine, sine]
    flops = 2 * tokens * D * QKV
    return local("project", kernel, [place.core], inputs, outs, extra=8 << 20, flops=flops, wait_for=wait_for)


def attend(place, query, pair, pair_away, lengths, offsets, wait_for):
    tokens = 256
    scale = HD**-0.5

    def kernel(at, offset, length, query_ref, own, away, probs, attended):
        core, start = at[0], at[1]
        off_a, off_b, len_a, len_b = offset[0, 0], offset[0, 1], length[0, 0], length[0, 1]

        def slot_of(index, base):
            other = index >= 128
            return base + jnp.where(other, (1 - core) * 128 - 128, core * 128) + index

        def which(slot):
            in_a = (slot >= off_a) & (slot < off_a + len_a)
            in_b = (slot >= off_b) & (slot < off_b + len_b)
            return jnp.where(in_a, 0, jnp.where(in_b, 1, -1))

        rows = slot_of(lax.broadcasted_iota(jnp.int32, (tokens, 1), 0), start)
        lane = lax.broadcasted_iota(jnp.int32, (1, 2 * tokens), 1)
        columns = jnp.where(lane < tokens, slot_of(lane, start), slot_of(lane - tokens, tokens - start))
        number, key_number = which(rows), which(columns)
        allowed = ((number == key_number) & (number >= 0) & (columns <= rows)) | (columns == rows)
        keys = jnp.concatenate([own[:, :HD], away[:, :HD]], axis=0)
        values = jnp.concatenate([own[:, HD:], away[:, HD:]], axis=0)
        for h in range(GROUP):
            scores = lax.dot_general(query_ref[h], keys, (((1,), (1,)), ((), ())), preferred_element_type=f32) * scale
            scores = jnp.where(allowed, scores, -1e30)
            raised = jnp.exp(scores - jnp.max(scores, axis=1, keepdims=True))
            result = raised * (1.0 / jnp.sum(raised, axis=1, keepdims=True))
            probs[h] = result
            attended[:, h * HD : (h + 1) * HD] = jnp.dot(
                result.astype(bf16), values, preferred_element_type=f32
            ).astype(bf16)

    scalars, tables = [place.core, place.x_hi * tokens], [offsets, lengths]
    outs = [whole((GROUP, tokens, 2 * tokens), f32), whole((tokens, HEADS))]
    flops = 8 * GROUP * tokens * tokens * HD
    return local(
        "attend", kernel, scalars, [query, pair, pair_away], outs, (), 6 << 20, flops, wait_for, tables
    )


def branch(place, attended, attended_away, out_mine, out_other, inputs, gains, wait_for):
    def kernel(at, mine, away, weight, weight_away, x_ref, gain, middle, normed, every):
        first = at[0] == 0
        for half, (a, b) in enumerate(((mine[:128], away[128:]), (mine[128:], away[:128]))):
            rows = slice(128 * half, 128 * (half + 1))
            every[rows, :HEADS] = select(first, a, b).astype(bf16)
            every[rows, HEADS:] = select(first, b, a).astype(bf16)
        left = every[:128]
        a = jnp.dot(left, weight[...], preferred_element_type=f32)
        b = jnp.dot(left, weight_away[...], preferred_element_type=f32)
        x = x_ref[...].astype(f32)
        low = x[:, :HEADS] + jnp.where(first, a, b)
        high = x[:, HEADS:] + jnp.where(first, b, a)
        middle[:, :HEADS], middle[:, HEADS:] = low, high
        squares = jnp.sum(low * low, axis=1, keepdims=True) + jnp.sum(high * high, axis=1, keepdims=True)
        inverse = lax.rsqrt(squares * (1.0 / D) + epsilon)
        normed[:, :HEADS] = (low * inverse * gain[1:2, :HEADS]).astype(bf16)
        normed[:, HEADS:] = (high * inverse * gain[1:2, HEADS:]).astype(bf16)

    outs = [whole((128, D), f32), whole((128, D)), whole((256, D))]
    inputs = [attended, attended_away, out_mine, out_other, inputs, gains]
    return local(
        "branch", kernel, [place.core], inputs, outs, extra=6 << 20, flops=2 * 128 * D * D, wait_for=wait_for
    )


def branch_back(place, shares, middle, gains, cotangent, out_mine, out_other, wait_for):
    def kernel(at, own, left, right, opposite, mid_ref, gain, cot, weight, weight_away, grad, gain_grad, mine, heads, away):
        first = at[0] == 0
        total = own[...] + left[...].astype(f32) + right[...].astype(f32) + opposite[...].astype(f32)
        mid = mid_ref[...]
        inverse = lax.rsqrt(jnp.mean(mid * mid, axis=1, keepdims=True) + epsilon)
        scaled = total * gain[1:2]
        mean = jnp.mean(scaled * mid, axis=1, keepdims=True)
        result = cot[...].astype(f32) + inverse * scaled - mid * (inverse * inverse * inverse * mean)
        grad[...] = result
        gain_grad[...] = jnp.sum(total * mid * inverse, axis=0, keepdims=True)
        low, high = result[:, :HEADS], result[:, HEADS:]
        mine[...] = jnp.where(first, low, high).astype(bf16)
        away[:, :HEADS] = jnp.where(first, high, low).astype(bf16)
        back = lax.dot_general(mine[...], weight[...], (((1,), (1,)), ((), ())), preferred_element_type=f32)
        back += lax.dot_general(
            away[:, :HEADS], weight_away[...], (((1,), (1,)), ((), ())), preferred_element_type=f32
        )
        low, high = back[:, :HEADS], back[:, HEADS:]
        heads[...] = jnp.where(first, low, high).astype(bf16)
        away[:, HEADS:] = jnp.where(first, high, low).astype(bf16)

    outs = [whole((128, D), f32), whole((1, D), f32), whole((128, HEADS)), whole((128, HEADS)), whole((128, D))]
    inputs = [*shares, middle, gains, cotangent, out_mine, out_other]
    return local(
        "branch_back", kernel, [place.core], inputs, outs, extra=8 << 20, flops=2 * 128 * D * D, wait_for=wait_for
    )


def attend_back(probs, query, pair, pair_away, heads, received, cosine, sine, wait_for):
    tokens = 256
    scale = HD**-0.5

    def kernel(at, probs_ref, query_ref, own, away, mine, others, cos_ref, sin_ref, mixed, pair_own, pair_send, total):
        keys = jnp.concatenate([own[:, :HD], away[:, :HD]], axis=0)
        values = jnp.concatenate([own[:, HD:], away[:, HD:]], axis=0)
        cos, sin = cos_ref[...], sin_ref[...]
        for h in range(GROUP):
            cut = slice(h * HD, (h + 1) * HD)
            grad = jnp.concatenate([mine[:, cut], others[:, HEADS + h * HD : HEADS + (h + 1) * HD]], axis=0)
            p = probs_ref[h]
            by_prob = lax.dot_general(grad, values, (((1,), (1,)), ((), ())), preferred_element_type=f32)
            row = jnp.sum(p * by_prob, axis=1, keepdims=True)
            by_score = (p * (by_prob - row)).astype(bf16)
            by_query = jnp.dot(by_score, keys, preferred_element_type=f32) * scale
            mixed[:, cut] = turn(by_query, cos, -sin).astype(bf16)
            by_key = lax.dot_general(by_score, query_ref[h], (((0,), (0,)), ((), ())), preferred_element_type=f32)
            by_value = lax.dot_general(p.astype(bf16), grad, (((0,), (0,)), ((), ())), preferred_element_type=f32)
            if h == 0:
                total[:, :HD], total[:, HD:] = by_key * scale, by_value
            else:
                total[:, :HD] += by_key * scale
                total[:, HD:] += by_value
        pair_own[...] = total[:tokens]
        pair_send[...] = total[tokens:].astype(bf16)

    outs = [whole((tokens, HEADS)), whole((tokens, 2 * HD), f32), whole((tokens, 2 * HD))]
    inputs = [probs, query, pair, pair_away, heads, received, cosine, sine]
    scratch = [pltpu.VMEM((2 * tokens, 2 * HD), f32)]
    flops = 20 * GROUP * tokens * tokens * HD
    return local("attend_back", kernel, nothing(), inputs, outs, scratch, 8 << 20, flops, wait_for)


def out_back(every, mine, received, wait_for):
    def kernel(at, every_ref, mine_ref, others, out):
        both = jnp.concatenate([mine_ref[...], others[:, :HEADS]], axis=0)
        for r in range(0, D, 384):
            out[r : r + 384] = lax.dot_general(
                every_ref[:, r : r + 384], both, (((0,), (0,)), ((), ())), preferred_element_type=f32
            ).astype(bf16)

    flops = 2 * 256 * D * HEADS
    inputs = [every, mine, received]
    return local("out_back", kernel, nothing(), inputs, [whole((D, HEADS))], (), 6 << 20, flops, wait_for)[0]


def project_back(place, mixed, pair_own, pair_received, cosine, sine, projections, normed, inputs, inputs_away, two, out,
                 wait_for):
    width = QKV + EXTRA

    def kernel(at, mix, own_ref, got, cos_ref, sin_ref, weight, norm_ref, x_ref, x_away, two_ref, out_ref, mine, away, *rest):
        shares, (held, grads, rows) = rest[:4], rest[4:]
        core = at[32]
        total = own_ref[...] + got[...].astype(f32)
        grads[:, :HEADS] = mix[...]
        grads[:, HEADS : HEADS + HD] = turn(total[:, :HD], cos_ref[...], -sin_ref[...]).astype(bf16)
        grads[:, HEADS + HD :] = total[:, HD:].astype(bf16)
        one = jnp.zeros((1, D), f32)
        for half, (x_from, ref) in enumerate(((x_ref, mine), (x_away, away))):
            part = lax.dot_general(
                grads[128 * half : 128 * (half + 1)],
                weight[...],
                (((1,), (1,)), ((), ())),
                preferred_element_type=f32,
            )
            ref[...] = part
            x = x_from[...].astype(f32)
            inverse = lax.rsqrt(jnp.mean(x * x, axis=1, keepdims=True) + epsilon)
            one += jnp.sum(part * x * inverse, axis=0, keepdims=True)
        for r in range(0, D, 384):
            part = lax.dot_general(
                norm_ref[:, r : r + 384], grads[...], (((0,), (0,)), ((), ())), preferred_element_type=f32
            ).astype(bf16)
            held[r // ROWS : r // ROWS + 8, :, :QKV] = part.reshape(8, ROWS, QKV)
        rows[...] = jnp.zeros((EXTRA, D), f32)
        rows[0:1], rows[1:2] = one, two_ref[...]
        held[:, :, QKV:] = jnp.transpose(rows[...]).reshape(WIDE, ROWS, EXTRA).astype(bf16)
        bias = jnp.sum(grads[...].astype(f32), axis=0, keepdims=True)
        lane = lax.broadcasted_iota(jnp.int32, (ROWS, EXTRA), 1)
        row = lax.broadcasted_iota(jnp.int32, (ROWS, EXTRA), 0)
        spot = (lane >= 2) & (lane < 66) & (lax.rem(row, 12) == 0)
        for i in range(8):
            tile = bias[:, i * HD : (i + 1) * HD]
            base = 12 * core + 2 * i if i < GROUP else 24 + 4 * (i - GROUP) + 2 * core
            for odd, shift in ((0, 2), (1, 66)):
                moved = pltpu.roll(tile, shift, 1)
                before = held[base + odd, :, QKV:].astype(f32)
                held[base + odd, :, QKV:] = jnp.where(spot, moved, before).astype(bf16)
        for k in range(4):
            for j in range(8):
                shares[k][j, :, :width] = held[at[8 * k + j]]
                shares[k][j, :, width:] = out_ref[at[8 * k + j]]

    outs = [whole((128, D), f32)] * 2 + [whole((8, ROWS, TOTAL))] * 4
    scratch = [pltpu.VMEM((WIDE, ROWS, width), bf16), pltpu.VMEM((256, QKV), bf16), pltpu.VMEM((EXTRA, D), f32)]
    inputs = [mixed, pair_own, pair_received, cosine, sine, projections, normed, inputs, inputs_away, two, out]
    scalars = slots_b(place) + [place.core]
    flops = 4 * 256 * D * QKV
    mine, away, *shares = local("project_back", kernel, scalars, inputs, outs, scratch, 10 << 20, flops, wait_for)
    return mine, away, shares


def prepare_attention(place, qkv_weight, out_weight, norm_one, norm_two, qkv_bias):
    def kernel(at, qkv, out, one, two, bias, result):
        narrow = at[0]
        lane = lax.broadcasted_iota(jnp.int32, (12, EXTRA), 1)
        row = lax.broadcasted_iota(jnp.int32, (12, EXTRA), 0)
        diagonal = lax.broadcasted_iota(jnp.int32, (12, 12), 0) == lax.broadcasted_iota(jnp.int32, (12, 12), 1)

        def column(gain):
            return jnp.sum(jnp.where(diagonal, gain[...].astype(f32), 0.0), axis=1, keepdims=True)

        extra = jnp.where(lane == 0, column(one), 0.0) + jnp.where(lane == 1, column(two), 0.0)
        spread = jnp.concatenate([bias[...].astype(f32)] * 8, axis=1)
        base = 2 + 16 * narrow
        shifted = pltpu.roll(spread, 2, 1)
        extra = extra + jnp.where((row == 0) & (lane >= base) & (lane < base + 16), shifted, 0.0)
        extra = extra.astype(bf16)
        for k in range(8):
            c = k % 2
            result[k, :, :HEADS] = qkv[:, c * HEADS : (c + 1) * HEADS]
            for i in range(2):
                at_lane = D + (2 * i + c) * HD
                result[k, :, HEADS + i * HD : HEADS + (i + 1) * HD] = qkv[:, at_lane : at_lane + HD]
            result[k, :, QKV : QKV + EXTRA] = extra
            result[k, :, QKV + EXTRA :] = out[:, c * HEADS : (c + 1) * HEADS]

    inputs = [
        in_hbm(a)
        for a in (qkv_weight, out_weight, norm_one.reshape(1, 12), norm_two.reshape(1, 12), qkv_bias.reshape(1, 16))
    ]
    return local("prepare_attention", kernel, [place.narrow], inputs, [whole((8, 12, TOTAL))])[0]


def prepare_ffn(place, weights):
    def kernel(at, gate, up, down, mine, other):
        zero = at[0] == 0
        for i, weight in enumerate((gate, up, down)):
            low = weight[:, :HALF].astype(f32)
            high = jnp.concatenate([weight[:, HALF:].astype(f32), jnp.zeros((ROWS, HALF - SPARE), f32)], axis=1)
            mine[:, i * HALF : (i + 1) * HALF] = jnp.where(zero, low, high).astype(bf16)
            other[:, i * HALF : (i + 1) * HALF] = jnp.where(zero, high, low).astype(bf16)

    outs = (whole((ROWS, 3 * HALF)),) * 2
    return local("prepare_ffn", kernel, [place.x_lo], [in_hbm(w) for w in weights], outs)


def by_x_lo(place, mine, other, wait_for):
    def kernel(at, mine_ref, other_ref, out):
        out[at[0]] = mine_ref[...]
        out[1 - at[0]] = other_ref[...]

    return local("by_x_lo", kernel, [place.x_lo], [mine, other], [whole((2, *mine.shape))], wait_for=wait_for)[0]


def part_x_lo(place, both):
    def kernel(at, source, mine, other):
        mine[...] = source[at[0]]
        other[...] = source[1 - at[0]]

    return local("part_x_lo", kernel, [place.x_lo], [both], [whole(both.shape[1:])] * 2)


def finish_ffn(place, keep, gone):
    def kernel(at, keep_ref, gone_ref, *outs):
        zero, (*outs, mark) = at[0] == 0, outs
        mark[...] = jnp.zeros((8, 128), f32)
        for i, out in enumerate(outs):
            a = keep_ref[:, i * HALF : (i + 1) * HALF].astype(f32)
            b = gone_ref[:, i * HALF : (i + 1) * HALF].astype(f32)
            out[:, :HALF] = jnp.where(zero, a, b)
            out[:, HALF:] = jnp.where(zero, b, a)[:, :SPARE]

    outs = [whole((ROWS, HALF + SPARE), f32)] * 3 + [whole((8, 128), f32)]
    return local("finish_ffn", kernel, [place.x_lo], [keep, gone], outs)


def ffn_rows(x_mine, x_other, c_mine, c_other, gathered):
    half, step = x_mine.shape[0], 256
    chunks = 2 * half // step
    tokens = (x_mine, x_other, c_mine, c_other)

    def kernel(*refs):
        far_tokens, source, rows, mine, other, down = refs[:4], *refs[4:9]
        weights, held, near, grads, sems, token_sems, out_sems, row_sems, grad_sems = refs[9:]
        loads = [[] for _ in range(3)]
        token_loads = [pltpu.make_async_copy(far_tokens[i], near.at[i], token_sems.at[i]) for i in range(4)]

        def load_weight(m):
            for y in range(4):
                for x_lo in range(2):
                    load = pltpu.make_async_copy(
                        source.at[y, :, x_lo, :, pl.ds(m * HALF, HALF)],
                        weights.at[m, pl.ds(y * 8 + x_lo * 4, 4)],
                        sems.at[(m * 4 + y) * 2 + x_lo],
                    )
                    load.start()
                    loads[m].append(load)

        token_loads[0].start()
        load_weight(0)
        load_weight(1)
        token_loads[2].start()
        load_weight(2)
        token_loads[1].start()
        token_loads[3].start()
        per_side = half // step

        def store_chunk(n, side, here, start):
            there = pl.ds(pl.multiple_of(n * step, step), step)
            for i in range(3):
                copy = pltpu.make_async_copy(held.at[i, there], rows.at[i, there], row_sems.at[3 * n + i])
                copy.start() if start else copy.wait()
            for k, out in enumerate((mine, other)):

                @pl.when(side == k)
                def _():
                    copy = pltpu.make_async_copy(grads.at[there], out.at[here], grad_sems.at[n])
                    copy.start() if start else copy.wait()

        def chunk(n, _):
            side, here = n // per_side, pl.ds(pl.multiple_of(lax.rem(n, per_side) * step, step), step)
            there = pl.ds(pl.multiple_of(n * step, step), step)
            products = []
            for m in range(3):
                i = side if m < 2 else 2 + side

                @pl.when(n == 0)
                def _():
                    for load in loads[m] + [token_loads[0 if m < 2 else 2]] * (m != 1):
                        load.wait()

                @pl.when(n == per_side)
                def _():
                    for load in [token_loads[1 if m < 2 else 3]] * (m != 1):
                        load.wait()

                products.append(jnp.dot(near[i, here], weights[m].reshape(D, HALF), preferred_element_type=f32))
            gate, upward, grad = products
            sigmoid = 1.0 / (1.0 + jnp.exp(-gate))
            silu = gate * sigmoid
            held[0, there] = (grad * upward * (sigmoid * (1.0 + gate * (1.0 - sigmoid)))).astype(bf16)
            held[1, there] = (grad * silu).astype(bf16)
            held[2, there] = (silu * upward).astype(bf16)
            back = sum(
                lax.dot_general(
                    held[m, there], weights[m].reshape(D, HALF), (((1,), (1,)), ((), ())), preferred_element_type=f32
                )
                for m in range(2)
            )
            grads[there] = back.astype(bf16)
            store_chunk(n, side, here, True)

            @pl.when(n == 0)
            def _():
                down_store.start()

            return 0

        down_store = pltpu.make_async_copy(weights.at[2], down, out_sems.at[0])
        lax.fori_loop(0, chunks, chunk, 0)
        down_store.wait()
        for n in range(chunks):
            store_chunk(n, n // per_side, pl.ds(n % per_side * step, step), False)

    outs = (
        pltpu.HBM((3, 2 * half, HALF), bf16),
        pltpu.HBM((half, D), bf16),
        pltpu.HBM((half, D), bf16),
        pltpu.HBM((WIDE, ROWS, HALF), bf16),
    )
    return pl.pallas_call(
        kernel,
        out_shape=outs,
        in_specs=[pl.BlockSpec(memory_space=pl.ANY)] * 5,
        out_specs=(pl.BlockSpec(memory_space=pl.ANY),) * 4,
        scratch_shapes=[
            pltpu.VMEM((3, WIDE, ROWS, HALF), bf16),
            pltpu.VMEM((3, 2 * half, HALF), bf16),
            pltpu.VMEM((4, half, D), bf16),
            pltpu.VMEM((2 * half, D), bf16),
            pltpu.SemaphoreType.DMA((24,)),
            pltpu.SemaphoreType.DMA((4,)),
            pltpu.SemaphoreType.DMA((1,)),
            pltpu.SemaphoreType.DMA((3 * chunks,)),
            pltpu.SemaphoreType.DMA((chunks,)),
        ],
        compiler_params=pltpu.CompilerParams(vmem_limit_bytes=40 << 20),
        cost_estimate=cost(20 * half * D * HALF, *tokens, gathered),
        name="ffn_rows",
    )(*(in_hbm(t) for t in tokens), gathered)


def ffn_back(name, rows, parts, weights, half, wait_for=()):
    count, pairs = rows.shape[1] // 2, len(parts)
    n, cut = 3, D // 3

    def kernel(*refs):
        out = refs[-1]
        for r in range(0, count, 256):
            out[r : r + 256] = sum(
                lax.dot_general(
                    refs[i][0, r : r + 256], refs[pairs + i][...], (((1,), (1,)), ((), ())), preferred_element_type=f32
                )
                for i in range(pairs)
            ).astype(bf16)

    out = whole((count, D))
    return pl.pallas_call(
        kernel,
        grid=(n,),
        out_shape=out,
        in_specs=[pl.BlockSpec((1, count, HALF), lambda j, m=m: (m, half, 0)) for m in parts]
        + [pl.BlockSpec((cut, HALF), lambda j: (j, 0))] * pairs
        + [pl.BlockSpec(memory_space=pl.ANY)] * len(wait_for),
        out_specs=pl.BlockSpec((count, cut), lambda j: (0, j)),
        compiler_params=pltpu.CompilerParams(vmem_limit_bytes=20 << 20),
        cost_estimate=cost(2 * pairs * count * D * HALF, out, out, out),
        name=name,
    )(*([in_hbm(rows)] * pairs), *(in_hbm(w) for w in weights), *wait_for)


def weight_grads(x_mine, x_other, c_mine, c_other, rows, wait_for):
    count = x_mine.shape[0]

    def kernel(xa, xb, ca, cb, r, *refs):
        out, mark = refs[-2:]
        mark[...] = jnp.zeros((8, 128), f32)

        def products(a, b):
            left = jnp.concatenate([a[...], b[...]], axis=0)
            part = lax.dot_general(left, r[0], (((0,), (0,)), ((), ())), preferred_element_type=f32).astype(bf16)
            for w in range(WIDE):
                y, rest = divmod(w, 8)
                x_lo, z = divmod(rest, 4)
                out[y * 8 + z * 2 + x_lo] = part[w * ROWS : (w + 1) * ROWS]

        @pl.when(pl.program_id(0) < 2)
        def _():
            products(xa, xb)

        @pl.when(pl.program_id(0) == 2)
        def _():
            products(ca, cb)

    left_spec = pl.BlockSpec((count, D), lambda m: (0, 0), pipeline_mode=pl.Buffered(1))
    return pl.pallas_call(
        kernel,
        grid=(3,),
        out_shape=(pltpu.HBM((WIDE, ROWS, 3 * HALF), bf16), whole((8, 128), f32)),
        in_specs=[left_spec] * 4
        + [pl.BlockSpec((1, 2 * count, HALF), lambda m: (m, 0, 0))]
        + [pl.BlockSpec(memory_space=pl.ANY)] * len(wait_for),
        out_specs=(
            pl.BlockSpec((WIDE, ROWS, HALF), lambda m: (0, 0, m)),
            pl.BlockSpec((8, 128), lambda m: (0, 0)),
        ),
        compiler_params=pltpu.CompilerParams(vmem_limit_bytes=46 << 20),
        cost_estimate=cost(12 * count * D * HALF, rows),
        name="weight_grads",
    )(*(in_hbm(v) for v in (x_mine, x_other, c_mine, c_other, rows)), *wait_for)


def pass_on(array, wait_for):
    def kernel(*refs):
        pass

    return pl.pallas_call(
        kernel,
        out_shape=pltpu.HBM(array.shape, array.dtype),
        in_specs=[pl.BlockSpec(memory_space=pl.ANY)] * (1 + len(wait_for)),
        out_specs=pl.BlockSpec(memory_space=pl.ANY),
        input_output_aliases={0: 0},
        compiler_params=pltpu.CompilerParams(vmem_limit_bytes=1 << 20),
        name="pass_on",
    )(in_hbm(array), *wait_for)


def rope_tables(position):
    halfway = HD // 2
    inverse = rope_base ** (-jnp.arange(halfway, dtype=f32) * 2.0 / HD)
    angles = position.astype(f32)[:, None] * inverse[None, :]
    angles = jnp.concatenate([angles, angles], axis=1)
    return jnp.cos(angles), jnp.sin(angles)


def dot(left, right, dims):
    return lax.dot_general(left, right, (dims, ((), ())), preferred_element_type=f32)


def per_device(
    inputs,
    norm_one,
    qkv_weight,
    qkv_bias,
    out_weight,
    norm_two,
    gate_weight,
    up_weight,
    down_weight,
    lengths,
    offsets,
    cotangent,
):
    place = Place()
    own = inputs.shape[0]
    zero = place.x_lo == 0
    with jax.named_scope("weights"):
        mine, other = prepare_ffn(place, (gate_weight, up_weight, down_weight.T))
        other = partner_x(other)
        blocks = prepare_attention(place, qkv_weight, out_weight, norm_one, norm_two, qkv_bias)
        blocks = lax.all_to_all(blocks, RING, 0, 0, tiled=True)
        inputs_away = other_core(inputs)
        got = send_ring(cotangent)
        message, quarter = gather_a(place, arrange(blocks, [inputs_away]), got[1:3])
        block = by_x_lo(place, mine, other, [message])
        gathered = lax.all_gather(block.reshape(2 * ROWS, 3 * HALF), ("y", "z"), axis=0, tiled=True)
        projections, lanes, quarters = gather_b(place, message, quarter)
        projections = projections.reshape(D, QKV)
    with jax.named_scope("layout"):
        start = place.x_hi * 2 * own
        ramp = jnp.arange(own, dtype=jnp.int32)
        slots = jnp.concatenate([start + place.core * own + ramp, start + (1 - place.core) * own + ramp])
        inside = (slots[:, None] >= offsets[0][None, :]) & (slots[:, None] < (offsets[0] + lengths[0])[None, :])
        position = jnp.sum(jnp.where(inside, slots[:, None] - offsets[0][None, :], 0), axis=1)
        cosine, sine = rope_tables(position)
        sine = jnp.where(jnp.arange(HD)[None, :] < HD // 2, -sine, sine)
    with jax.named_scope("attention"):
        normed_one, query, pair, gains = project(
            place, inputs, inputs_away, projections, lanes, cosine, sine, []
        )
        cotangent_mine = ring("ring_cotangent", got, [pair])
        cotangent_other = other_core(cotangent_mine)
        quarters.append(along_x(quarters[0], 2))
        pair_away = along_x(pair, 2)
        probs, attended = attend(place, query, pair, pair_away, lengths, offsets, quarters[3:])
        out_mine = gather_x(place, quarters, [pair]).reshape(D, HEADS)
        out_other = other_core(out_mine)
        middle, normed_two, every = branch(
            place, attended, other_core(attended), out_mine, out_other, inputs, gains, got[3:]
        )
    with jax.named_scope("ffn"):
        normed_mine = ring("ring_normed", send_ring(normed_two))
        normed_other = other_core(normed_mine)
        gathered = in_hbm(gathered.reshape(4, 4, 2, ROWS, 3 * HALF))
        rows, grad_mine, grad_other, down_full = ffn_rows(
            normed_mine, normed_other, cotangent_mine, cotangent_other, gathered
        )
        down_full = down_full.reshape(D, HALF)
        shares = scatter_ring("ring_grad", in_hbm(grad_mine), other_core(grad_other))
        wgrad, mark = weight_grads(normed_mine, normed_other, cotangent_mine, cotangent_other, rows, [shares[0]])
        wgrad = pass_on(wgrad, shares[1:])
        summed = lax.psum_scatter(wgrad.reshape(D, 3 * HALF), ("y", "z"), scatter_dimension=0, tiled=True)
    with jax.named_scope("attention_back"):
        middle_grad, two_grad, branch_mine, heads, away = branch_back(
            place, shares, in_hbm(middle), gains, cotangent, in_hbm(out_mine), in_hbm(out_other), [mark]
        )
        received = other_core(away)
        mixed, pair_own, pair_send = attend_back(
            in_hbm(probs),
            in_hbm(query),
            in_hbm(pair),
            in_hbm(pair_away),
            heads,
            received,
            in_hbm(cosine),
            in_hbm(sine),
            [],
        )
        out_grad = out_back(in_hbm(every), branch_mine, received, [mixed]).reshape(WIDE, ROWS, HEADS)
        one_mine, one_away, attn_shares = project_back(
            place,
            mixed,
            pair_own,
            along_x(pair_send, 2),
            in_hbm(cosine),
            in_hbm(sine),
            in_hbm(projections),
            in_hbm(normed_one),
            inputs,
            inputs_away,
            two_grad,
            out_grad,
            [],
        )
    with jax.named_scope("results"):
        attn_sent = send_b(attn_shares)
        part_other = ffn_back("ffn_out", rows, (2,), [down_full], 1, [one_mine])
        part_mine = ffn_back("ffn_out", rows, (2,), [down_full], 0, [part_other])
        output_shares = scatter_ring("ring_output", part_mine, other_core(part_other))
        output = (middle + add(*output_shares)).astype(bf16)
        source = inputs.astype(f32)
        inverse_one = lax.rsqrt(jnp.mean(source * source, axis=1, keepdims=True) + epsilon)
        scaled_one = (one_mine + other_core(one_away)) * gains[:1]
        input_grad = (
            middle_grad
            + inverse_one * scaled_one
            - source * inverse_one**3 * jnp.mean(scaled_one * source, axis=1, keepdims=True)
        )
        keep, gone = part_x_lo(place, in_hbm(summed.reshape(2, ROWS, 3 * HALF)))
        *ffn_grads, done = finish_ffn(place, keep, partner_x(gone))
        sums = deal(scatter_a(place, "attn_grad_a", [attn_sent], output_shares[:3]), [done])
        qkv_grad, out_grad, extra = finish(place, lax.all_to_all(sums, RING, 0, 0, tiled=True))
        bias_grad = lax.dynamic_slice(extra, (0, 2 + 16 * place.narrow), (1, 16))[0]
    return (
        output,
        input_grad,
        extra[:, 0],
        qkv_grad,
        bias_grad,
        out_grad,
        extra[:, 1],
        ffn_grads[0],
        ffn_grads[1],
        ffn_grads[2].T,
    )


def solution(mesh):
    split_mesh = Mesh(mesh.devices.reshape(4, 2, 4, 2, 2), BOTH)
    return jax.shard_map(
        per_device,
        mesh=split_mesh,
        in_specs=(
            P(BOTH, None),
            P(BOTH),
            P(BOTH, None),
            P(BOTH),
            P(BOTH, None),
            P(BOTH),
            P(WIDE_AXES, NARROW_AXES),
            P(WIDE_AXES, NARROW_AXES),
            P(NARROW_AXES, WIDE_AXES),
            P(WIDE_AXES, None),
            P(WIDE_AXES, None),
            P(BOTH, None),
        ),
        out_specs=(
            P(BOTH, None),
            P(BOTH, None),
            P(BOTH),
            P(BOTH, None),
            P(BOTH),
            P(BOTH, None),
            P(BOTH),
            P(WIDE_AXES, NARROW_AXES),
            P(WIDE_AXES, NARROW_AXES),
            P(NARROW_AXES, WIDE_AXES),
        ),
        check_vma=False,
    )
```

```python
import math

import jax
import jax.numpy as jnp
from jax import lax
from jax.experimental import pallas as pl
from jax.experimental.pallas import tpu as pltpu
from jax.sharding import Mesh
from jax.sharding import PartitionSpec as P

D = 1536
QH = 12
KVH = 2
HD = 128
FF = 8960
GROUP = QH // KVH
HEADS = GROUP * HD
QKV = HEADS + 2 * HD
HALF = 1152
SPARE = FF // 4 - HALF
EXTRA = 128
WIDE = 32
ROWS = 48
WIDE_AXES = ("y", "x_lo", "z")
NARROW_AXES = ("x_hi", "core")
BOTH = WIDE_AXES + NARROW_AXES
RING = ("x_lo", "x_hi", "core")
epsilon = 1e-06
rope_base = 10000.0
bf16 = jnp.bfloat16
f32 = jnp.float32


def coords(index):
    wide, narrow = divmod(index, 4)
    y, rest = divmod(wide, 8)
    x_lo, z = divmod(rest, 4)
    x_hi, core = divmod(narrow, 2)
    return x_hi * 2 + x_lo, y, z, core


def number_of(x, y, z, core):
    x_hi, x_lo = divmod(x % 4, 2)
    return (((y % 4) * 2 + x_lo) * 4 + z % 4) * 4 + x_hi * 2 + core


def send(value, move):
    pairs = [(i, number_of(*move(*coords(i)))) for i in range(128)]
    return lax.ppermute(value, BOTH, pairs)


def other_core(value):
    return send(value, lambda x, y, z, c: (x, y, z, 1 - c))


def along_x(value, step):
    return send(value, lambda x, y, z, c: (x + step, y, z, c))


def partner_x(value):
    return send(value, lambda x, y, z, c: (x ^ 1, y, z, c))


def along_a(value, step):
    return send(value, lambda x, y, z, c: (x, y, z + step, c) if c == 0 else (x, y + step, z, c))


def along_b(value, step):
    return send(value, lambda x, y, z, c: (x, y + step, z, c) if c == 0 else (x, y, z + step, c))


class Place:
    def __init__(self):
        self.y, self.x_lo, self.z, self.x_hi, self.core = (lax.axis_index(axis) for axis in BOTH)
        self.narrow = self.x_hi * 2 + self.core
        self.x = self.x_hi * 2 + self.x_lo
        first = self.core == 0
        self.a = jnp.where(first, self.z, self.y)
        self.b = jnp.where(first, self.y, self.z)
        self.first = first

    def slot_a(self, x_lo, step):
        at = (self.a + step) % 4
        return jnp.where(self.first, x_lo * 4 + at, at * 2 + x_lo)

    def slot_b(self, j, step):
        at = (self.b + step) % 4
        return jnp.where(self.first, at * 8 + j, j * 4 + at)


STEPS = (0, -1, 1, 2)


def after(value, *others):
    return lax.optimization_barrier((value, *others))[0]


def whole(shape, dtype=bf16):
    return jax.ShapeDtypeStruct(shape, dtype)


def size(*arrays):
    return sum(math.prod(a.shape) * jnp.dtype(a.dtype).itemsize for a in arrays)


def cost(flops, *arrays):
    return pl.CostEstimate(flops=int(flops), bytes_accessed=int(size(*arrays)), transcendentals=0)


SCALARS = pl.BlockSpec(memory_space=pltpu.SMEM)
IN_VMEM = pl.BlockSpec(memory_space=pltpu.VMEM)
TOTAL = QKV + EXTRA + HEADS


def local(name, kernel, scalars, inputs, outs, scratch=(), extra=0, flops=0, wait_for=(), tables=()):
    outs = tuple(outs)
    held = sum(size(s) for s in scratch)
    n, m = len(tables) + len(inputs), len(wait_for)

    def body(at, *refs):
        kernel(at, *refs[:n], *refs[n + m :])

    return pl.pallas_call(
        body,
        out_shape=outs,
        in_specs=[SCALARS] * (1 + len(tables)) + [IN_VMEM] * len(inputs) + [pl.BlockSpec(memory_space=pl.ANY)] * m,
        out_specs=(IN_VMEM,) * len(outs),
        scratch_shapes=list(scratch),
        compiler_params=pltpu.CompilerParams(vmem_limit_bytes=int(size(*inputs, *outs) + held + extra + (2 << 20))),
        cost_estimate=cost(flops, *inputs, *outs),
        name=name,
    )(jnp.stack(scalars).astype(jnp.int32), *tables, *inputs, *wait_for)


def in_hbm(array):
    return pltpu.with_memory_space_constraint(array, pltpu.HBM)


def nothing():
    return [jnp.int32(0)]


PACKED = 2 * ROWS * HEADS // (QKV + EXTRA)


def pack(first, second):
    rows = jnp.concatenate([first, second], axis=0)
    tiles = jnp.concatenate([rows[:, i : i + 128] for i in range(0, HEADS, 128)], axis=0)
    return jnp.concatenate([tiles[i : i + PACKED] for i in range(0, tiles.shape[0], PACKED)], axis=1)


def unpack(packed):
    tiles = jnp.concatenate([packed[:, i : i + 128] for i in range(0, QKV + EXTRA, 128)], axis=0)
    rows = jnp.concatenate([tiles[i : i + 2 * ROWS] for i in range(0, tiles.shape[0], 2 * ROWS)], axis=1)
    return rows[:ROWS], rows[ROWS:]


def gather_a(place, block, wait_for):
    got = [block, *(along_a(block, step) for step in (1, -1, 2))]
    slots = [place.slot_a(x_lo, step) for step in STEPS for x_lo in range(2)]
    width = QKV + EXTRA

    def kernel(at, *refs):
        out, quarter, held = refs[4:]
        for k in range(4):
            for x_lo in range(2):
                slot = at[2 * k + x_lo]
                out[pl.ds(pl.multiple_of(slot * ROWS, ROWS), ROWS), :] = refs[k][x_lo, :, :width]
                held[slot] = refs[k][x_lo, :, width:]
        first, second = held[2 * at[8]], held[2 * at[8] + 1]
        out[8 * ROWS :] = pack(first, second)
        quarter[0], quarter[1] = first, second

    outs = [whole((8 * ROWS + PACKED, width)), whole((2, ROWS, HEADS))]
    scratch = [pltpu.VMEM((8, ROWS, HEADS), bf16)]
    return local("gather_a", kernel, slots + [place.x], got, outs, scratch, 2 << 20, wait_for=wait_for)


def gather_b(place, message, quarter):
    left, right = along_b(message, 1), along_b(message, -1)
    far = along_b(quarter, 2)
    half = 4 * ROWS

    def forward(at, near_ref, left_ref, right_ref, far_ref, out, top, bottom):
        for k, ref in enumerate((left_ref, right_ref)):
            out[2 * k + 2], out[2 * k + 3] = unpack(ref[2 * half :])
        for i in range(2):
            out[i], out[6 + i] = near_ref[i], far_ref[i]
        top[...], bottom[...] = left_ref[:half], right_ref[half : 2 * half]

    outs = [whole((8, ROWS, HEADS))] + [whole((half, QKV + EXTRA))] * 2
    inputs = [quarter, left, right, far]
    quarter, top, bottom = local("forward", forward, nothing(), inputs, outs, (), 2 << 20)
    quarters = [quarter, along_x(quarter, 1), along_x(quarter, -1)]
    top, bottom = along_b(top, 1), along_b(bottom, -1)

    def kernel(at, *refs):
        main, extra = refs[5:]
        for k in range(4):
            for j in range(8):
                source, spot = (k, j) if k < 3 else (3 + j // 4, j % 4)
                rows = slice(spot * ROWS, (spot + 1) * ROWS)
                main[at[8 * k + j]] = refs[source][rows, :QKV]
                extra[at[8 * k + j]] = refs[source][rows, QKV:]

    inputs = [message, left, right, top, bottom]
    outs = [whole((WIDE, ROWS, QKV)), whole((WIDE, ROWS, EXTRA))]
    main, extra = local("gather_b", kernel, slots_b(place), inputs, outs, (), 1 << 20, wait_for=quarters[1:])
    return main, extra, quarters


def gather_x(place, quarters, wait_for):
    slots = []
    for back in (0, 1, 3, 2):
        x = (place.x - back) % 4
        slots += [place.slot_b(2 * x + i, step) for step in STEPS for i in range(2)]

    def kernel(at, *refs):
        for n in range(4):
            for k in range(8):
                refs[4][at[8 * n + k]] = refs[n][k]

    return local("gather_x", kernel, slots, quarters, [whole((WIDE, ROWS, HEADS))], wait_for=wait_for)[0]


def add(*terms):
    return sum(t.astype(f32) for t in terms)


def slots_b(place):
    return [place.slot_b(j, step) for step in STEPS for j in range(8)]


def send_x(shares):
    own, left, right, top, bottom = shares
    from_right, from_left = along_x(top, -1), along_x(bottom, 1)

    def kernel(at, left_ref, right_ref, top_ref, bottom_ref, left_out, right_out):
        left_out[:8] = (left_ref[:8].astype(f32) + top_ref[...].astype(f32)).astype(bf16)
        left_out[8:] = left_ref[8:]
        right_out[:8] = right_ref[:8]
        right_out[8:] = (right_ref[8:].astype(f32) + bottom_ref[...].astype(f32)).astype(bf16)

    inputs = [left, right, from_right, from_left]
    left, right = local("relay", kernel, nothing(), inputs, [whole(left.shape)] * 2, (), 4 << 20)
    return [own, along_x(left, -1), along_x(right, 1)]


def scatter_b(place, shares):
    slots = []
    for step in STEPS:
        at = (place.b + step) % 4
        slots += [jnp.where(place.first, at * 4 + a, a * 4 + at) for a in range(4)]

    def kernel(at, *refs):
        for k in range(4):
            for a in range(4):
                spot = at[4 * k + a]
                total = sum(refs[n][spot].astype(f32) for n in range(3))
                refs[3 + k][a] = total.astype(bf16)

    outs = [whole((4, *shares[0].shape[1:]))] * 4
    own, left, right, opposite = local("scatter_b", kernel, slots, shares, outs, (), 2 << 20)
    return [own, along_b(left, -1), along_b(right, 1), along_b(opposite, 2)], own


def scatter_a(place, shares, wait_for):
    slots = [(place.a + step) % 4 for step in STEPS]

    def kernel(at, *refs):
        for k in range(4):
            total = sum(refs[n][at[k]].astype(f32) for n in range(4))
            refs[4 + k][...] = total.astype(bf16)

    outs = [whole(shares[0].shape[1:])] * 4
    own, left, right, opposite = local("scatter_a", kernel, slots, shares, outs, (), 2 << 20, wait_for=wait_for)
    return [own, along_a(left, -1), along_a(right, 1), along_a(opposite, 2)]


def scatter_core(place, shares, wait_for):
    width = shares[0].shape[1]

    def kernel(at, *refs):
        total = sum(refs[n][...].astype(f32) for n in range(4))
        first, low, high = at[0] == 0, total[:12], total[12:]
        refs[4][...] = jnp.where(first, low, high)
        refs[5][...] = jnp.where(first, high, low).astype(bf16)

    outs = [whole((12, width), f32), whole((12, width))]
    return local("scatter_core", kernel, [place.core], shares, outs, (), 2 << 20, wait_for=wait_for)


def arrange(got, wait_for):
    width = got.shape[2]

    def kernel(at, source, out, rows):
        for x_lo in range(2):
            for k in range(4):
                rows[x_lo, 12 * k : 12 * k + 12, :] = source[x_lo * 4 + k].astype(f32)
        out[...] = rows[...].astype(bf16)

    scratch = [pltpu.VMEM((2, ROWS, width), f32)]
    return local("arrange", kernel, nothing(), [got], [whole((2, ROWS, width))], scratch, wait_for=wait_for)[0]


def finish(place, mine, received):
    def kernel(at, mine_ref, got, qkv, out, extra):
        first, a, b = at[0] == 0, mine_ref[...], got[...].astype(f32)
        low, high = jnp.where(first, a, b), jnp.where(first, b, a)
        qkv[:, :HEADS], qkv[:, HEADS:D] = low[:, :HEADS], high[:, :HEADS]
        for i in range(2):
            cut = slice(HEADS + i * HD, HEADS + (i + 1) * HD)
            at_lane = D + 2 * i * HD
            qkv[:, at_lane : at_lane + HD], qkv[:, at_lane + HD : at_lane + 2 * HD] = low[:, cut], high[:, cut]
        extra[...] = (a + b)[:, QKV : QKV + EXTRA]
        out[:, :HEADS], out[:, HEADS:] = low[:, QKV + EXTRA :], high[:, QKV + EXTRA :]

    outs = (whole((12, 2 * QKV), f32), whole((12, D), f32), whole((12, EXTRA), f32))
    return local("finish", kernel, [place.core], [mine, received], outs)


def send_ring(rows):
    return [rows, along_x(rows, 1), along_x(rows, -1), along_x(rows, 2)]


def ring(name, got, wait_for=()):
    def kernel(at, *refs):
        for k in range(4):
            refs[4][128 * k : 128 * (k + 1)] = refs[k][...]

    return local(name, kernel, nothing(), got, [whole((512, D))], wait_for=wait_for)[0]


def scatter_ring(name, mine, other, wait_for=()):
    def kernel(at, mine_ref, other_ref, own, *rest):
        for k in range(4):
            rows = slice(128 * k, 128 * (k + 1))
            total = mine_ref[rows].astype(f32) + other_ref[rows].astype(f32)
            if k == 0:
                own[...] = total
            else:
                rest[k - 1][...] = total.astype(bf16)

    outs = [whole((128, D), f32)] + [whole((128, D))] * 3
    own, left, right, opposite = local(name, kernel, nothing(), [mine, other], outs, wait_for=wait_for)
    return [own, along_x(left, -1), along_x(right, 1), along_x(opposite, 2)]


def select(first, low, high):
    return jnp.where(first, low.astype(f32), high.astype(f32))


def turn(values, cosine, sine):
    return values * cosine + pltpu.roll(values, HD // 2, 1) * sine


def project(place, inputs, inputs_away, projections, lanes, cosine, sine, wait_for):
    tokens = 256

    def kernel(at, own, away, weight, lane_ref, cos_ref, sin_ref, normed, query, pair, gains):
        first = at[0] == 0
        table = lane_ref[...].astype(f32)
        gains_all = jnp.transpose(table.reshape(D, EXTRA))
        gains[...] = gains_all[:8]
        sums = jnp.sum(table, axis=1)
        left, right = pltpu.roll(sums, EXTRA - 2, 1), pltpu.roll(sums, 62, 1)
        lane = lax.broadcasted_iota(jnp.int32, (1, EXTRA), 1)

        def bias_at(low, high):
            def tile(j):
                return jnp.where(lane < 64, left[2 * j : 2 * j + 1], right[2 * j + 1 : 2 * j + 2])

            return jnp.where(first, tile(low), tile(high))

        for half, ref in enumerate((own, away)):
            rows = slice(128 * half, 128 * (half + 1))
            x = ref[...].astype(f32)
            inverse = lax.rsqrt(jnp.mean(x * x, axis=1, keepdims=True) + epsilon)
            normed[rows] = (x * inverse * gains_all[:1]).astype(bf16)
        cos, sin = cos_ref[...], sin_ref[...]
        mixed = jnp.dot(normed[...], weight[...], preferred_element_type=f32)
        for h in range(GROUP):
            values = mixed[:, h * HD : (h + 1) * HD] + bias_at(h, GROUP + h)
            query[h] = turn(values, cos, sin).astype(bf16)
        key = mixed[:, HEADS : HEADS + HD] + bias_at(12, 13)
        pair[:, :HD] = turn(key, cos, sin).astype(bf16)
        pair[:, HD:] = (mixed[:, HEADS + HD :] + bias_at(14, 15)).astype(bf16)

    outs = [whole((tokens, D)), whole((GROUP, tokens, HD)), whole((tokens, 2 * HD)), whole((8, D), f32)]
    inputs = [inputs, inputs_away, projections, lanes, cosine, sine]
    flops = 2 * tokens * D * QKV
    return local("project", kernel, [place.core], inputs, outs, extra=8 << 20, flops=flops, wait_for=wait_for)


def attend(place, query, pair, pair_away, lengths, offsets, wait_for):
    tokens = 256
    scale = HD**-0.5

    def kernel(at, offset, length, query_ref, own, away, probs, attended):
        core, start = at[0], at[1]
        off_a, off_b, len_a, len_b = offset[0, 0], offset[0, 1], length[0, 0], length[0, 1]

        def slot_of(index, base):
            other = index >= 128
            return base + jnp.where(other, (1 - core) * 128 - 128, core * 128) + index

        def which(slot):
            in_a = (slot >= off_a) & (slot < off_a + len_a)
            in_b = (slot >= off_b) & (slot < off_b + len_b)
            return jnp.where(in_a, 0, jnp.where(in_b, 1, -1))

        rows = slot_of(lax.broadcasted_iota(jnp.int32, (tokens, 1), 0), start)
        lane = lax.broadcasted_iota(jnp.int32, (1, 2 * tokens), 1)
        columns = jnp.where(lane < tokens, slot_of(lane, start), slot_of(lane - tokens, tokens - start))
        number, key_number = which(rows), which(columns)
        allowed = ((number == key_number) & (number >= 0) & (columns <= rows)) | (columns == rows)
        keys = jnp.concatenate([own[:, :HD], away[:, :HD]], axis=0)
        values = jnp.concatenate([own[:, HD:], away[:, HD:]], axis=0)
        for h in range(GROUP):
            scores = lax.dot_general(query_ref[h], keys, (((1,), (1,)), ((), ())), preferred_element_type=f32) * scale
            scores = jnp.where(allowed, scores, -1e30)
            raised = jnp.exp(scores - jnp.max(scores, axis=1, keepdims=True))
            result = raised * (1.0 / jnp.sum(raised, axis=1, keepdims=True))
            probs[h] = result
            attended[:, h * HD : (h + 1) * HD] = jnp.dot(
                result.astype(bf16), values, preferred_element_type=f32
            ).astype(bf16)

    scalars, tables = [place.core, place.x_hi * tokens], [offsets, lengths]
    outs = [whole((GROUP, tokens, 2 * tokens), f32), whole((tokens, HEADS))]
    flops = 8 * GROUP * tokens * tokens * HD
    return local(
        "attend", kernel, scalars, [query, pair, pair_away], outs, (), 6 << 20, flops, wait_for, tables
    )


def branch(place, attended, attended_away, out_mine, out_other, inputs, gains, wait_for):
    def kernel(at, mine, away, weight, weight_away, x_ref, gain, middle, normed, every):
        first = at[0] == 0
        for half, (a, b) in enumerate(((mine[:128], away[128:]), (mine[128:], away[:128]))):
            rows = slice(128 * half, 128 * (half + 1))
            every[rows, :HEADS] = select(first, a, b).astype(bf16)
            every[rows, HEADS:] = select(first, b, a).astype(bf16)
        left = every[:128]
        a = jnp.dot(left, weight[...], preferred_element_type=f32)
        b = jnp.dot(left, weight_away[...], preferred_element_type=f32)
        x = x_ref[...].astype(f32)
        low = x[:, :HEADS] + jnp.where(first, a, b)
        high = x[:, HEADS:] + jnp.where(first, b, a)
        middle[:, :HEADS], middle[:, HEADS:] = low, high
        squares = jnp.sum(low * low, axis=1, keepdims=True) + jnp.sum(high * high, axis=1, keepdims=True)
        inverse = lax.rsqrt(squares * (1.0 / D) + epsilon)
        normed[:, :HEADS] = (low * inverse * gain[1:2, :HEADS]).astype(bf16)
        normed[:, HEADS:] = (high * inverse * gain[1:2, HEADS:]).astype(bf16)

    outs = [whole((128, D), f32), whole((128, D)), whole((256, D))]
    inputs = [attended, attended_away, out_mine, out_other, inputs, gains]
    return local(
        "branch", kernel, [place.core], inputs, outs, extra=6 << 20, flops=2 * 128 * D * D, wait_for=wait_for
    )


def branch_back(place, shares, middle, gains, cotangent, out_mine, out_other, wait_for):
    def kernel(at, own, left, right, opposite, mid_ref, gain, cot, weight, weight_away, grad, gain_grad, mine, heads, away):
        first = at[0] == 0
        total = own[...] + left[...].astype(f32) + right[...].astype(f32) + opposite[...].astype(f32)
        mid = mid_ref[...]
        inverse = lax.rsqrt(jnp.mean(mid * mid, axis=1, keepdims=True) + epsilon)
        scaled = total * gain[1:2]
        mean = jnp.mean(scaled * mid, axis=1, keepdims=True)
        result = cot[...].astype(f32) + inverse * scaled - mid * (inverse * inverse * inverse * mean)
        grad[...] = result
        gain_grad[...] = jnp.sum(total * mid * inverse, axis=0, keepdims=True)
        low, high = result[:, :HEADS], result[:, HEADS:]
        mine[...] = jnp.where(first, low, high).astype(bf16)
        away[:, :HEADS] = jnp.where(first, high, low).astype(bf16)
        back = lax.dot_general(mine[...], weight[...], (((1,), (1,)), ((), ())), preferred_element_type=f32)
        back += lax.dot_general(
            away[:, :HEADS], weight_away[...], (((1,), (1,)), ((), ())), preferred_element_type=f32
        )
        low, high = back[:, :HEADS], back[:, HEADS:]
        heads[...] = jnp.where(first, low, high).astype(bf16)
        away[:, HEADS:] = jnp.where(first, high, low).astype(bf16)

    outs = [whole((128, D), f32), whole((1, D), f32), whole((128, HEADS)), whole((128, HEADS)), whole((128, D))]
    inputs = [*shares, middle, gains, cotangent, out_mine, out_other]
    return local(
        "branch_back", kernel, [place.core], inputs, outs, extra=8 << 20, flops=2 * 128 * D * D, wait_for=wait_for
    )


def attend_back(probs, query, pair, pair_away, heads, received, cosine, sine, wait_for):
    tokens = 256
    scale = HD**-0.5

    def kernel(at, probs_ref, query_ref, own, away, mine, others, cos_ref, sin_ref, mixed, pair_own, pair_send, total):
        keys = jnp.concatenate([own[:, :HD], away[:, :HD]], axis=0)
        values = jnp.concatenate([own[:, HD:], away[:, HD:]], axis=0)
        cos, sin = cos_ref[...], sin_ref[...]
        for h in range(GROUP):
            cut = slice(h * HD, (h + 1) * HD)
            grad = jnp.concatenate([mine[:, cut], others[:, HEADS + h * HD : HEADS + (h + 1) * HD]], axis=0)
            p = probs_ref[h]
            by_prob = lax.dot_general(grad, values, (((1,), (1,)), ((), ())), preferred_element_type=f32)
            row = jnp.sum(p * by_prob, axis=1, keepdims=True)
            by_score = (p * (by_prob - row)).astype(bf16)
            by_query = jnp.dot(by_score, keys, preferred_element_type=f32) * scale
            mixed[:, cut] = turn(by_query, cos, -sin).astype(bf16)
            by_key = lax.dot_general(by_score, query_ref[h], (((0,), (0,)), ((), ())), preferred_element_type=f32)
            by_value = lax.dot_general(p.astype(bf16), grad, (((0,), (0,)), ((), ())), preferred_element_type=f32)
            if h == 0:
                total[:, :HD], total[:, HD:] = by_key * scale, by_value
            else:
                total[:, :HD] += by_key * scale
                total[:, HD:] += by_value
        pair_own[...] = total[:tokens]
        pair_send[...] = total[tokens:].astype(bf16)

    outs = [whole((tokens, HEADS)), whole((tokens, 2 * HD), f32), whole((tokens, 2 * HD))]
    inputs = [probs, query, pair, pair_away, heads, received, cosine, sine]
    scratch = [pltpu.VMEM((2 * tokens, 2 * HD), f32)]
    flops = 20 * GROUP * tokens * tokens * HD
    return local("attend_back", kernel, nothing(), inputs, outs, scratch, 8 << 20, flops, wait_for)


def out_back(every, mine, received, wait_for):
    def kernel(at, every_ref, mine_ref, others, out):
        both = jnp.concatenate([mine_ref[...], others[:, :HEADS]], axis=0)
        for r in range(0, D, 384):
            part = lax.dot_general(
                every_ref[:, r : r + 384], both, (((0,), (0,)), ((), ())), preferred_element_type=f32
            )
            out[r // 24 : r // 24 + 16] = part.reshape(16, 24, HEADS).astype(bf16)

    flops = 2 * 256 * D * HEADS
    inputs = [every, mine, received]
    return local("out_back", kernel, nothing(), inputs, [whole((2 * WIDE, 24, HEADS))], (), 6 << 20, flops, wait_for)[0]


def project_back(place, mixed, pair_own, pair_received, cosine, sine, projections, normed, inputs, inputs_away, two, out,
                 wait_for):
    width = QKV + EXTRA

    def kernel(at, mix, own_ref, got, cos_ref, sin_ref, weight, norm_ref, x_ref, x_away, two_ref, out_ref, mine, away, *rest):
        shares, (held, grads, rows) = rest[:5], rest[5:]
        core = at[4]
        total = own_ref[...] + got[...].astype(f32)
        grads[:, :HEADS] = mix[...]
        grads[:, HEADS : HEADS + HD] = turn(total[:, :HD], cos_ref[...], -sin_ref[...]).astype(bf16)
        grads[:, HEADS + HD :] = total[:, HD:].astype(bf16)
        one = jnp.zeros((1, D), f32)
        for half, (x_from, ref) in enumerate(((x_ref, mine), (x_away, away))):
            part = lax.dot_general(
                grads[128 * half : 128 * (half + 1)],
                weight[...],
                (((1,), (1,)), ((), ())),
                preferred_element_type=f32,
            )
            ref[...] = part
            x = x_from[...].astype(f32)
            inverse = lax.rsqrt(jnp.mean(x * x, axis=1, keepdims=True) + epsilon)
            one += jnp.sum(part * x * inverse, axis=0, keepdims=True)
        for r in range(0, D, 384):
            part = lax.dot_general(
                norm_ref[:, r : r + 384], grads[...], (((0,), (0,)), ((), ())), preferred_element_type=f32
            )
            held[r // 24 : r // 24 + 16, :, :QKV] = part.reshape(16, 24, QKV).astype(bf16)
        rows[...] = jnp.zeros((EXTRA, D), f32)
        rows[0:1], rows[1:2] = one, two_ref[...]
        held[:, :, QKV:] = jnp.transpose(rows[...]).reshape(2 * WIDE, 24, EXTRA).astype(bf16)
        bias = jnp.sum(grads[...].astype(f32), axis=0, keepdims=True)
        lane = lax.broadcasted_iota(jnp.int32, (24, EXTRA), 1)
        row = lax.broadcasted_iota(jnp.int32, (24, EXTRA), 0)
        spot = (lane >= 2) & (lane < 66) & (lax.rem(row, 12) == 0)
        for i in range(8):
            tile = bias[:, i * HD : (i + 1) * HD]
            base = 12 * core + 2 * i if i < GROUP else 24 + 4 * (i - GROUP) + 2 * core
            for odd, shift in ((0, 2), (1, 66)):
                moved = pltpu.roll(tile, shift, 1)
                for half in range(2):
                    at_block = 2 * (base + odd) + half
                    before = held[at_block, :, QKV:].astype(f32)
                    held[at_block, :, QKV:] = jnp.where(spot, moved, before).astype(bf16)
        for k in range(4):
            for n in range(16):
                ref, spot = (shares[k], n) if k < 3 else (shares[3 + n // 8], n % 8)
                source = at[k] + n // 4 * 16 + n % 4 * 2
                ref[spot, :, :width] = held[source]
                ref[spot, :, width:] = out_ref[source]

    outs = [whole((128, D), f32)] * 2 + [whole((n, 24, TOTAL)) for n in (16, 16, 16, 8, 8)]
    scratch = [pltpu.VMEM((2 * WIDE, 24, width), bf16), pltpu.VMEM((256, QKV), bf16), pltpu.VMEM((EXTRA, D), f32)]
    inputs = [mixed, pair_own, pair_received, cosine, sine, projections, normed, inputs, inputs_away, two, out]
    scalars = [x % 2 * 8 + x // 2 for x in ((place.x + step) % 4 for step in STEPS)] + [place.core]
    flops = 4 * 256 * D * QKV
    mine, away, *shares = local("project_back", kernel, scalars, inputs, outs, scratch, 14 << 20, flops, wait_for)
    return mine, away, shares


def prepare_attention(place, qkv_weight, out_weight, norm_one, norm_two, qkv_bias):
    def kernel(at, qkv, out, one, two, bias, result):
        narrow = at[0]
        lane = lax.broadcasted_iota(jnp.int32, (12, EXTRA), 1)
        row = lax.broadcasted_iota(jnp.int32, (12, EXTRA), 0)
        diagonal = lax.broadcasted_iota(jnp.int32, (12, 12), 0) == lax.broadcasted_iota(jnp.int32, (12, 12), 1)

        def column(gain):
            return jnp.sum(jnp.where(diagonal, gain[...].astype(f32), 0.0), axis=1, keepdims=True)

        extra = jnp.where(lane == 0, column(one), 0.0) + jnp.where(lane == 1, column(two), 0.0)
        spread = jnp.concatenate([bias[...].astype(f32)] * 8, axis=1)
        base = 2 + 16 * narrow
        shifted = pltpu.roll(spread, 2, 1)
        extra = extra + jnp.where((row == 0) & (lane >= base) & (lane < base + 16), shifted, 0.0)
        extra = extra.astype(bf16)
        for k in range(8):
            c = k % 2
            result[k, :, :HEADS] = qkv[:, c * HEADS : (c + 1) * HEADS]
            for i in range(2):
                at_lane = D + (2 * i + c) * HD
                result[k, :, HEADS + i * HD : HEADS + (i + 1) * HD] = qkv[:, at_lane : at_lane + HD]
            result[k, :, QKV : QKV + EXTRA] = extra
            result[k, :, QKV + EXTRA :] = out[:, c * HEADS : (c + 1) * HEADS]

    inputs = [
        in_hbm(a)
        for a in (qkv_weight, out_weight, norm_one.reshape(1, 12), norm_two.reshape(1, 12), qkv_bias.reshape(1, 16))
    ]
    return local("prepare_attention", kernel, [place.narrow], inputs, [whole((8, 12, TOTAL))])[0]


def prepare_ffn(place, weights):
    def kernel(at, gate, up, down, mine, other):
        zero = at[0] == 0
        for i, weight in enumerate((gate, up, down)):
            low = weight[:, :HALF].astype(f32)
            high = jnp.concatenate([weight[:, HALF:].astype(f32), jnp.zeros((ROWS, HALF - SPARE), f32)], axis=1)
            mine[:, i * HALF : (i + 1) * HALF] = jnp.where(zero, low, high).astype(bf16)
            other[:, i * HALF : (i + 1) * HALF] = jnp.where(zero, high, low).astype(bf16)

    outs = (whole((ROWS, 3 * HALF)),) * 2
    return local("prepare_ffn", kernel, [place.x_lo], [in_hbm(w) for w in weights], outs)


def by_x_lo(place, mine, other, wait_for):
    def kernel(at, mine_ref, other_ref, out):
        out[at[0]] = mine_ref[...]
        out[1 - at[0]] = other_ref[...]

    return local("by_x_lo", kernel, [place.x_lo], [mine, other], [whole((2, *mine.shape))], wait_for=wait_for)[0]


def part_x_lo(place, both, wait_for):
    def kernel(at, source, mine, other):
        mine[...] = source[at[0]]
        other[...] = source[1 - at[0]]

    return local("part_x_lo", kernel, [place.x_lo], [both], [whole(both.shape[1:])] * 2, wait_for=wait_for)


def finish_ffn(place, keep, gone, wait_for):
    def kernel(at, keep_ref, gone_ref, *outs):
        zero, (*outs, mark) = at[0] == 0, outs
        mark[...] = jnp.zeros((8, 128), f32)
        for i, out in enumerate(outs):
            a = keep_ref[:, i * HALF : (i + 1) * HALF].astype(f32)
            b = gone_ref[:, i * HALF : (i + 1) * HALF].astype(f32)
            out[:, :HALF] = jnp.where(zero, a, b)
            out[:, HALF:] = jnp.where(zero, b, a)[:, :SPARE]

    outs = [whole((ROWS, HALF + SPARE), f32)] * 3 + [whole((8, 128), f32)]
    return local("finish_ffn", kernel, [place.x_lo], [keep, gone], outs, wait_for=wait_for)


def ffn_rows(x_mine, x_other, c_mine, c_other, gathered):
    half, step = x_mine.shape[0], 256
    chunks = 2 * half // step
    tokens = (x_mine, x_other, c_mine, c_other)

    def kernel(*refs):
        far_tokens, source, rows, mine, other, down = refs[:4], *refs[4:9]
        weights, held, near, grads, sems, token_sems, out_sems, row_sems, grad_sems = refs[9:]
        loads = [[] for _ in range(3)]
        token_loads = [pltpu.make_async_copy(far_tokens[i], near.at[i], token_sems.at[i]) for i in range(4)]

        def load_weight(m):
            for y in range(4):
                for x_lo in range(2):
                    load = pltpu.make_async_copy(
                        source.at[y, :, x_lo, :, pl.ds(m * HALF, HALF)],
                        weights.at[m, pl.ds(y * 8 + x_lo * 4, 4)],
                        sems.at[(m * 4 + y) * 2 + x_lo],
                    )
                    load.start()
                    loads[m].append(load)

        token_loads[0].start()
        load_weight(0)
        load_weight(1)
        token_loads[2].start()
        load_weight(2)
        token_loads[1].start()
        token_loads[3].start()
        per_side = half // step

        def store_chunk(n, side, here, start):
            there = pl.ds(pl.multiple_of(n * step, step), step)
            for i in range(3):
                copy = pltpu.make_async_copy(held.at[i, there], rows.at[i, there], row_sems.at[3 * n + i])
                copy.start() if start else copy.wait()
            for k, out in enumerate((mine, other)):

                @pl.when(side == k)
                def _():
                    copy = pltpu.make_async_copy(grads.at[there], out.at[here], grad_sems.at[n])
                    copy.start() if start else copy.wait()

        def chunk(n, _):
            side, here = n // per_side, pl.ds(pl.multiple_of(lax.rem(n, per_side) * step, step), step)
            there = pl.ds(pl.multiple_of(n * step, step), step)
            products = []
            for m in range(3):
                i = side if m < 2 else 2 + side

                @pl.when(n == 0)
                def _():
                    for load in loads[m] + [token_loads[0 if m < 2 else 2]] * (m != 1):
                        load.wait()

                @pl.when(n == per_side)
                def _():
                    for load in [token_loads[1 if m < 2 else 3]] * (m != 1):
                        load.wait()

                products.append(jnp.dot(near[i, here], weights[m].reshape(D, HALF), preferred_element_type=f32))
            gate, upward, grad = products
            sigmoid = 1.0 / (1.0 + jnp.exp(-gate))
            silu = gate * sigmoid
            held[0, there] = (grad * upward * (sigmoid * (1.0 + gate * (1.0 - sigmoid)))).astype(bf16)
            held[1, there] = (grad * silu).astype(bf16)
            held[2, there] = (silu * upward).astype(bf16)
            back = sum(
                lax.dot_general(
                    held[m, there], weights[m].reshape(D, HALF), (((1,), (1,)), ((), ())), preferred_element_type=f32
                )
                for m in range(2)
            )
            grads[there] = back.astype(bf16)
            store_chunk(n, side, here, True)

            @pl.when(n == 0)
            def _():
                down_store.start()

            return 0

        down_store = pltpu.make_async_copy(weights.at[2], down, out_sems.at[0])
        lax.fori_loop(0, chunks, chunk, 0)
        down_store.wait()
        for n in range(chunks):
            store_chunk(n, n // per_side, pl.ds(n % per_side * step, step), False)

    outs = (
        pltpu.HBM((3, 2 * half, HALF), bf16),
        pltpu.HBM((half, D), bf16),
        pltpu.HBM((half, D), bf16),
        pltpu.HBM((WIDE, ROWS, HALF), bf16),
    )
    return pl.pallas_call(
        kernel,
        out_shape=outs,
        in_specs=[pl.BlockSpec(memory_space=pl.ANY)] * 5,
        out_specs=(pl.BlockSpec(memory_space=pl.ANY),) * 4,
        scratch_shapes=[
            pltpu.VMEM((3, WIDE, ROWS, HALF), bf16),
            pltpu.VMEM((3, 2 * half, HALF), bf16),
            pltpu.VMEM((4, half, D), bf16),
            pltpu.VMEM((2 * half, D), bf16),
            pltpu.SemaphoreType.DMA((24,)),
            pltpu.SemaphoreType.DMA((4,)),
            pltpu.SemaphoreType.DMA((1,)),
            pltpu.SemaphoreType.DMA((3 * chunks,)),
            pltpu.SemaphoreType.DMA((chunks,)),
        ],
        compiler_params=pltpu.CompilerParams(vmem_limit_bytes=40 << 20),
        cost_estimate=cost(20 * half * D * HALF, *tokens, gathered),
        name="ffn_rows",
    )(*(in_hbm(t) for t in tokens), gathered)


def ffn_back(name, rows, parts, weights, half, wait_for=()):
    count, pairs = rows.shape[1] // 2, len(parts)
    n, cut = 3, D // 3

    def kernel(*refs):
        out = refs[-1]
        for r in range(0, count, 256):
            out[r : r + 256] = sum(
                lax.dot_general(
                    refs[i][0, r : r + 256], refs[pairs + i][...], (((1,), (1,)), ((), ())), preferred_element_type=f32
                )
                for i in range(pairs)
            ).astype(bf16)

    out = whole((count, D))
    return pl.pallas_call(
        kernel,
        grid=(n,),
        out_shape=out,
        in_specs=[pl.BlockSpec((1, count, HALF), lambda j, m=m: (m, half, 0)) for m in parts]
        + [pl.BlockSpec((cut, HALF), lambda j: (j, 0))] * pairs
        + [pl.BlockSpec(memory_space=pl.ANY)] * len(wait_for),
        out_specs=pl.BlockSpec((count, cut), lambda j: (0, j)),
        compiler_params=pltpu.CompilerParams(vmem_limit_bytes=20 << 20),
        cost_estimate=cost(2 * pairs * count * D * HALF, out, out, out),
        name=name,
    )(*([in_hbm(rows)] * pairs), *(in_hbm(w) for w in weights), *wait_for)


def weight_grads(x_mine, x_other, c_mine, c_other, rows, wait_for):
    count = x_mine.shape[0]

    def kernel(xa, xb, ca, cb, r, *refs):
        out, mark = refs[-2:]
        mark[...] = jnp.zeros((8, 128), f32)

        def products(a, b):
            left = jnp.concatenate([a[...], b[...]], axis=0)
            part = lax.dot_general(left, r[0], (((0,), (0,)), ((), ())), preferred_element_type=f32).astype(bf16)
            for w in range(WIDE):
                y, rest = divmod(w, 8)
                x_lo, z = divmod(rest, 4)
                out[y * 8 + z * 2 + x_lo] = part[w * ROWS : (w + 1) * ROWS]

        @pl.when(pl.program_id(0) < 2)
        def _():
            products(xa, xb)

        @pl.when(pl.program_id(0) == 2)
        def _():
            products(ca, cb)

    left_spec = pl.BlockSpec((count, D), lambda m: (0, 0), pipeline_mode=pl.Buffered(1))
    return pl.pallas_call(
        kernel,
        grid=(3,),
        out_shape=(pltpu.HBM((WIDE, ROWS, 3 * HALF), bf16), whole((8, 128), f32)),
        in_specs=[left_spec] * 4
        + [pl.BlockSpec((1, 2 * count, HALF), lambda m: (m, 0, 0))]
        + [pl.BlockSpec(memory_space=pl.ANY)] * len(wait_for),
        out_specs=(
            pl.BlockSpec((WIDE, ROWS, HALF), lambda m: (0, 0, m)),
            pl.BlockSpec((8, 128), lambda m: (0, 0)),
        ),
        compiler_params=pltpu.CompilerParams(vmem_limit_bytes=46 << 20),
        cost_estimate=cost(12 * count * D * HALF, rows),
        name="weight_grads",
    )(*(in_hbm(v) for v in (x_mine, x_other, c_mine, c_other, rows)), *wait_for)


def pass_on(array, wait_for):
    def kernel(*refs):
        pass

    return pl.pallas_call(
        kernel,
        out_shape=pltpu.HBM(array.shape, array.dtype),
        in_specs=[pl.BlockSpec(memory_space=pl.ANY)] * (1 + len(wait_for)),
        out_specs=pl.BlockSpec(memory_space=pl.ANY),
        input_output_aliases={0: 0},
        compiler_params=pltpu.CompilerParams(vmem_limit_bytes=1 << 20),
        name="pass_on",
    )(in_hbm(array), *wait_for)


def rope_tables(position):
    halfway = HD // 2
    inverse = rope_base ** (-jnp.arange(halfway, dtype=f32) * 2.0 / HD)
    angles = position.astype(f32)[:, None] * inverse[None, :]
    angles = jnp.concatenate([angles, angles], axis=1)
    return jnp.cos(angles), jnp.sin(angles)


def dot(left, right, dims):
    return lax.dot_general(left, right, (dims, ((), ())), preferred_element_type=f32)


def per_device(
    inputs,
    norm_one,
    qkv_weight,
    qkv_bias,
    out_weight,
    norm_two,
    gate_weight,
    up_weight,
    down_weight,
    lengths,
    offsets,
    cotangent,
):
    place = Place()
    own = inputs.shape[0]
    zero = place.x_lo == 0
    with jax.named_scope("weights"):
        mine, other = prepare_ffn(place, (gate_weight, up_weight, down_weight.T))
        other = partner_x(other)
        blocks = prepare_attention(place, qkv_weight, out_weight, norm_one, norm_two, qkv_bias)
        blocks = lax.all_to_all(blocks, RING, 0, 0, tiled=True)
        inputs_away = other_core(inputs)
        got = send_ring(cotangent)
        message, quarter = gather_a(place, arrange(blocks, [inputs_away]), got[1:3])
        block = by_x_lo(place, mine, other, [message])
        gathered = lax.all_gather(block.reshape(2 * ROWS, 3 * HALF), ("y", "z"), axis=0, tiled=True)
        projections, lanes, quarters = gather_b(place, message, quarter)
        projections = projections.reshape(D, QKV)
    with jax.named_scope("layout"):
        start = place.x_hi * 2 * own
        ramp = jnp.arange(own, dtype=jnp.int32)
        slots = jnp.concatenate([start + place.core * own + ramp, start + (1 - place.core) * own + ramp])
        inside = (slots[:, None] >= offsets[0][None, :]) & (slots[:, None] < (offsets[0] + lengths[0])[None, :])
        position = jnp.sum(jnp.where(inside, slots[:, None] - offsets[0][None, :], 0), axis=1)
        cosine, sine = rope_tables(position)
        sine = jnp.where(jnp.arange(HD)[None, :] < HD // 2, -sine, sine)
    with jax.named_scope("attention"):
        normed_one, query, pair, gains = project(
            place, inputs, inputs_away, projections, lanes, cosine, sine, []
        )
        cotangent_mine = ring("ring_cotangent", got, [pair])
        cotangent_other = other_core(cotangent_mine)
        quarters.append(along_x(quarters[0], 2))
        pair_away = along_x(pair, 2)
        probs, attended = attend(place, query, pair, pair_away, lengths, offsets, quarters[3:])
        out_mine = gather_x(place, quarters, [pair]).reshape(D, HEADS)
        out_other = other_core(out_mine)
        middle, normed_two, every = branch(
            place, attended, other_core(attended), out_mine, out_other, inputs, gains, got[3:]
        )
    with jax.named_scope("ffn"):
        normed_mine = ring("ring_normed", send_ring(normed_two))
        normed_other = other_core(normed_mine)
        gathered = in_hbm(gathered.reshape(4, 4, 2, ROWS, 3 * HALF))
        rows, grad_mine, grad_other, down_full = ffn_rows(
            normed_mine, normed_other, cotangent_mine, cotangent_other, gathered
        )
        down_full = down_full.reshape(D, HALF)
        shares = scatter_ring("ring_grad", in_hbm(grad_mine), other_core(grad_other))
        wgrad, mark = weight_grads(normed_mine, normed_other, cotangent_mine, cotangent_other, rows, [shares[0]])
        wgrad = pass_on(wgrad, shares[1:])
        summed = lax.psum_scatter(wgrad.reshape(D, 3 * HALF), ("y", "z"), scatter_dimension=0, tiled=True)
    with jax.named_scope("attention_back"):
        middle_grad, two_grad, branch_mine, heads, away = branch_back(
            place, shares, in_hbm(middle), gains, cotangent, in_hbm(out_mine), in_hbm(out_other), [mark]
        )
        received = other_core(away)
        mixed, pair_own, pair_send = attend_back(
            in_hbm(probs),
            in_hbm(query),
            in_hbm(pair),
            in_hbm(pair_away),
            heads,
            received,
            in_hbm(cosine),
            in_hbm(sine),
            [],
        )
        out_grad = out_back(in_hbm(every), branch_mine, received, [mixed])
        one_mine, one_away, attn_shares = project_back(
            place,
            mixed,
            pair_own,
            along_x(pair_send, 2),
            in_hbm(cosine),
            in_hbm(sine),
            in_hbm(projections),
            in_hbm(normed_one),
            inputs,
            inputs_away,
            two_grad,
            out_grad,
            [],
        )
    with jax.named_scope("results"):
        part_other = ffn_back("ffn_out", rows, (2,), [down_full], 1, [one_mine])
        part_mine = ffn_back("ffn_out", rows, (2,), [down_full], 0, [part_other])
        shares, summed_x = scatter_b(place, send_x(attn_shares))
        output_shares = scatter_ring("ring_output", part_mine, in_hbm(other_core(part_other)), [summed_x])
        output = (middle + add(*output_shares)).astype(bf16)
        source = inputs.astype(f32)
        inverse_one = lax.rsqrt(jnp.mean(source * source, axis=1, keepdims=True) + epsilon)
        scaled_one = (one_mine + other_core(one_away)) * gains[:1]
        input_grad = (
            middle_grad
            + inverse_one * scaled_one
            - source * inverse_one**3 * jnp.mean(scaled_one * source, axis=1, keepdims=True)
        )
        keep, gone = part_x_lo(place, in_hbm(summed.reshape(2, ROWS, 3 * HALF)), output_shares[:1])
        *ffn_grads, done = finish_ffn(place, keep, partner_x(gone), output_shares[1:])
        mine, gone = scatter_core(place, scatter_a(place, shares, output_shares[:1]), [done])
        qkv_grad, out_grad, extra = finish(place, mine, other_core(gone))
        bias_grad = lax.dynamic_slice(extra, (0, 2 + 16 * place.narrow), (1, 16))[0]
    return (
        output,
        input_grad,
        extra[:, 0],
        qkv_grad,
        bias_grad,
        out_grad,
        extra[:, 1],
        ffn_grads[0],
        ffn_grads[1],
        ffn_grads[2].T,
    )


def solution(mesh):
    split_mesh = Mesh(mesh.devices.reshape(4, 2, 4, 2, 2), BOTH)
    return jax.shard_map(
        per_device,
        mesh=split_mesh,
        in_specs=(
            P(BOTH, None),
            P(BOTH),
            P(BOTH, None),
            P(BOTH),
            P(BOTH, None),
            P(BOTH),
            P(WIDE_AXES, NARROW_AXES),
            P(WIDE_AXES, NARROW_AXES),
            P(NARROW_AXES, WIDE_AXES),
            P(WIDE_AXES, None),
            P(WIDE_AXES, None),
            P(BOTH, None),
        ),
        out_specs=(
            P(BOTH, None),
            P(BOTH, None),
            P(BOTH),
            P(BOTH, None),
            P(BOTH),
            P(BOTH, None),
            P(BOTH),
            P(WIDE_AXES, NARROW_AXES),
            P(WIDE_AXES, NARROW_AXES),
            P(NARROW_AXES, WIDE_AXES),
        ),
        check_vma=False,
    )
```

```python
import math

import jax
import jax.numpy as jnp
from jax import lax
from jax.experimental import pallas as pl
from jax.experimental.pallas import tpu as pltpu
from jax.sharding import Mesh
from jax.sharding import PartitionSpec as P

D = 1536
QH = 12
KVH = 2
HD = 128
FF = 8960
GROUP = QH // KVH
HEADS = GROUP * HD
QKV = HEADS + 2 * HD
HALF = 1152
SPARE = FF // 4 - HALF
EXTRA = 128
WIDE = 32
ROWS = 48
WIDE_AXES = ("y", "x_lo", "z")
NARROW_AXES = ("x_hi", "core")
BOTH = WIDE_AXES + NARROW_AXES
RING = ("x_lo", "x_hi", "core")
epsilon = 1e-06
rope_base = 10000.0
bf16 = jnp.bfloat16
f32 = jnp.float32


def coords(index):
    wide, narrow = divmod(index, 4)
    y, rest = divmod(wide, 8)
    x_lo, z = divmod(rest, 4)
    x_hi, core = divmod(narrow, 2)
    return x_hi * 2 + x_lo, y, z, core


def number_of(x, y, z, core):
    x_hi, x_lo = divmod(x % 4, 2)
    return (((y % 4) * 2 + x_lo) * 4 + z % 4) * 4 + x_hi * 2 + core


def send(value, move):
    pairs = [(i, number_of(*move(*coords(i)))) for i in range(128)]
    return lax.ppermute(value, BOTH, pairs)


def other_core(value):
    return send(value, lambda x, y, z, c: (x, y, z, 1 - c))


def along_x(value, step):
    return send(value, lambda x, y, z, c: (x + step, y, z, c))


def partner_x(value):
    return send(value, lambda x, y, z, c: (x ^ 1, y, z, c))


def along_a(value, step):
    return send(value, lambda x, y, z, c: (x, y, z + step, c) if c == 0 else (x, y + step, z, c))


def along_b(value, step):
    return send(value, lambda x, y, z, c: (x, y + step, z, c) if c == 0 else (x, y, z + step, c))


class Place:
    def __init__(self):
        self.y, self.x_lo, self.z, self.x_hi, self.core = (lax.axis_index(axis) for axis in BOTH)
        self.narrow = self.x_hi * 2 + self.core
        self.x = self.x_hi * 2 + self.x_lo
        first = self.core == 0
        self.a = jnp.where(first, self.z, self.y)
        self.b = jnp.where(first, self.y, self.z)
        self.first = first

    def slot_a(self, x_lo, step):
        at = (self.a + step) % 4
        return jnp.where(self.first, x_lo * 4 + at, at * 2 + x_lo)

    def slot_b(self, j, step):
        at = (self.b + step) % 4
        return jnp.where(self.first, at * 8 + j, j * 4 + at)


STEPS = (0, -1, 1, 2)


def after(value, *others):
    return lax.optimization_barrier((value, *others))[0]


def whole(shape, dtype=bf16):
    return jax.ShapeDtypeStruct(shape, dtype)


def size(*arrays):
    return sum(math.prod(a.shape) * jnp.dtype(a.dtype).itemsize for a in arrays)


def cost(flops, *arrays):
    return pl.CostEstimate(flops=int(flops), bytes_accessed=int(size(*arrays)), transcendentals=0)


SCALARS = pl.BlockSpec(memory_space=pltpu.SMEM)
IN_VMEM = pl.BlockSpec(memory_space=pltpu.VMEM)
TOTAL = QKV + EXTRA + HEADS


def local(name, kernel, scalars, inputs, outs, scratch=(), extra=0, flops=0, wait_for=(), tables=()):
    outs = tuple(outs)
    held = sum(size(s) for s in scratch)
    n, m = len(tables) + len(inputs), len(wait_for)

    def body(at, *refs):
        kernel(at, *refs[:n], *refs[n + m :])

    return pl.pallas_call(
        body,
        out_shape=outs,
        in_specs=[SCALARS] * (1 + len(tables)) + [IN_VMEM] * len(inputs) + [pl.BlockSpec(memory_space=pl.ANY)] * m,
        out_specs=(IN_VMEM,) * len(outs),
        scratch_shapes=list(scratch),
        compiler_params=pltpu.CompilerParams(vmem_limit_bytes=int(size(*inputs, *outs) + held + extra + (2 << 20))),
        cost_estimate=cost(flops, *inputs, *outs),
        name=name,
    )(jnp.stack(scalars).astype(jnp.int32), *tables, *inputs, *wait_for)


def in_hbm(array):
    return pltpu.with_memory_space_constraint(array, pltpu.HBM)


def nothing():
    return [jnp.int32(0)]


PACKED = 2 * ROWS * HEADS // (QKV + EXTRA)


def pack(first, second):
    rows = jnp.concatenate([first, second], axis=0)
    tiles = jnp.concatenate([rows[:, i : i + 128] for i in range(0, HEADS, 128)], axis=0)
    return jnp.concatenate([tiles[i : i + PACKED] for i in range(0, tiles.shape[0], PACKED)], axis=1)


def unpack(packed):
    tiles = jnp.concatenate([packed[:, i : i + 128] for i in range(0, QKV + EXTRA, 128)], axis=0)
    rows = jnp.concatenate([tiles[i : i + 2 * ROWS] for i in range(0, tiles.shape[0], 2 * ROWS)], axis=1)
    return rows[:ROWS], rows[ROWS:]


def gather_a(place, block, wait_for):
    got = [block, *(along_a(block, step) for step in (1, -1, 2))]
    slots = [place.slot_a(x_lo, step) for step in STEPS for x_lo in range(2)]
    width = QKV + EXTRA

    def kernel(at, *refs):
        out, quarter, held = refs[4:]
        for k in range(4):
            for x_lo in range(2):
                slot = at[2 * k + x_lo]
                out[pl.ds(pl.multiple_of(slot * ROWS, ROWS), ROWS), :] = refs[k][x_lo, :, :width]
                held[slot] = refs[k][x_lo, :, width:]
        first, second = held[2 * at[8]], held[2 * at[8] + 1]
        out[8 * ROWS :] = pack(first, second)
        quarter[0], quarter[1] = first, second

    outs = [whole((8 * ROWS + PACKED, width)), whole((2, ROWS, HEADS))]
    scratch = [pltpu.VMEM((8, ROWS, HEADS), bf16)]
    return local("gather_a", kernel, slots + [place.x], got, outs, scratch, 2 << 20, wait_for=wait_for)


def gather_b(place, message, quarter):
    left, right = along_b(message, 1), along_b(message, -1)
    far = along_b(quarter, 2)
    half = 4 * ROWS

    def forward(at, left_ref, right_ref, top, bottom):
        top[...], bottom[...] = left_ref[:half], right_ref[half : 2 * half]

    def collect(at, near_ref, left_ref, right_ref, far_ref, out):
        for k, ref in enumerate((left_ref, right_ref)):
            out[2 * k + 2], out[2 * k + 3] = unpack(ref[2 * half :])
        for i in range(2):
            out[i], out[6 + i] = near_ref[i], far_ref[i]

    top, bottom = local("forward", forward, nothing(), [left, right], [whole((half, QKV + EXTRA))] * 2)
    sent, outs = top, [whole((8, ROWS, HEADS))]
    quarter = local("collect", collect, nothing(), [quarter, left, right, far], outs, (), 2 << 20, wait_for=[top])[0]
    quarters = [quarter, along_x(quarter, 1), along_x(quarter, -1)]
    top, bottom = along_b(top, 1), along_b(bottom, -1)

    def kernel(at, *refs):
        main, extra = refs[5:]
        for k in range(4):
            for j in range(8):
                source, spot = (k, j) if k < 3 else (3 + j // 4, j % 4)
                rows = slice(spot * ROWS, (spot + 1) * ROWS)
                main[at[8 * k + j]] = refs[source][rows, :QKV]
                extra[at[8 * k + j]] = refs[source][rows, QKV:]

    inputs = [message, left, right, top, bottom]
    outs = [whole((WIDE, ROWS, QKV)), whole((WIDE, ROWS, EXTRA))]
    main, extra = local("gather_b", kernel, slots_b(place), inputs, outs, (), 1 << 20)
    return main, extra, quarters, sent


def gather_x(place, quarters, wait_for):
    slots = []
    for back in (0, 1, 3, 2):
        x = (place.x - back) % 4
        slots += [place.slot_b(2 * x + i, step) for step in STEPS for i in range(2)]

    def kernel(at, *refs):
        for n in range(4):
            for k in range(8):
                refs[4][at[8 * n + k]] = refs[n][k]

    return local("gather_x", kernel, slots, quarters, [whole((WIDE, ROWS, HEADS))], wait_for=wait_for)[0]


def add(*terms):
    return sum(t.astype(f32) for t in terms)


def slots_b(place):
    return [place.slot_b(j, step) for step in STEPS for j in range(8)]


def send_x(shares):
    own, left, right, top, bottom = shares
    from_right, from_left = along_x(top, -1), along_x(bottom, 1)

    def kernel(at, left_ref, right_ref, top_ref, bottom_ref, left_out, right_out):
        left_out[:8] = (left_ref[:8].astype(f32) + top_ref[...].astype(f32)).astype(bf16)
        left_out[8:] = left_ref[8:]
        right_out[:8] = right_ref[:8]
        right_out[8:] = (right_ref[8:].astype(f32) + bottom_ref[...].astype(f32)).astype(bf16)

    inputs = [left, right, from_right, from_left]
    left, right = local("relay", kernel, nothing(), inputs, [whole(left.shape)] * 2, (), 4 << 20)
    return [own, along_x(left, -1), along_x(right, 1)], left


def scatter_b(place, shares):
    slots = []
    for step in STEPS:
        at = (place.b + step) % 4
        slots += [jnp.where(place.first, at * 4 + a, a * 4 + at) for a in range(4)]

    def kernel(at, *refs):
        for k in range(4):
            for a in range(4):
                spot = at[4 * k + a]
                total = sum(refs[n][spot].astype(f32) for n in range(3))
                refs[3 + k][a] = total.astype(bf16)

    outs = [whole((4, *shares[0].shape[1:]))] * 4
    own, left, right, opposite = local("scatter_b", kernel, slots, shares, outs, (), 2 << 20)
    return [own, along_b(left, -1), along_b(right, 1), along_b(opposite, 2)], own


def scatter_a(place, shares, wait_for):
    slots = [(place.a + step) % 4 for step in STEPS]

    def kernel(at, *refs):
        for k in range(4):
            total = sum(refs[n][at[k]].astype(f32) for n in range(4))
            refs[4 + k][...] = total.astype(bf16)

    outs = [whole(shares[0].shape[1:])] * 4
    own, left, right, opposite = local("scatter_a", kernel, slots, shares, outs, (), 2 << 20, wait_for=wait_for)
    return [own, along_a(left, -1), along_a(right, 1), along_a(opposite, 2)]


def scatter_core(place, shares, wait_for):
    width = shares[0].shape[1]

    def kernel(at, *refs):
        total = sum(refs[n][...].astype(f32) for n in range(4))
        first, low, high = at[0] == 0, total[:12], total[12:]
        refs[4][...] = jnp.where(first, low, high)
        refs[5][...] = jnp.where(first, high, low).astype(bf16)

    outs = [whole((12, width), f32), whole((12, width))]
    return local("scatter_core", kernel, [place.core], shares, outs, (), 2 << 20, wait_for=wait_for)


def arrange(got, wait_for):
    width = got.shape[2]

    def kernel(at, source, out, rows):
        for x_lo in range(2):
            for k in range(4):
                rows[x_lo, 12 * k : 12 * k + 12, :] = source[x_lo * 4 + k].astype(f32)
        out[...] = rows[...].astype(bf16)

    scratch = [pltpu.VMEM((2, ROWS, width), f32)]
    return local("arrange", kernel, nothing(), [got], [whole((2, ROWS, width))], scratch, wait_for=wait_for)[0]


def finish(place, mine, received):
    def kernel(at, mine_ref, got, qkv, out, extra):
        first, a, b = at[0] == 0, mine_ref[...], got[...].astype(f32)
        low, high = jnp.where(first, a, b), jnp.where(first, b, a)
        qkv[:, :HEADS], qkv[:, HEADS:D] = low[:, :HEADS], high[:, :HEADS]
        for i in range(2):
            cut = slice(HEADS + i * HD, HEADS + (i + 1) * HD)
            at_lane = D + 2 * i * HD
            qkv[:, at_lane : at_lane + HD], qkv[:, at_lane + HD : at_lane + 2 * HD] = low[:, cut], high[:, cut]
        extra[...] = (a + b)[:, QKV : QKV + EXTRA]
        out[:, :HEADS], out[:, HEADS:] = low[:, QKV + EXTRA :], high[:, QKV + EXTRA :]

    outs = (whole((12, 2 * QKV), f32), whole((12, D), f32), whole((12, EXTRA), f32))
    return local("finish", kernel, [place.core], [mine, received], outs)


def send_ring(rows):
    return [rows, along_x(rows, 1), along_x(rows, -1), along_x(rows, 2)]


def ring(name, got, wait_for=()):
    def kernel(at, *refs):
        for k in range(4):
            refs[4][128 * k : 128 * (k + 1)] = refs[k][...]

    return local(name, kernel, nothing(), got, [whole((512, D))], wait_for=wait_for)[0]


def scatter_ring(name, mine, other, wait_for=()):
    def kernel(at, mine_ref, other_ref, own, *rest):
        for k in range(4):
            rows = slice(128 * k, 128 * (k + 1))
            total = mine_ref[rows].astype(f32) + other_ref[rows].astype(f32)
            if k == 0:
                own[...] = total
            else:
                rest[k - 1][...] = total.astype(bf16)

    outs = [whole((128, D), f32)] + [whole((128, D))] * 3
    own, left, right, opposite = local(name, kernel, nothing(), [mine, other], outs, wait_for=wait_for)
    return [own, along_x(left, -1), along_x(right, 1), along_x(opposite, 2)]


def select(first, low, high):
    return jnp.where(first, low.astype(f32), high.astype(f32))


def turn(values, cosine, sine):
    return values * cosine + pltpu.roll(values, HD // 2, 1) * sine


def project(place, inputs, inputs_away, projections, lanes, cosine, sine, wait_for):
    tokens = 256

    def kernel(at, own, away, weight, lane_ref, cos_ref, sin_ref, normed, query, pair, gains):
        first = at[0] == 0
        table = lane_ref[...].astype(f32)
        gains_all = jnp.transpose(table.reshape(D, EXTRA))
        gains[...] = gains_all[:8]
        sums = jnp.sum(table, axis=1)
        left, right = pltpu.roll(sums, EXTRA - 2, 1), pltpu.roll(sums, 62, 1)
        lane = lax.broadcasted_iota(jnp.int32, (1, EXTRA), 1)

        def bias_at(low, high):
            def tile(j):
                return jnp.where(lane < 64, left[2 * j : 2 * j + 1], right[2 * j + 1 : 2 * j + 2])

            return jnp.where(first, tile(low), tile(high))

        for half, ref in enumerate((own, away)):
            rows = slice(128 * half, 128 * (half + 1))
            x = ref[...].astype(f32)
            inverse = lax.rsqrt(jnp.mean(x * x, axis=1, keepdims=True) + epsilon)
            normed[rows] = (x * inverse * gains_all[:1]).astype(bf16)
        cos, sin = cos_ref[...], sin_ref[...]
        mixed = jnp.dot(normed[...], weight[...], preferred_element_type=f32)
        for h in range(GROUP):
            values = mixed[:, h * HD : (h + 1) * HD] + bias_at(h, GROUP + h)
            query[h] = turn(values, cos, sin).astype(bf16)
        key = mixed[:, HEADS : HEADS + HD] + bias_at(12, 13)
        pair[:, :HD] = turn(key, cos, sin).astype(bf16)
        pair[:, HD:] = (mixed[:, HEADS + HD :] + bias_at(14, 15)).astype(bf16)

    outs = [whole((tokens, D)), whole((GROUP, tokens, HD)), whole((tokens, 2 * HD)), whole((8, D), f32)]
    inputs = [inputs, inputs_away, projections, lanes, cosine, sine]
    flops = 2 * tokens * D * QKV
    return local("project", kernel, [place.core], inputs, outs, extra=8 << 20, flops=flops, wait_for=wait_for)


def attend(place, query, pair, pair_away, lengths, offsets, wait_for):
    tokens = 256
    scale = HD**-0.5

    def kernel(at, offset, length, query_ref, own, away, probs, attended):
        core, start = at[0], at[1]
        off_a, off_b, len_a, len_b = offset[0, 0], offset[0, 1], length[0, 0], length[0, 1]

        def slot_of(index, base):
            other = index >= 128
            return base + jnp.where(other, (1 - core) * 128 - 128, core * 128) + index

        def which(slot):
            in_a = (slot >= off_a) & (slot < off_a + len_a)
            in_b = (slot >= off_b) & (slot < off_b + len_b)
            return jnp.where(in_a, 0, jnp.where(in_b, 1, -1))

        rows = slot_of(lax.broadcasted_iota(jnp.int32, (tokens, 1), 0), start)
        lane = lax.broadcasted_iota(jnp.int32, (1, 2 * tokens), 1)
        columns = jnp.where(lane < tokens, slot_of(lane, start), slot_of(lane - tokens, tokens - start))
        number, key_number = which(rows), which(columns)
        allowed = ((number == key_number) & (number >= 0) & (columns <= rows)) | (columns == rows)
        keys = jnp.concatenate([own[:, :HD], away[:, :HD]], axis=0)
        values = jnp.concatenate([own[:, HD:], away[:, HD:]], axis=0)
        for h in range(GROUP):
            scores = lax.dot_general(query_ref[h], keys, (((1,), (1,)), ((), ())), preferred_element_type=f32) * scale
            scores = jnp.where(allowed, scores, -1e30)
            raised = jnp.exp(scores - jnp.max(scores, axis=1, keepdims=True))
            result = raised * (1.0 / jnp.sum(raised, axis=1, keepdims=True))
            probs[h] = result
            attended[:, h * HD : (h + 1) * HD] = jnp.dot(
                result.astype(bf16), values, preferred_element_type=f32
            ).astype(bf16)

    scalars, tables = [place.core, place.x_hi * tokens], [offsets, lengths]
    outs = [whole((GROUP, tokens, 2 * tokens), f32), whole((tokens, HEADS))]
    flops = 8 * GROUP * tokens * tokens * HD
    return local(
        "attend", kernel, scalars, [query, pair, pair_away], outs, (), 6 << 20, flops, wait_for, tables
    )


def branch(place, attended, attended_away, out_mine, out_other, inputs, gains, wait_for):
    def kernel(at, mine, away, weight, weight_away, x_ref, gain, middle, normed, every):
        first = at[0] == 0
        for half, (a, b) in enumerate(((mine[:128], away[128:]), (mine[128:], away[:128]))):
            rows = slice(128 * half, 128 * (half + 1))
            every[rows, :HEADS] = select(first, a, b).astype(bf16)
            every[rows, HEADS:] = select(first, b, a).astype(bf16)
        left = every[:128]
        a = jnp.dot(left, weight[...], preferred_element_type=f32)
        b = jnp.dot(left, weight_away[...], preferred_element_type=f32)
        x = x_ref[...].astype(f32)
        low = x[:, :HEADS] + jnp.where(first, a, b)
        high = x[:, HEADS:] + jnp.where(first, b, a)
        middle[:, :HEADS], middle[:, HEADS:] = low, high
        squares = jnp.sum(low * low, axis=1, keepdims=True) + jnp.sum(high * high, axis=1, keepdims=True)
        inverse = lax.rsqrt(squares * (1.0 / D) + epsilon)
        normed[:, :HEADS] = (low * inverse * gain[1:2, :HEADS]).astype(bf16)
        normed[:, HEADS:] = (high * inverse * gain[1:2, HEADS:]).astype(bf16)

    outs = [whole((128, D), f32), whole((128, D)), whole((256, D))]
    inputs = [attended, attended_away, out_mine, out_other, inputs, gains]
    return local(
        "branch", kernel, [place.core], inputs, outs, extra=6 << 20, flops=2 * 128 * D * D, wait_for=wait_for
    )


def branch_back(place, shares, middle, gains, cotangent, out_mine, out_other, wait_for):
    def kernel(at, own, left, right, opposite, mid_ref, gain, cot, weight, weight_away, grad, gain_grad, mine, heads, away):
        first = at[0] == 0
        total = own[...] + left[...].astype(f32) + right[...].astype(f32) + opposite[...].astype(f32)
        mid = mid_ref[...]
        inverse = lax.rsqrt(jnp.mean(mid * mid, axis=1, keepdims=True) + epsilon)
        scaled = total * gain[1:2]
        mean = jnp.mean(scaled * mid, axis=1, keepdims=True)
        result = cot[...].astype(f32) + inverse * scaled - mid * (inverse * inverse * inverse * mean)
        grad[...] = result
        gain_grad[...] = jnp.sum(total * mid * inverse, axis=0, keepdims=True)
        low, high = result[:, :HEADS], result[:, HEADS:]
        mine[...] = jnp.where(first, low, high).astype(bf16)
        away[:, :HEADS] = jnp.where(first, high, low).astype(bf16)
        back = lax.dot_general(mine[...], weight[...], (((1,), (1,)), ((), ())), preferred_element_type=f32)
        back += lax.dot_general(
            away[:, :HEADS], weight_away[...], (((1,), (1,)), ((), ())), preferred_element_type=f32
        )
        low, high = back[:, :HEADS], back[:, HEADS:]
        heads[...] = jnp.where(first, low, high).astype(bf16)
        away[:, HEADS:] = jnp.where(first, high, low).astype(bf16)

    outs = [whole((128, D), f32), whole((1, D), f32), whole((128, HEADS)), whole((128, HEADS)), whole((128, D))]
    inputs = [*shares, middle, gains, cotangent, out_mine, out_other]
    return local(
        "branch_back", kernel, [place.core], inputs, outs, extra=8 << 20, flops=2 * 128 * D * D, wait_for=wait_for
    )


def attend_back(probs, query, pair, pair_away, heads, received, cosine, sine, wait_for):
    tokens = 256
    scale = HD**-0.5

    def kernel(at, probs_ref, query_ref, own, away, mine, others, cos_ref, sin_ref, mixed, pair_own, pair_send, total):
        keys = jnp.concatenate([own[:, :HD], away[:, :HD]], axis=0)
        values = jnp.concatenate([own[:, HD:], away[:, HD:]], axis=0)
        cos, sin = cos_ref[...], sin_ref[...]
        for h in range(GROUP):
            cut = slice(h * HD, (h + 1) * HD)
            grad = jnp.concatenate([mine[:, cut], others[:, HEADS + h * HD : HEADS + (h + 1) * HD]], axis=0)
            p = probs_ref[h]
            by_prob = lax.dot_general(grad, values, (((1,), (1,)), ((), ())), preferred_element_type=f32)
            row = jnp.sum(p * by_prob, axis=1, keepdims=True)
            by_score = (p * (by_prob - row)).astype(bf16)
            by_query = jnp.dot(by_score, keys, preferred_element_type=f32) * scale
            mixed[:, cut] = turn(by_query, cos, -sin).astype(bf16)
            by_key = lax.dot_general(by_score, query_ref[h], (((0,), (0,)), ((), ())), preferred_element_type=f32)
            by_value = lax.dot_general(p.astype(bf16), grad, (((0,), (0,)), ((), ())), preferred_element_type=f32)
            if h == 0:
                total[:, :HD], total[:, HD:] = by_key * scale, by_value
            else:
                total[:, :HD] += by_key * scale
                total[:, HD:] += by_value
        pair_own[...] = total[:tokens]
        pair_send[...] = total[tokens:].astype(bf16)

    outs = [whole((tokens, HEADS)), whole((tokens, 2 * HD), f32), whole((tokens, 2 * HD))]
    inputs = [probs, query, pair, pair_away, heads, received, cosine, sine]
    scratch = [pltpu.VMEM((2 * tokens, 2 * HD), f32)]
    flops = 20 * GROUP * tokens * tokens * HD
    return local("attend_back", kernel, nothing(), inputs, outs, scratch, 8 << 20, flops, wait_for)


def out_back(every, mine, received, wait_for):
    def kernel(at, every_ref, mine_ref, others, out):
        both = jnp.concatenate([mine_ref[...], others[:, :HEADS]], axis=0)
        for r in range(0, D, 384):
            part = lax.dot_general(
                every_ref[:, r : r + 384], both, (((0,), (0,)), ((), ())), preferred_element_type=f32
            )
            out[r // 24 : r // 24 + 16] = part.reshape(16, 24, HEADS).astype(bf16)

    flops = 2 * 256 * D * HEADS
    inputs = [every, mine, received]
    return local("out_back", kernel, nothing(), inputs, [whole((2 * WIDE, 24, HEADS))], (), 6 << 20, flops, wait_for)[0]


def project_back(place, mixed, pair_own, pair_received, cosine, sine, projections, normed, inputs, inputs_away, two, out,
                 wait_for):
    width = QKV + EXTRA

    def kernel(at, mix, own_ref, got, cos_ref, sin_ref, weight, norm_ref, x_ref, x_away, two_ref, out_ref, mine, away, *rest):
        shares, (held, grads, rows) = rest[:5], rest[5:]
        core = at[4]
        total = own_ref[...] + got[...].astype(f32)
        grads[:, :HEADS] = mix[...]
        grads[:, HEADS : HEADS + HD] = turn(total[:, :HD], cos_ref[...], -sin_ref[...]).astype(bf16)
        grads[:, HEADS + HD :] = total[:, HD:].astype(bf16)
        one = jnp.zeros((1, D), f32)
        for half, (x_from, ref) in enumerate(((x_ref, mine), (x_away, away))):
            part = lax.dot_general(
                grads[128 * half : 128 * (half + 1)],
                weight[...],
                (((1,), (1,)), ((), ())),
                preferred_element_type=f32,
            )
            ref[...] = part
            x = x_from[...].astype(f32)
            inverse = lax.rsqrt(jnp.mean(x * x, axis=1, keepdims=True) + epsilon)
            one += jnp.sum(part * x * inverse, axis=0, keepdims=True)
        for r in range(0, D, 384):
            part = lax.dot_general(
                norm_ref[:, r : r + 384], grads[...], (((0,), (0,)), ((), ())), preferred_element_type=f32
            )
            held[r // 24 : r // 24 + 16, :, :QKV] = part.reshape(16, 24, QKV).astype(bf16)
        rows[...] = jnp.zeros((EXTRA, D), f32)
        rows[0:1], rows[1:2] = one, two_ref[...]
        held[:, :, QKV:] = jnp.transpose(rows[...]).reshape(2 * WIDE, 24, EXTRA).astype(bf16)
        bias = jnp.sum(grads[...].astype(f32), axis=0, keepdims=True)
        lane = lax.broadcasted_iota(jnp.int32, (24, EXTRA), 1)
        row = lax.broadcasted_iota(jnp.int32, (24, EXTRA), 0)
        spot = (lane >= 2) & (lane < 66) & (lax.rem(row, 12) == 0)
        for i in range(8):
            tile = bias[:, i * HD : (i + 1) * HD]
            base = 12 * core + 2 * i if i < GROUP else 24 + 4 * (i - GROUP) + 2 * core
            for odd, shift in ((0, 2), (1, 66)):
                moved = pltpu.roll(tile, shift, 1)
                for half in range(2):
                    at_block = 2 * (base + odd) + half
                    before = held[at_block, :, QKV:].astype(f32)
                    held[at_block, :, QKV:] = jnp.where(spot, moved, before).astype(bf16)
        for k in range(4):
            for n in range(16):
                ref, spot = (shares[k], n) if k < 3 else (shares[3 + n // 8], n % 8)
                source = at[k] + n // 4 * 16 + n % 4 * 2
                ref[spot, :, :width] = held[source]
                ref[spot, :, width:] = out_ref[source]

    outs = [whole((128, D), f32)] * 2 + [whole((n, 24, TOTAL)) for n in (16, 16, 16, 8, 8)]
    scratch = [pltpu.VMEM((2 * WIDE, 24, width), bf16), pltpu.VMEM((256, QKV), bf16), pltpu.VMEM((EXTRA, D), f32)]
    inputs = [mixed, pair_own, pair_received, cosine, sine, projections, normed, inputs, inputs_away, two, out]
    scalars = [x % 2 * 8 + x // 2 for x in ((place.x + step) % 4 for step in STEPS)] + [place.core]
    flops = 4 * 256 * D * QKV
    mine, away, *shares = local("project_back", kernel, scalars, inputs, outs, scratch, 14 << 20, flops, wait_for)
    return mine, away, shares


def prepare_attention(place, qkv_weight, out_weight, norm_one, norm_two, qkv_bias):
    def kernel(at, qkv, out, one, two, bias, result):
        narrow = at[0]
        lane = lax.broadcasted_iota(jnp.int32, (12, EXTRA), 1)
        row = lax.broadcasted_iota(jnp.int32, (12, EXTRA), 0)
        diagonal = lax.broadcasted_iota(jnp.int32, (12, 12), 0) == lax.broadcasted_iota(jnp.int32, (12, 12), 1)

        def column(gain):
            return jnp.sum(jnp.where(diagonal, gain[...].astype(f32), 0.0), axis=1, keepdims=True)

        extra = jnp.where(lane == 0, column(one), 0.0) + jnp.where(lane == 1, column(two), 0.0)
        spread = jnp.concatenate([bias[...].astype(f32)] * 8, axis=1)
        base = 2 + 16 * narrow
        shifted = pltpu.roll(spread, 2, 1)
        extra = extra + jnp.where((row == 0) & (lane >= base) & (lane < base + 16), shifted, 0.0)
        extra = extra.astype(bf16)
        for k in range(8):
            c = k % 2
            result[k, :, :HEADS] = qkv[:, c * HEADS : (c + 1) * HEADS]
            for i in range(2):
                at_lane = D + (2 * i + c) * HD
                result[k, :, HEADS + i * HD : HEADS + (i + 1) * HD] = qkv[:, at_lane : at_lane + HD]
            result[k, :, QKV : QKV + EXTRA] = extra
            result[k, :, QKV + EXTRA :] = out[:, c * HEADS : (c + 1) * HEADS]

    inputs = [
        in_hbm(a)
        for a in (qkv_weight, out_weight, norm_one.reshape(1, 12), norm_two.reshape(1, 12), qkv_bias.reshape(1, 16))
    ]
    return local("prepare_attention", kernel, [place.narrow], inputs, [whole((8, 12, TOTAL))])[0]


def prepare_ffn(place, weights):
    def kernel(at, gate, up, down, mine, other):
        zero = at[0] == 0
        for i, weight in enumerate((gate, up, down)):
            low = weight[:, :HALF].astype(f32)
            high = jnp.concatenate([weight[:, HALF:].astype(f32), jnp.zeros((ROWS, HALF - SPARE), f32)], axis=1)
            mine[:, i * HALF : (i + 1) * HALF] = jnp.where(zero, low, high).astype(bf16)
            other[:, i * HALF : (i + 1) * HALF] = jnp.where(zero, high, low).astype(bf16)

    outs = (whole((ROWS, 3 * HALF)),) * 2
    return local("prepare_ffn", kernel, [place.x_lo], [in_hbm(w) for w in weights], outs)


def by_x_lo(place, mine, other, wait_for):
    def kernel(at, mine_ref, other_ref, out):
        out[at[0]] = mine_ref[...]
        out[1 - at[0]] = other_ref[...]

    return local("by_x_lo", kernel, [place.x_lo], [mine, other], [whole((2, *mine.shape))], wait_for=wait_for)[0]


def part_x_lo(place, both, wait_for):
    def kernel(at, source, mine, other):
        mine[...] = source[at[0]]
        other[...] = source[1 - at[0]]

    return local("part_x_lo", kernel, [place.x_lo], [both], [whole(both.shape[1:])] * 2, wait_for=wait_for)


def finish_ffn(place, keep, gone, wait_for):
    def kernel(at, keep_ref, gone_ref, *outs):
        zero, (*outs, mark) = at[0] == 0, outs
        mark[...] = jnp.zeros((8, 128), f32)
        for i, out in enumerate(outs):
            a = keep_ref[:, i * HALF : (i + 1) * HALF].astype(f32)
            b = gone_ref[:, i * HALF : (i + 1) * HALF].astype(f32)
            out[:, :HALF] = jnp.where(zero, a, b)
            out[:, HALF:] = jnp.where(zero, b, a)[:, :SPARE]

    outs = [whole((ROWS, HALF + SPARE), f32)] * 3 + [whole((8, 128), f32)]
    return local("finish_ffn", kernel, [place.x_lo], [keep, gone], outs, wait_for=wait_for)


def ffn_rows(x_mine, x_other, c_mine, c_other, gathered):
    half, step = x_mine.shape[0], 256
    chunks = 2 * half // step
    tokens = (x_mine, x_other, c_mine, c_other)

    def kernel(*refs):
        far_tokens, source, rows, mine, other, down = refs[:4], *refs[4:9]
        weights, held, near, grads, sems, token_sems, out_sems, row_sems, grad_sems = refs[9:]
        loads = [[] for _ in range(3)]
        token_loads = [pltpu.make_async_copy(far_tokens[i], near.at[i], token_sems.at[i]) for i in range(4)]

        def load_weight(m):
            for y in range(4):
                for x_lo in range(2):
                    load = pltpu.make_async_copy(
                        source.at[y, :, x_lo, :, pl.ds(m * HALF, HALF)],
                        weights.at[m, pl.ds(y * 8 + x_lo * 4, 4)],
                        sems.at[(m * 4 + y) * 2 + x_lo],
                    )
                    load.start()
                    loads[m].append(load)

        token_loads[0].start()
        load_weight(0)
        load_weight(1)
        token_loads[2].start()
        load_weight(2)
        token_loads[1].start()
        token_loads[3].start()
        per_side = half // step

        def store_chunk(n, side, here, start):
            there = pl.ds(pl.multiple_of(n * step, step), step)
            for i in range(3):
                copy = pltpu.make_async_copy(held.at[i, there], rows.at[i, there], row_sems.at[3 * n + i])
                copy.start() if start else copy.wait()
            for k, out in enumerate((mine, other)):

                @pl.when(side == k)
                def _():
                    copy = pltpu.make_async_copy(grads.at[there], out.at[here], grad_sems.at[n])
                    copy.start() if start else copy.wait()

        def chunk(n, _):
            side, here = n // per_side, pl.ds(pl.multiple_of(lax.rem(n, per_side) * step, step), step)
            there = pl.ds(pl.multiple_of(n * step, step), step)
            products = []
            for m in range(3):
                i = side if m < 2 else 2 + side

                @pl.when(n == 0)
                def _():
                    for load in loads[m] + [token_loads[0 if m < 2 else 2]] * (m != 1):
                        load.wait()

                @pl.when(n == per_side)
                def _():
                    for load in [token_loads[1 if m < 2 else 3]] * (m != 1):
                        load.wait()

                products.append(jnp.dot(near[i, here], weights[m].reshape(D, HALF), preferred_element_type=f32))
            gate, upward, grad = products
            sigmoid = 1.0 / (1.0 + jnp.exp(-gate))
            silu = gate * sigmoid
            held[0, there] = (grad * upward * (sigmoid * (1.0 + gate * (1.0 - sigmoid)))).astype(bf16)
            held[1, there] = (grad * silu).astype(bf16)
            held[2, there] = (silu * upward).astype(bf16)
            back = sum(
                lax.dot_general(
                    held[m, there], weights[m].reshape(D, HALF), (((1,), (1,)), ((), ())), preferred_element_type=f32
                )
                for m in range(2)
            )
            grads[there] = back.astype(bf16)
            store_chunk(n, side, here, True)

            @pl.when(n == 0)
            def _():
                down_store.start()

            return 0

        down_store = pltpu.make_async_copy(weights.at[2], down, out_sems.at[0])
        lax.fori_loop(0, chunks, chunk, 0)
        down_store.wait()
        for n in range(chunks):
            store_chunk(n, n // per_side, pl.ds(n % per_side * step, step), False)

    outs = (
        pltpu.HBM((3, 2 * half, HALF), bf16),
        pltpu.HBM((half, D), bf16),
        pltpu.HBM((half, D), bf16),
        pltpu.HBM((WIDE, ROWS, HALF), bf16),
    )
    return pl.pallas_call(
        kernel,
        out_shape=outs,
        in_specs=[pl.BlockSpec(memory_space=pl.ANY)] * 5,
        out_specs=(pl.BlockSpec(memory_space=pl.ANY),) * 4,
        scratch_shapes=[
            pltpu.VMEM((3, WIDE, ROWS, HALF), bf16),
            pltpu.VMEM((3, 2 * half, HALF), bf16),
            pltpu.VMEM((4, half, D), bf16),
            pltpu.VMEM((2 * half, D), bf16),
            pltpu.SemaphoreType.DMA((24,)),
            pltpu.SemaphoreType.DMA((4,)),
            pltpu.SemaphoreType.DMA((1,)),
            pltpu.SemaphoreType.DMA((3 * chunks,)),
            pltpu.SemaphoreType.DMA((chunks,)),
        ],
        compiler_params=pltpu.CompilerParams(vmem_limit_bytes=40 << 20),
        cost_estimate=cost(20 * half * D * HALF, *tokens, gathered),
        name="ffn_rows",
    )(*(in_hbm(t) for t in tokens), gathered)


def ffn_back(name, rows, parts, weights, half, wait_for=()):
    count, pairs = rows.shape[1] // 2, len(parts)
    n, cut = 3, D // 3

    def kernel(*refs):
        out = refs[-1]
        for r in range(0, count, 256):
            out[r : r + 256] = sum(
                lax.dot_general(
                    refs[i][0, r : r + 256], refs[pairs + i][...], (((1,), (1,)), ((), ())), preferred_element_type=f32
                )
                for i in range(pairs)
            ).astype(bf16)

    out = whole((count, D))
    return pl.pallas_call(
        kernel,
        grid=(n,),
        out_shape=out,
        in_specs=[pl.BlockSpec((1, count, HALF), lambda j, m=m: (m, half, 0)) for m in parts]
        + [pl.BlockSpec((cut, HALF), lambda j: (j, 0))] * pairs
        + [pl.BlockSpec(memory_space=pl.ANY)] * len(wait_for),
        out_specs=pl.BlockSpec((count, cut), lambda j: (0, j)),
        compiler_params=pltpu.CompilerParams(vmem_limit_bytes=20 << 20),
        cost_estimate=cost(2 * pairs * count * D * HALF, out, out, out),
        name=name,
    )(*([in_hbm(rows)] * pairs), *(in_hbm(w) for w in weights), *wait_for)


def weight_grads(x_mine, x_other, c_mine, c_other, rows, wait_for):
    count = x_mine.shape[0]

    def kernel(xa, xb, ca, cb, r, *refs):
        out, mark = refs[-2:]
        mark[...] = jnp.zeros((8, 128), f32)

        def products(a, b):
            left = jnp.concatenate([a[...], b[...]], axis=0)
            part = lax.dot_general(left, r[0], (((0,), (0,)), ((), ())), preferred_element_type=f32).astype(bf16)
            for w in range(WIDE):
                y, rest = divmod(w, 8)
                x_lo, z = divmod(rest, 4)
                out[y * 8 + z * 2 + x_lo] = part[w * ROWS : (w + 1) * ROWS]

        @pl.when(pl.program_id(0) < 2)
        def _():
            products(xa, xb)

        @pl.when(pl.program_id(0) == 2)
        def _():
            products(ca, cb)

    left_spec = pl.BlockSpec((count, D), lambda m: (0, 0), pipeline_mode=pl.Buffered(1))
    return pl.pallas_call(
        kernel,
        grid=(3,),
        out_shape=(pltpu.HBM((WIDE, ROWS, 3 * HALF), bf16), whole((8, 128), f32)),
        in_specs=[left_spec] * 4
        + [pl.BlockSpec((1, 2 * count, HALF), lambda m: (m, 0, 0))]
        + [pl.BlockSpec(memory_space=pl.ANY)] * len(wait_for),
        out_specs=(
            pl.BlockSpec((WIDE, ROWS, HALF), lambda m: (0, 0, m)),
            pl.BlockSpec((8, 128), lambda m: (0, 0)),
        ),
        compiler_params=pltpu.CompilerParams(vmem_limit_bytes=46 << 20),
        cost_estimate=cost(12 * count * D * HALF, rows),
        name="weight_grads",
    )(*(in_hbm(v) for v in (x_mine, x_other, c_mine, c_other, rows)), *wait_for)


def pass_on(array, wait_for):
    def kernel(*refs):
        pass

    return pl.pallas_call(
        kernel,
        out_shape=pltpu.HBM(array.shape, array.dtype),
        in_specs=[pl.BlockSpec(memory_space=pl.ANY)] * (1 + len(wait_for)),
        out_specs=pl.BlockSpec(memory_space=pl.ANY),
        input_output_aliases={0: 0},
        compiler_params=pltpu.CompilerParams(vmem_limit_bytes=1 << 20),
        name="pass_on",
    )(in_hbm(array), *wait_for)


def rope_tables(position):
    halfway = HD // 2
    inverse = rope_base ** (-jnp.arange(halfway, dtype=f32) * 2.0 / HD)
    angles = position.astype(f32)[:, None] * inverse[None, :]
    angles = jnp.concatenate([angles, angles], axis=1)
    return jnp.cos(angles), jnp.sin(angles)


def dot(left, right, dims):
    return lax.dot_general(left, right, (dims, ((), ())), preferred_element_type=f32)


def per_device(
    inputs,
    norm_one,
    qkv_weight,
    qkv_bias,
    out_weight,
    norm_two,
    gate_weight,
    up_weight,
    down_weight,
    lengths,
    offsets,
    cotangent,
):
    place = Place()
    own = inputs.shape[0]
    zero = place.x_lo == 0
    with jax.named_scope("weights"):
        mine, other = prepare_ffn(place, (gate_weight, up_weight, down_weight.T))
        other = partner_x(other)
        blocks = prepare_attention(place, qkv_weight, out_weight, norm_one, norm_two, qkv_bias)
        blocks = lax.all_to_all(blocks, RING, 0, 0, tiled=True)
        inputs_away = other_core(inputs)
        got = send_ring(cotangent)
        message, quarter = gather_a(place, arrange(blocks, [inputs_away]), got[1:3])
        projections, lanes, quarters, sent = gather_b(place, message, quarter)
        block = by_x_lo(place, mine, other, [sent])
        gathered = lax.all_gather(block.reshape(2 * ROWS, 3 * HALF), ("y", "z"), axis=0, tiled=True)
        projections = projections.reshape(D, QKV)
    with jax.named_scope("layout"):
        start = place.x_hi * 2 * own
        ramp = jnp.arange(own, dtype=jnp.int32)
        slots = jnp.concatenate([start + place.core * own + ramp, start + (1 - place.core) * own + ramp])
        inside = (slots[:, None] >= offsets[0][None, :]) & (slots[:, None] < (offsets[0] + lengths[0])[None, :])
        position = jnp.sum(jnp.where(inside, slots[:, None] - offsets[0][None, :], 0), axis=1)
        cosine, sine = rope_tables(position)
        sine = jnp.where(jnp.arange(HD)[None, :] < HD // 2, -sine, sine)
    with jax.named_scope("attention"):
        normed_one, query, pair, gains = project(
            place, inputs, inputs_away, projections, lanes, cosine, sine, []
        )
        cotangent_mine = ring("ring_cotangent", got, [pair])
        cotangent_other = other_core(cotangent_mine)
        quarters.append(along_x(quarters[0], 2))
        pair_away = along_x(pair, 2)
        probs, attended = attend(place, query, pair, pair_away, lengths, offsets, quarters[1:])
        out_mine = gather_x(place, quarters, [pair]).reshape(D, HEADS)
        out_other = other_core(out_mine)
        middle, normed_two, every = branch(
            place, attended, other_core(attended), out_mine, out_other, inputs, gains, got[3:]
        )
    with jax.named_scope("ffn"):
        normed_mine = ring("ring_normed", send_ring(normed_two))
        normed_other = other_core(normed_mine)
        gathered = in_hbm(gathered.reshape(4, 4, 2, ROWS, 3 * HALF))
        rows, grad_mine, grad_other, down_full = ffn_rows(
            normed_mine, normed_other, cotangent_mine, cotangent_other, gathered
        )
        down_full = down_full.reshape(D, HALF)
        shares = scatter_ring("ring_grad", in_hbm(grad_mine), other_core(grad_other))
        wgrad, mark = weight_grads(normed_mine, normed_other, cotangent_mine, cotangent_other, rows, [shares[0]])
        wgrad = pass_on(wgrad, shares[1:])
        summed = lax.psum_scatter(wgrad.reshape(D, 3 * HALF), ("y", "z"), scatter_dimension=0, tiled=True)
    with jax.named_scope("attention_back"):
        middle_grad, two_grad, branch_mine, heads, away = branch_back(
            place, shares, in_hbm(middle), gains, cotangent, in_hbm(out_mine), in_hbm(out_other), [mark]
        )
        received = other_core(away)
        mixed, pair_own, pair_send = attend_back(
            in_hbm(probs),
            in_hbm(query),
            in_hbm(pair),
            in_hbm(pair_away),
            heads,
            received,
            in_hbm(cosine),
            in_hbm(sine),
            [],
        )
        out_grad = out_back(in_hbm(every), branch_mine, received, [mixed])
        one_mine, one_away, attn_shares = project_back(
            place,
            mixed,
            pair_own,
            along_x(pair_send, 2),
            in_hbm(cosine),
            in_hbm(sine),
            in_hbm(projections),
            in_hbm(normed_one),
            inputs,
            inputs_away,
            two_grad,
            out_grad,
            [],
        )
    with jax.named_scope("results"):
        part_other = ffn_back("ffn_out", rows, (2,), [down_full], 1, [one_mine])
        part_mine = ffn_back("ffn_out", rows, (2,), [down_full], 0, [part_other])
        shares, relayed = send_x(attn_shares)
        shares, _ = scatter_b(place, shares)
        output_shares = scatter_ring("ring_output", part_mine, in_hbm(other_core(part_other)), [relayed])
        output = (middle + add(*output_shares)).astype(bf16)
        source = inputs.astype(f32)
        inverse_one = lax.rsqrt(jnp.mean(source * source, axis=1, keepdims=True) + epsilon)
        scaled_one = (one_mine + other_core(one_away)) * gains[:1]
        input_grad = (
            middle_grad
            + inverse_one * scaled_one
            - source * inverse_one**3 * jnp.mean(scaled_one * source, axis=1, keepdims=True)
        )
        keep, gone = part_x_lo(place, in_hbm(summed.reshape(2, ROWS, 3 * HALF)), output_shares[:1])
        *ffn_grads, done = finish_ffn(place, keep, partner_x(gone), output_shares[1:])
        mine, gone = scatter_core(place, scatter_a(place, shares, [*output_shares[:3], keep]), [done])
        qkv_grad, out_grad, extra = finish(place, mine, other_core(gone))
        bias_grad = lax.dynamic_slice(extra, (0, 2 + 16 * place.narrow), (1, 16))[0]
    return (
        output,
        input_grad,
        extra[:, 0],
        qkv_grad,
        bias_grad,
        out_grad,
        extra[:, 1],
        ffn_grads[0],
        ffn_grads[1],
        ffn_grads[2].T,
    )


def solution(mesh):
    split_mesh = Mesh(mesh.devices.reshape(4, 2, 4, 2, 2), BOTH)
    return jax.shard_map(
        per_device,
        mesh=split_mesh,
        in_specs=(
            P(BOTH, None),
            P(BOTH),
            P(BOTH, None),
            P(BOTH),
            P(BOTH, None),
            P(BOTH),
            P(WIDE_AXES, NARROW_AXES),
            P(WIDE_AXES, NARROW_AXES),
            P(NARROW_AXES, WIDE_AXES),
            P(WIDE_AXES, None),
            P(WIDE_AXES, None),
            P(BOTH, None),
        ),
        out_specs=(
            P(BOTH, None),
            P(BOTH, None),
            P(BOTH),
            P(BOTH, None),
            P(BOTH),
            P(BOTH, None),
            P(BOTH),
            P(WIDE_AXES, NARROW_AXES),
            P(WIDE_AXES, NARROW_AXES),
            P(NARROW_AXES, WIDE_AXES),
        ),
        check_vma=False,
    )
```

```python
import math

import jax
import jax.numpy as jnp
from jax import lax
from jax.experimental import pallas as pl
from jax.experimental.pallas import tpu as pltpu
from jax.sharding import Mesh
from jax.sharding import PartitionSpec as P

D = 1536
QH = 12
KVH = 2
HD = 128
FF = 8960
GROUP = QH // KVH
HEADS = GROUP * HD
QKV = HEADS + 2 * HD
HALF = 1152
SPARE = FF // 4 - HALF
EXTRA = 128
WIDE = 32
ROWS = 48
WIDE_AXES = ("y", "x_lo", "z")
NARROW_AXES = ("x_hi", "core")
BOTH = WIDE_AXES + NARROW_AXES
RING = ("x_lo", "x_hi", "core")
epsilon = 1e-06
rope_base = 10000.0
bf16 = jnp.bfloat16
f32 = jnp.float32


def coords(index):
    wide, narrow = divmod(index, 4)
    y, rest = divmod(wide, 8)
    x_lo, z = divmod(rest, 4)
    x_hi, core = divmod(narrow, 2)
    return x_hi * 2 + x_lo, y, z, core


def number_of(x, y, z, core):
    x_hi, x_lo = divmod(x % 4, 2)
    return (((y % 4) * 2 + x_lo) * 4 + z % 4) * 4 + x_hi * 2 + core


def send(value, move):
    pairs = [(i, number_of(*move(*coords(i)))) for i in range(128)]
    return lax.ppermute(value, BOTH, pairs)


def other_core(value):
    return send(value, lambda x, y, z, c: (x, y, z, 1 - c))


def along_x(value, step):
    return send(value, lambda x, y, z, c: (x + step, y, z, c))


def partner_x(value):
    return send(value, lambda x, y, z, c: (x ^ 1, y, z, c))


def along_a(value, step):
    return send(value, lambda x, y, z, c: (x, y, z + step, c) if c == 0 else (x, y + step, z, c))


def along_b(value, step):
    return send(value, lambda x, y, z, c: (x, y + step, z, c) if c == 0 else (x, y, z + step, c))


class Place:
    def __init__(self):
        self.y, self.x_lo, self.z, self.x_hi, self.core = (lax.axis_index(axis) for axis in BOTH)
        self.narrow = self.x_hi * 2 + self.core
        self.x = self.x_hi * 2 + self.x_lo
        first = self.core == 0
        self.a = jnp.where(first, self.z, self.y)
        self.b = jnp.where(first, self.y, self.z)
        self.first = first

    def slot_a(self, x_lo, step):
        at = (self.a + step) % 4
        return jnp.where(self.first, x_lo * 4 + at, at * 2 + x_lo)

    def slot_b(self, j, step):
        at = (self.b + step) % 4
        return jnp.where(self.first, at * 8 + j, j * 4 + at)


STEPS = (0, -1, 1, 2)


def after(value, *others):
    return lax.optimization_barrier((value, *others))[0]


def whole(shape, dtype=bf16):
    return jax.ShapeDtypeStruct(shape, dtype)


def size(*arrays):
    return sum(math.prod(a.shape) * jnp.dtype(a.dtype).itemsize for a in arrays)


def cost(flops, *arrays):
    return pl.CostEstimate(flops=int(flops), bytes_accessed=int(size(*arrays)), transcendentals=0)


SCALARS = pl.BlockSpec(memory_space=pltpu.SMEM)
IN_VMEM = pl.BlockSpec(memory_space=pltpu.VMEM)
TOTAL = QKV + EXTRA + HEADS


def local(name, kernel, scalars, inputs, outs, scratch=(), extra=0, flops=0, wait_for=(), tables=()):
    outs = tuple(outs)
    held = sum(size(s) for s in scratch)
    n, m = len(tables) + len(inputs), len(wait_for)

    def body(at, *refs):
        kernel(at, *refs[:n], *refs[n + m :])

    return pl.pallas_call(
        body,
        out_shape=outs,
        in_specs=[SCALARS] * (1 + len(tables)) + [IN_VMEM] * len(inputs) + [pl.BlockSpec(memory_space=pl.ANY)] * m,
        out_specs=(IN_VMEM,) * len(outs),
        scratch_shapes=list(scratch),
        compiler_params=pltpu.CompilerParams(vmem_limit_bytes=int(size(*inputs, *outs) + held + extra + (2 << 20))),
        cost_estimate=cost(flops, *inputs, *outs),
        name=name,
    )(jnp.stack(scalars).astype(jnp.int32), *tables, *inputs, *wait_for)


def in_hbm(array):
    return pltpu.with_memory_space_constraint(array, pltpu.HBM)


def nothing():
    return [jnp.int32(0)]


PACKED = 2 * ROWS * HEADS // (QKV + EXTRA)


def pack(first, second):
    rows = jnp.concatenate([first, second], axis=0)
    tiles = jnp.concatenate([rows[:, i : i + 128] for i in range(0, HEADS, 128)], axis=0)
    return jnp.concatenate([tiles[i : i + PACKED] for i in range(0, tiles.shape[0], PACKED)], axis=1)


def unpack(packed):
    tiles = jnp.concatenate([packed[:, i : i + 128] for i in range(0, QKV + EXTRA, 128)], axis=0)
    rows = jnp.concatenate([tiles[i : i + 2 * ROWS] for i in range(0, tiles.shape[0], 2 * ROWS)], axis=1)
    return rows[:ROWS], rows[ROWS:]


def gather_a(place, block, wait_for):
    got = [block, *(along_a(block, step) for step in (1, -1, 2))]
    slots = [place.slot_a(x_lo, step) for step in STEPS for x_lo in range(2)]
    width = QKV + EXTRA

    def kernel(at, *refs):
        out, quarter, held = refs[4:]
        for k in range(4):
            for x_lo in range(2):
                slot = at[2 * k + x_lo]
                out[pl.ds(pl.multiple_of(slot * ROWS, ROWS), ROWS), :] = refs[k][x_lo, :, :width]
                held[slot] = refs[k][x_lo, :, width:]
        first, second = held[2 * at[8]], held[2 * at[8] + 1]
        out[8 * ROWS :] = pack(first, second)
        quarter[0], quarter[1] = first, second

    outs = [whole((8 * ROWS + PACKED, width)), whole((2, ROWS, HEADS))]
    scratch = [pltpu.VMEM((8, ROWS, HEADS), bf16)]
    return local("gather_a", kernel, slots + [place.x], got, outs, scratch, 2 << 20, wait_for=wait_for)


def gather_b(place, message, quarter):
    left, right = along_b(message, 1), along_b(message, -1)
    far = along_b(quarter, 2)
    half = 4 * ROWS

    def forward(at, left_ref, right_ref, top, bottom):
        top[...], bottom[...] = left_ref[:half], right_ref[half : 2 * half]

    def collect(at, near_ref, left_ref, right_ref, far_ref, out):
        for k, ref in enumerate((left_ref, right_ref)):
            out[2 * k + 2], out[2 * k + 3] = unpack(ref[2 * half :])
        for i in range(2):
            out[i], out[6 + i] = near_ref[i], far_ref[i]

    top, bottom = local("forward", forward, nothing(), [left, right], [whole((half, QKV + EXTRA))] * 2)
    sent, outs = top, [whole((8, ROWS, HEADS))]
    quarter = local("collect", collect, nothing(), [quarter, left, right, far], outs, (), 2 << 20, wait_for=[top])[0]
    quarters = [quarter, along_x(quarter, 1), along_x(quarter, -1)]
    top, bottom = along_b(top, 1), along_b(bottom, -1)

    def kernel(at, *refs):
        main, extra = refs[5:]
        for k in range(4):
            for j in range(8):
                source, spot = (k, j) if k < 3 else (3 + j // 4, j % 4)
                rows = slice(spot * ROWS, (spot + 1) * ROWS)
                main[at[8 * k + j]] = refs[source][rows, :QKV]
                extra[at[8 * k + j]] = refs[source][rows, QKV:]

    inputs = [message, left, right, top, bottom]
    outs = [whole((WIDE, ROWS, QKV)), whole((WIDE, ROWS, EXTRA))]
    main, extra = local("gather_b", kernel, slots_b(place), inputs, outs, (), 1 << 20)
    return main, extra, quarters, sent


def gather_x(place, quarters, wait_for):
    slots = []
    for back in (0, 1, 3, 2):
        x = (place.x - back) % 4
        slots += [place.slot_b(2 * x + i, step) for step in STEPS for i in range(2)]

    def kernel(at, *refs):
        for n in range(4):
            for k in range(8):
                refs[4][at[8 * n + k]] = refs[n][k]

    return local("gather_x", kernel, slots, quarters, [whole((WIDE, ROWS, HEADS))], wait_for=wait_for)[0]


def add(*terms):
    return sum(t.astype(f32) for t in terms)


def slots_b(place):
    return [place.slot_b(j, step) for step in STEPS for j in range(8)]


def send_x(shares):
    own, left, right, top, bottom = shares
    from_right, from_left = along_x(top, -1), along_x(bottom, 1)

    def kernel(at, left_ref, right_ref, top_ref, bottom_ref, left_out, right_out):
        left_out[:8] = (left_ref[:8].astype(f32) + top_ref[...].astype(f32)).astype(bf16)
        left_out[8:] = left_ref[8:]
        right_out[:8] = right_ref[:8]
        right_out[8:] = (right_ref[8:].astype(f32) + bottom_ref[...].astype(f32)).astype(bf16)

    inputs = [left, right, from_right, from_left]
    left, right = local("relay", kernel, nothing(), inputs, [whole(left.shape)] * 2, (), 4 << 20)
    return [own, along_x(left, -1), along_x(right, 1)], left


def scatter_b(place, shares):
    slots = []
    for step in STEPS:
        at = (place.b + step) % 4
        slots += [jnp.where(place.first, at * 4 + a, a * 4 + at) for a in range(4)]

    def kernel(at, *refs):
        for k in range(4):
            for a in range(4):
                spot = at[4 * k + a]
                total = sum(refs[n][spot].astype(f32) for n in range(3))
                refs[3 + k][a] = total.astype(bf16)

    outs = [whole((4, *shares[0].shape[1:]))] * 4
    own, left, right, opposite = local("scatter_b", kernel, slots, shares, outs, (), 2 << 20)
    return [own, along_b(left, -1), along_b(right, 1), along_b(opposite, 2)], own


def scatter_a(place, shares, wait_for):
    slots = [(place.a + step) % 4 for step in STEPS]

    def kernel(at, *refs):
        for k in range(4):
            total = sum(refs[n][at[k]].astype(f32) for n in range(4))
            refs[4 + k][...] = total.astype(bf16)

    outs = [whole(shares[0].shape[1:])] * 4
    own, left, right, opposite = local("scatter_a", kernel, slots, shares, outs, (), 2 << 20, wait_for=wait_for)
    return [own, along_a(left, -1), along_a(right, 1), along_a(opposite, 2)]


def scatter_core(place, shares, wait_for):
    width = shares[0].shape[1]

    def kernel(at, *refs):
        total = sum(refs[n][...].astype(f32) for n in range(4))
        first, low, high = at[0] == 0, total[:12], total[12:]
        refs[4][...] = jnp.where(first, low, high)
        refs[5][...] = jnp.where(first, high, low).astype(bf16)

    outs = [whole((12, width), f32), whole((12, width))]
    return local("scatter_core", kernel, [place.core], shares, outs, (), 2 << 20, wait_for=wait_for)


def arrange(got, wait_for):
    width = got.shape[2]

    def kernel(at, source, out, rows):
        for x_lo in range(2):
            for k in range(4):
                rows[x_lo, 12 * k : 12 * k + 12, :] = source[x_lo * 4 + k].astype(f32)
        out[...] = rows[...].astype(bf16)

    scratch = [pltpu.VMEM((2, ROWS, width), f32)]
    return local("arrange", kernel, nothing(), [got], [whole((2, ROWS, width))], scratch, wait_for=wait_for)[0]


def finish(place, mine, received):
    def kernel(at, mine_ref, got, qkv, out, extra):
        first, a, b = at[0] == 0, mine_ref[...], got[...].astype(f32)
        low, high = jnp.where(first, a, b), jnp.where(first, b, a)
        qkv[:, :HEADS], qkv[:, HEADS:D] = low[:, :HEADS], high[:, :HEADS]
        for i in range(2):
            cut = slice(HEADS + i * HD, HEADS + (i + 1) * HD)
            at_lane = D + 2 * i * HD
            qkv[:, at_lane : at_lane + HD], qkv[:, at_lane + HD : at_lane + 2 * HD] = low[:, cut], high[:, cut]
        extra[...] = (a + b)[:, QKV : QKV + EXTRA]
        out[:, :HEADS], out[:, HEADS:] = low[:, QKV + EXTRA :], high[:, QKV + EXTRA :]

    outs = (whole((12, 2 * QKV), f32), whole((12, D), f32), whole((12, EXTRA), f32))
    return local("finish", kernel, [place.core], [mine, received], outs)


def send_ring(rows):
    return [rows, along_x(rows, 1), along_x(rows, -1), along_x(rows, 2)]


def ring(name, got, wait_for=()):
    def kernel(at, *refs):
        for k in range(4):
            refs[4][128 * k : 128 * (k + 1)] = refs[k][...]

    return local(name, kernel, nothing(), got, [whole((512, D))], wait_for=wait_for)[0]


def scatter_ring(name, mine, other, wait_for=()):
    def kernel(at, mine_ref, other_ref, own, *rest):
        for k in range(4):
            rows = slice(128 * k, 128 * (k + 1))
            total = mine_ref[rows].astype(f32) + other_ref[rows].astype(f32)
            if k == 0:
                own[...] = total
            else:
                rest[k - 1][...] = total.astype(bf16)

    outs = [whole((128, D), f32)] + [whole((128, D))] * 3
    own, left, right, opposite = local(name, kernel, nothing(), [mine, other], outs, wait_for=wait_for)
    return [own, along_x(left, -1), along_x(right, 1), along_x(opposite, 2)]


def select(first, low, high):
    return jnp.where(first, low.astype(f32), high.astype(f32))


def turn(values, cosine, sine):
    return values * cosine + pltpu.roll(values, HD // 2, 1) * sine


def project(place, inputs, inputs_away, projections, lanes, cosine, sine, wait_for):
    tokens = 256

    def kernel(at, own, away, weight, lane_ref, cos_ref, sin_ref, normed, query, pair, gains):
        first = at[0] == 0
        table = lane_ref[...].astype(f32)
        gains_all = jnp.transpose(table.reshape(D, EXTRA))
        gains[...] = gains_all[:8]
        sums = jnp.sum(table, axis=1)
        left, right = pltpu.roll(sums, EXTRA - 2, 1), pltpu.roll(sums, 62, 1)
        lane = lax.broadcasted_iota(jnp.int32, (1, EXTRA), 1)

        def bias_at(low, high):
            def tile(j):
                return jnp.where(lane < 64, left[2 * j : 2 * j + 1], right[2 * j + 1 : 2 * j + 2])

            return jnp.where(first, tile(low), tile(high))

        for half, ref in enumerate((own, away)):
            rows = slice(128 * half, 128 * (half + 1))
            x = ref[...].astype(f32)
            inverse = lax.rsqrt(jnp.mean(x * x, axis=1, keepdims=True) + epsilon)
            normed[rows] = (x * inverse * gains_all[:1]).astype(bf16)
        cos, sin = cos_ref[...], sin_ref[...]
        mixed = jnp.dot(normed[...], weight[...], preferred_element_type=f32)
        for h in range(GROUP):
            values = mixed[:, h * HD : (h + 1) * HD] + bias_at(h, GROUP + h)
            query[h] = turn(values, cos, sin).astype(bf16)
        key = mixed[:, HEADS : HEADS + HD] + bias_at(12, 13)
        pair[:, :HD] = turn(key, cos, sin).astype(bf16)
        pair[:, HD:] = (mixed[:, HEADS + HD :] + bias_at(14, 15)).astype(bf16)

    outs = [whole((tokens, D)), whole((GROUP, tokens, HD)), whole((tokens, 2 * HD)), whole((8, D), f32)]
    inputs = [inputs, inputs_away, projections, lanes, cosine, sine]
    flops = 2 * tokens * D * QKV
    return local("project", kernel, [place.core], inputs, outs, extra=8 << 20, flops=flops, wait_for=wait_for)


def attend(place, query, pair, pair_away, lengths, offsets, wait_for):
    tokens = 256
    scale = HD**-0.5

    def kernel(at, offset, length, query_ref, own, away, probs, attended):
        core, start = at[0], at[1]
        off_a, off_b, len_a, len_b = offset[0, 0], offset[0, 1], length[0, 0], length[0, 1]

        def slot_of(index, base):
            other = index >= 128
            return base + jnp.where(other, (1 - core) * 128 - 128, core * 128) + index

        def which(slot):
            in_a = (slot >= off_a) & (slot < off_a + len_a)
            in_b = (slot >= off_b) & (slot < off_b + len_b)
            return jnp.where(in_a, 0, jnp.where(in_b, 1, -1))

        rows = slot_of(lax.broadcasted_iota(jnp.int32, (tokens, 1), 0), start)
        lane = lax.broadcasted_iota(jnp.int32, (1, 2 * tokens), 1)
        columns = jnp.where(lane < tokens, slot_of(lane, start), slot_of(lane - tokens, tokens - start))
        number, key_number = which(rows), which(columns)
        allowed = ((number == key_number) & (number >= 0) & (columns <= rows)) | (columns == rows)
        keys = jnp.concatenate([own[:, :HD], away[:, :HD]], axis=0)
        values = jnp.concatenate([own[:, HD:], away[:, HD:]], axis=0)
        for h in range(GROUP):
            scores = lax.dot_general(query_ref[h], keys, (((1,), (1,)), ((), ())), preferred_element_type=f32) * scale
            scores = jnp.where(allowed, scores, -1e30)
            raised = jnp.exp(scores - jnp.max(scores, axis=1, keepdims=True))
            result = raised * (1.0 / jnp.sum(raised, axis=1, keepdims=True))
            probs[h] = result
            attended[:, h * HD : (h + 1) * HD] = jnp.dot(
                result.astype(bf16), values, preferred_element_type=f32
            ).astype(bf16)

    scalars, tables = [place.core, place.x_hi * tokens], [offsets, lengths]
    outs = [whole((GROUP, tokens, 2 * tokens), f32), whole((tokens, HEADS))]
    flops = 8 * GROUP * tokens * tokens * HD
    return local(
        "attend", kernel, scalars, [query, pair, pair_away], outs, (), 6 << 20, flops, wait_for, tables
    )


def branch(place, attended, attended_away, out_mine, out_other, inputs, gains, wait_for):
    def kernel(at, mine, away, weight, weight_away, x_ref, gain, middle, normed, every):
        first = at[0] == 0
        for half, (a, b) in enumerate(((mine[:128], away[128:]), (mine[128:], away[:128]))):
            rows = slice(128 * half, 128 * (half + 1))
            every[rows, :HEADS] = select(first, a, b).astype(bf16)
            every[rows, HEADS:] = select(first, b, a).astype(bf16)
        left = every[:128]
        a = jnp.dot(left, weight[...], preferred_element_type=f32)
        b = jnp.dot(left, weight_away[...], preferred_element_type=f32)
        x = x_ref[...].astype(f32)
        low = x[:, :HEADS] + jnp.where(first, a, b)
        high = x[:, HEADS:] + jnp.where(first, b, a)
        middle[:, :HEADS], middle[:, HEADS:] = low, high
        squares = jnp.sum(low * low, axis=1, keepdims=True) + jnp.sum(high * high, axis=1, keepdims=True)
        inverse = lax.rsqrt(squares * (1.0 / D) + epsilon)
        normed[:, :HEADS] = (low * inverse * gain[1:2, :HEADS]).astype(bf16)
        normed[:, HEADS:] = (high * inverse * gain[1:2, HEADS:]).astype(bf16)

    outs = [whole((128, D), f32), whole((128, D)), whole((256, D))]
    inputs = [attended, attended_away, out_mine, out_other, inputs, gains]
    return local(
        "branch", kernel, [place.core], inputs, outs, extra=6 << 20, flops=2 * 128 * D * D, wait_for=wait_for
    )


def branch_back(place, shares, middle, gains, cotangent, out_mine, out_other, wait_for):
    def kernel(at, own, left, right, opposite, mid_ref, gain, cot, weight, weight_away, grad, gain_grad, mine, heads, away):
        first = at[0] == 0
        total = own[...] + left[...].astype(f32) + right[...].astype(f32) + opposite[...].astype(f32)
        mid = mid_ref[...]
        inverse = lax.rsqrt(jnp.mean(mid * mid, axis=1, keepdims=True) + epsilon)
        scaled = total * gain[1:2]
        mean = jnp.mean(scaled * mid, axis=1, keepdims=True)
        result = cot[...].astype(f32) + inverse * scaled - mid * (inverse * inverse * inverse * mean)
        grad[...] = result
        gain_grad[...] = jnp.sum(total * mid * inverse, axis=0, keepdims=True)
        low, high = result[:, :HEADS], result[:, HEADS:]
        mine[...] = jnp.where(first, low, high).astype(bf16)
        away[:, :HEADS] = jnp.where(first, high, low).astype(bf16)
        back = lax.dot_general(mine[...], weight[...], (((1,), (1,)), ((), ())), preferred_element_type=f32)
        back += lax.dot_general(
            away[:, :HEADS], weight_away[...], (((1,), (1,)), ((), ())), preferred_element_type=f32
        )
        low, high = back[:, :HEADS], back[:, HEADS:]
        heads[...] = jnp.where(first, low, high).astype(bf16)
        away[:, HEADS:] = jnp.where(first, high, low).astype(bf16)

    outs = [whole((128, D), f32), whole((1, D), f32), whole((128, HEADS)), whole((128, HEADS)), whole((128, D))]
    inputs = [*shares, middle, gains, cotangent, out_mine, out_other]
    return local(
        "branch_back", kernel, [place.core], inputs, outs, extra=8 << 20, flops=2 * 128 * D * D, wait_for=wait_for
    )


def attend_back(probs, query, pair, pair_away, heads, received, cosine, sine, wait_for):
    tokens = 256
    scale = HD**-0.5

    def kernel(at, probs_ref, query_ref, own, away, mine, others, cos_ref, sin_ref, mixed, pair_own, pair_send, total):
        keys = jnp.concatenate([own[:, :HD], away[:, :HD]], axis=0)
        values = jnp.concatenate([own[:, HD:], away[:, HD:]], axis=0)
        cos, sin = cos_ref[...], sin_ref[...]
        for h in range(GROUP):
            cut = slice(h * HD, (h + 1) * HD)
            grad = jnp.concatenate([mine[:, cut], others[:, HEADS + h * HD : HEADS + (h + 1) * HD]], axis=0)
            p = probs_ref[h]
            by_prob = lax.dot_general(grad, values, (((1,), (1,)), ((), ())), preferred_element_type=f32)
            row = jnp.sum(p * by_prob, axis=1, keepdims=True)
            by_score = (p * (by_prob - row)).astype(bf16)
            by_query = jnp.dot(by_score, keys, preferred_element_type=f32) * scale
            mixed[:, cut] = turn(by_query, cos, -sin).astype(bf16)
            by_key = lax.dot_general(by_score, query_ref[h], (((0,), (0,)), ((), ())), preferred_element_type=f32)
            by_value = lax.dot_general(p.astype(bf16), grad, (((0,), (0,)), ((), ())), preferred_element_type=f32)
            if h == 0:
                total[:, :HD], total[:, HD:] = by_key * scale, by_value
            else:
                total[:, :HD] += by_key * scale
                total[:, HD:] += by_value
        pair_own[...] = total[:tokens]
        pair_send[...] = total[tokens:].astype(bf16)

    outs = [whole((tokens, HEADS)), whole((tokens, 2 * HD), f32), whole((tokens, 2 * HD))]
    inputs = [probs, query, pair, pair_away, heads, received, cosine, sine]
    scratch = [pltpu.VMEM((2 * tokens, 2 * HD), f32)]
    flops = 20 * GROUP * tokens * tokens * HD
    return local("attend_back", kernel, nothing(), inputs, outs, scratch, 8 << 20, flops, wait_for)


def out_back(every, mine, received, wait_for):
    def kernel(at, every_ref, mine_ref, others, out):
        both = jnp.concatenate([mine_ref[...], others[:, :HEADS]], axis=0)
        for r in range(0, D, 384):
            part = lax.dot_general(
                every_ref[:, r : r + 384], both, (((0,), (0,)), ((), ())), preferred_element_type=f32
            )
            out[r // 24 : r // 24 + 16] = part.reshape(16, 24, HEADS).astype(bf16)

    flops = 2 * 256 * D * HEADS
    inputs = [every, mine, received]
    return local("out_back", kernel, nothing(), inputs, [whole((2 * WIDE, 24, HEADS))], (), 6 << 20, flops, wait_for)[0]


def project_back(place, mixed, pair_own, pair_received, cosine, sine, projections, normed, inputs, inputs_away, two, out,
                 wait_for):
    width = QKV + EXTRA

    def kernel(at, mix, own_ref, got, cos_ref, sin_ref, weight, norm_ref, x_ref, x_away, two_ref, out_ref, mine, away, *rest):
        shares, (held, grads, rows) = rest[:5], rest[5:]
        core = at[4]
        total = own_ref[...] + got[...].astype(f32)
        grads[:, :HEADS] = mix[...]
        grads[:, HEADS : HEADS + HD] = turn(total[:, :HD], cos_ref[...], -sin_ref[...]).astype(bf16)
        grads[:, HEADS + HD :] = total[:, HD:].astype(bf16)
        one = jnp.zeros((1, D), f32)
        for half, (x_from, ref) in enumerate(((x_ref, mine), (x_away, away))):
            part = lax.dot_general(
                grads[128 * half : 128 * (half + 1)],
                weight[...],
                (((1,), (1,)), ((), ())),
                preferred_element_type=f32,
            )
            ref[...] = part
            x = x_from[...].astype(f32)
            inverse = lax.rsqrt(jnp.mean(x * x, axis=1, keepdims=True) + epsilon)
            one += jnp.sum(part * x * inverse, axis=0, keepdims=True)
        for r in range(0, D, 384):
            part = lax.dot_general(
                norm_ref[:, r : r + 384], grads[...], (((0,), (0,)), ((), ())), preferred_element_type=f32
            )
            held[r // 24 : r // 24 + 16, :, :QKV] = part.reshape(16, 24, QKV).astype(bf16)
        rows[...] = jnp.zeros((EXTRA, D), f32)
        rows[0:1], rows[1:2] = one, two_ref[...]
        held[:, :, QKV:] = jnp.transpose(rows[...]).reshape(2 * WIDE, 24, EXTRA).astype(bf16)
        bias = jnp.sum(grads[...].astype(f32), axis=0, keepdims=True)
        lane = lax.broadcasted_iota(jnp.int32, (24, EXTRA), 1)
        row = lax.broadcasted_iota(jnp.int32, (24, EXTRA), 0)
        spot = (lane >= 2) & (lane < 66) & (lax.rem(row, 12) == 0)
        for i in range(8):
            tile = bias[:, i * HD : (i + 1) * HD]
            base = 12 * core + 2 * i if i < GROUP else 24 + 4 * (i - GROUP) + 2 * core
            for odd, shift in ((0, 2), (1, 66)):
                moved = pltpu.roll(tile, shift, 1)
                for half in range(2):
                    at_block = 2 * (base + odd) + half
                    before = held[at_block, :, QKV:].astype(f32)
                    held[at_block, :, QKV:] = jnp.where(spot, moved, before).astype(bf16)
        for k in range(4):
            for n in range(16):
                ref, spot = (shares[k], n) if k < 3 else (shares[3 + n // 8], n % 8)
                source = at[k] + n // 4 * 16 + n % 4 * 2
                ref[spot, :, :width] = held[source]
                ref[spot, :, width:] = out_ref[source]

    outs = [whole((128, D), f32)] * 2 + [whole((n, 24, TOTAL)) for n in (16, 16, 16, 8, 8)]
    scratch = [pltpu.VMEM((2 * WIDE, 24, width), bf16), pltpu.VMEM((256, QKV), bf16), pltpu.VMEM((EXTRA, D), f32)]
    inputs = [mixed, pair_own, pair_received, cosine, sine, projections, normed, inputs, inputs_away, two, out]
    scalars = [x % 2 * 8 + x // 2 for x in ((place.x + step) % 4 for step in STEPS)] + [place.core]
    flops = 4 * 256 * D * QKV
    mine, away, *shares = local("project_back", kernel, scalars, inputs, outs, scratch, 14 << 20, flops, wait_for)
    return mine, away, shares


def prepare_attention(place, qkv_weight, out_weight, norm_one, norm_two, qkv_bias):
    def kernel(at, qkv, out, one, two, bias, result):
        narrow = at[0]
        lane = lax.broadcasted_iota(jnp.int32, (12, EXTRA), 1)
        row = lax.broadcasted_iota(jnp.int32, (12, EXTRA), 0)
        diagonal = lax.broadcasted_iota(jnp.int32, (12, 12), 0) == lax.broadcasted_iota(jnp.int32, (12, 12), 1)

        def column(gain):
            return jnp.sum(jnp.where(diagonal, gain[...].astype(f32), 0.0), axis=1, keepdims=True)

        extra = jnp.where(lane == 0, column(one), 0.0) + jnp.where(lane == 1, column(two), 0.0)
        spread = jnp.concatenate([bias[...].astype(f32)] * 8, axis=1)
        base = 2 + 16 * narrow
        shifted = pltpu.roll(spread, 2, 1)
        extra = extra + jnp.where((row == 0) & (lane >= base) & (lane < base + 16), shifted, 0.0)
        extra = extra.astype(bf16)
        for k in range(8):
            c = k % 2
            result[k, :, :HEADS] = qkv[:, c * HEADS : (c + 1) * HEADS]
            for i in range(2):
                at_lane = D + (2 * i + c) * HD
                result[k, :, HEADS + i * HD : HEADS + (i + 1) * HD] = qkv[:, at_lane : at_lane + HD]
            result[k, :, QKV : QKV + EXTRA] = extra
            result[k, :, QKV + EXTRA :] = out[:, c * HEADS : (c + 1) * HEADS]

    inputs = [
        in_hbm(a)
        for a in (qkv_weight, out_weight, norm_one.reshape(1, 12), norm_two.reshape(1, 12), qkv_bias.reshape(1, 16))
    ]
    return local("prepare_attention", kernel, [place.narrow], inputs, [whole((8, 12, TOTAL))])[0]


def prepare_ffn(place, weights):
    def kernel(at, gate, up, down, mine, other):
        zero = at[0] == 0
        for i, weight in enumerate((gate, up, down)):
            low = weight[:, :HALF].astype(f32)
            high = jnp.concatenate([weight[:, HALF:].astype(f32), jnp.zeros((ROWS, HALF - SPARE), f32)], axis=1)
            mine[:, i * HALF : (i + 1) * HALF] = jnp.where(zero, low, high).astype(bf16)
            other[:, i * HALF : (i + 1) * HALF] = jnp.where(zero, high, low).astype(bf16)

    outs = (whole((ROWS, 3 * HALF)),) * 2
    return local("prepare_ffn", kernel, [place.x_lo], [in_hbm(w) for w in weights], outs)


def by_x_lo(place, mine, other, wait_for):
    def kernel(at, mine_ref, other_ref, out):
        out[at[0]] = mine_ref[...]
        out[1 - at[0]] = other_ref[...]

    return local("by_x_lo", kernel, [place.x_lo], [mine, other], [whole((2, *mine.shape))], wait_for=wait_for)[0]


def part_x_lo(place, both, wait_for):
    def kernel(at, source, mine, other):
        mine[...] = source[at[0]]
        other[...] = source[1 - at[0]]

    return local("part_x_lo", kernel, [place.x_lo], [both], [whole(both.shape[1:])] * 2, wait_for=wait_for)


def finish_ffn(place, keep, gone, wait_for):
    def kernel(at, keep_ref, gone_ref, *outs):
        zero, (*outs, mark) = at[0] == 0, outs
        mark[...] = jnp.zeros((8, 128), f32)
        for i, out in enumerate(outs):
            a = keep_ref[:, i * HALF : (i + 1) * HALF].astype(f32)
            b = gone_ref[:, i * HALF : (i + 1) * HALF].astype(f32)
            out[:, :HALF] = jnp.where(zero, a, b)
            out[:, HALF:] = jnp.where(zero, b, a)[:, :SPARE]

    outs = [whole((ROWS, HALF + SPARE), f32)] * 3 + [whole((8, 128), f32)]
    return local("finish_ffn", kernel, [place.x_lo], [keep, gone], outs, wait_for=wait_for)


def ffn_rows(x_mine, x_other, c_mine, c_other, gathered):
    half, step = x_mine.shape[0], 256
    chunks = 2 * half // step
    tokens = (x_mine, x_other, c_mine, c_other)

    def kernel(*refs):
        far_tokens, source, rows, mine, other, down = refs[:4], *refs[4:9]
        weights, held, near, grads, sems, token_sems, out_sems, row_sems, grad_sems = refs[9:]
        loads = [[] for _ in range(3)]
        token_loads = [pltpu.make_async_copy(far_tokens[i], near.at[i], token_sems.at[i]) for i in range(4)]

        def load_weight(m):
            for y in range(4):
                for x_lo in range(2):
                    load = pltpu.make_async_copy(
                        source.at[y, :, x_lo, :, pl.ds(m * HALF, HALF)],
                        weights.at[m, pl.ds(y * 8 + x_lo * 4, 4)],
                        sems.at[(m * 4 + y) * 2 + x_lo],
                    )
                    load.start()
                    loads[m].append(load)

        token_loads[0].start()
        load_weight(0)
        load_weight(1)
        token_loads[2].start()
        load_weight(2)
        token_loads[1].start()
        token_loads[3].start()
        per_side = half // step

        def store_chunk(n, side, here, start):
            there = pl.ds(pl.multiple_of(n * step, step), step)
            for i in range(3):
                copy = pltpu.make_async_copy(held.at[i, there], rows.at[i, there], row_sems.at[3 * n + i])
                copy.start() if start else copy.wait()
            for k, out in enumerate((mine, other)):

                @pl.when(side == k)
                def _():
                    copy = pltpu.make_async_copy(grads.at[there], out.at[here], grad_sems.at[n])
                    copy.start() if start else copy.wait()

        def chunk(n, _):
            side, here = n // per_side, pl.ds(pl.multiple_of(lax.rem(n, per_side) * step, step), step)
            there = pl.ds(pl.multiple_of(n * step, step), step)
            products = []
            for m in range(3):
                i = side if m < 2 else 2 + side

                @pl.when(n == 0)
                def _():
                    for load in loads[m] + [token_loads[0 if m < 2 else 2]] * (m != 1):
                        load.wait()

                @pl.when(n == per_side)
                def _():
                    for load in [token_loads[1 if m < 2 else 3]] * (m != 1):
                        load.wait()

                products.append(jnp.dot(near[i, here], weights[m].reshape(D, HALF), preferred_element_type=f32))
            gate, upward, grad = products
            sigmoid = 1.0 / (1.0 + jnp.exp(-gate))
            silu = gate * sigmoid
            held[0, there] = (grad * upward * (sigmoid * (1.0 + gate * (1.0 - sigmoid)))).astype(bf16)
            held[1, there] = (grad * silu).astype(bf16)
            held[2, there] = (silu * upward).astype(bf16)
            back = sum(
                lax.dot_general(
                    held[m, there], weights[m].reshape(D, HALF), (((1,), (1,)), ((), ())), preferred_element_type=f32
                )
                for m in range(2)
            )
            grads[there] = back.astype(bf16)
            store_chunk(n, side, here, True)

            @pl.when(n == 0)
            def _():
                down_store.start()

            return 0

        down_store = pltpu.make_async_copy(weights.at[2], down, out_sems.at[0])
        lax.fori_loop(0, chunks, chunk, 0)
        down_store.wait()
        for n in range(chunks):
            store_chunk(n, n // per_side, pl.ds(n % per_side * step, step), False)

    outs = (
        pltpu.HBM((3, 2 * half, HALF), bf16),
        pltpu.HBM((half, D), bf16),
        pltpu.HBM((half, D), bf16),
        pltpu.HBM((WIDE, ROWS, HALF), bf16),
    )
    return pl.pallas_call(
        kernel,
        out_shape=outs,
        in_specs=[pl.BlockSpec(memory_space=pl.ANY)] * 5,
        out_specs=(pl.BlockSpec(memory_space=pl.ANY),) * 4,
        scratch_shapes=[
            pltpu.VMEM((3, WIDE, ROWS, HALF), bf16),
            pltpu.VMEM((3, 2 * half, HALF), bf16),
            pltpu.VMEM((4, half, D), bf16),
            pltpu.VMEM((2 * half, D), bf16),
            pltpu.SemaphoreType.DMA((24,)),
            pltpu.SemaphoreType.DMA((4,)),
            pltpu.SemaphoreType.DMA((1,)),
            pltpu.SemaphoreType.DMA((3 * chunks,)),
            pltpu.SemaphoreType.DMA((chunks,)),
        ],
        compiler_params=pltpu.CompilerParams(vmem_limit_bytes=40 << 20),
        cost_estimate=cost(20 * half * D * HALF, *tokens, gathered),
        name="ffn_rows",
    )(*(in_hbm(t) for t in tokens), gathered)


def ffn_back(name, rows, parts, weights, half, wait_for=()):
    count, pairs = rows.shape[1] // 2, len(parts)
    n, cut = 3, D // 3

    def kernel(*refs):
        out = refs[-1]
        for r in range(0, count, 256):
            out[r : r + 256] = sum(
                lax.dot_general(
                    refs[i][0, r : r + 256], refs[pairs + i][...], (((1,), (1,)), ((), ())), preferred_element_type=f32
                )
                for i in range(pairs)
            ).astype(bf16)

    out = whole((count, D))
    return pl.pallas_call(
        kernel,
        grid=(n,),
        out_shape=out,
        in_specs=[pl.BlockSpec((1, count, HALF), lambda j, m=m: (m, half, 0)) for m in parts]
        + [pl.BlockSpec((cut, HALF), lambda j: (j, 0))] * pairs
        + [pl.BlockSpec(memory_space=pl.ANY)] * len(wait_for),
        out_specs=pl.BlockSpec((count, cut), lambda j: (0, j)),
        compiler_params=pltpu.CompilerParams(vmem_limit_bytes=20 << 20),
        cost_estimate=cost(2 * pairs * count * D * HALF, out, out, out),
        name=name,
    )(*([in_hbm(rows)] * pairs), *(in_hbm(w) for w in weights), *wait_for)


def weight_grads(x_mine, x_other, c_mine, c_other, rows, wait_for):
    count = x_mine.shape[0]

    def kernel(xa, xb, ca, cb, r, *refs):
        out, mark = refs[-2:]
        mark[...] = jnp.zeros((8, 128), f32)

        def products(a, b):
            left = jnp.concatenate([a[...], b[...]], axis=0)
            part = lax.dot_general(left, r[0], (((0,), (0,)), ((), ())), preferred_element_type=f32).astype(bf16)
            for w in range(WIDE):
                y, rest = divmod(w, 8)
                x_lo, z = divmod(rest, 4)
                out[y * 8 + z * 2 + x_lo] = part[w * ROWS : (w + 1) * ROWS]

        @pl.when(pl.program_id(0) < 2)
        def _():
            products(xa, xb)

        @pl.when(pl.program_id(0) == 2)
        def _():
            products(ca, cb)

    left_spec = pl.BlockSpec((count, D), lambda m: (0, 0), pipeline_mode=pl.Buffered(1))
    return pl.pallas_call(
        kernel,
        grid=(3,),
        out_shape=(pltpu.HBM((WIDE, ROWS, 3 * HALF), bf16), whole((8, 128), f32)),
        in_specs=[left_spec] * 4
        + [pl.BlockSpec((1, 2 * count, HALF), lambda m: (m, 0, 0))]
        + [pl.BlockSpec(memory_space=pl.ANY)] * len(wait_for),
        out_specs=(
            pl.BlockSpec((WIDE, ROWS, HALF), lambda m: (0, 0, m)),
            pl.BlockSpec((8, 128), lambda m: (0, 0)),
        ),
        compiler_params=pltpu.CompilerParams(vmem_limit_bytes=46 << 20),
        cost_estimate=cost(12 * count * D * HALF, rows),
        name="weight_grads",
    )(*(in_hbm(v) for v in (x_mine, x_other, c_mine, c_other, rows)), *wait_for)


def pass_on(array, wait_for):
    def kernel(*refs):
        pass

    return pl.pallas_call(
        kernel,
        out_shape=pltpu.HBM(array.shape, array.dtype),
        in_specs=[pl.BlockSpec(memory_space=pl.ANY)] * (1 + len(wait_for)),
        out_specs=pl.BlockSpec(memory_space=pl.ANY),
        input_output_aliases={0: 0},
        compiler_params=pltpu.CompilerParams(vmem_limit_bytes=1 << 20),
        name="pass_on",
    )(in_hbm(array), *wait_for)


def rope_tables(position):
    halfway = HD // 2
    inverse = rope_base ** (-jnp.arange(halfway, dtype=f32) * 2.0 / HD)
    angles = position.astype(f32)[:, None] * inverse[None, :]
    angles = jnp.concatenate([angles, angles], axis=1)
    return jnp.cos(angles), jnp.sin(angles)


def dot(left, right, dims):
    return lax.dot_general(left, right, (dims, ((), ())), preferred_element_type=f32)


def per_device(
    inputs,
    norm_one,
    qkv_weight,
    qkv_bias,
    out_weight,
    norm_two,
    gate_weight,
    up_weight,
    down_weight,
    lengths,
    offsets,
    cotangent,
):
    place = Place()
    own = inputs.shape[0]
    zero = place.x_lo == 0
    with jax.named_scope("weights"):
        mine, other = prepare_ffn(place, (gate_weight, up_weight, down_weight.T))
        other = partner_x(other)
        blocks = prepare_attention(place, qkv_weight, out_weight, norm_one, norm_two, qkv_bias)
        blocks = lax.all_to_all(blocks, RING, 0, 0, tiled=True)
        inputs_away = other_core(inputs)
        got = send_ring(cotangent)
        message, quarter = gather_a(place, arrange(blocks, [inputs_away]), got[1:3])
        projections, lanes, quarters, sent = gather_b(place, message, quarter)
        block = pass_on(by_x_lo(place, mine, other, [message]), [sent])
        gathered = lax.all_gather(block.reshape(2 * ROWS, 3 * HALF), ("y", "z"), axis=0, tiled=True)
        projections = projections.reshape(D, QKV)
    with jax.named_scope("layout"):
        start = place.x_hi * 2 * own
        ramp = jnp.arange(own, dtype=jnp.int32)
        slots = jnp.concatenate([start + place.core * own + ramp, start + (1 - place.core) * own + ramp])
        inside = (slots[:, None] >= offsets[0][None, :]) & (slots[:, None] < (offsets[0] + lengths[0])[None, :])
        position = jnp.sum(jnp.where(inside, slots[:, None] - offsets[0][None, :], 0), axis=1)
        cosine, sine = rope_tables(position)
        sine = jnp.where(jnp.arange(HD)[None, :] < HD // 2, -sine, sine)
    with jax.named_scope("attention"):
        normed_one, query, pair, gains = project(
            place, inputs, inputs_away, projections, lanes, cosine, sine, []
        )
        cotangent_mine = ring("ring_cotangent", got, [pair])
        cotangent_other = other_core(cotangent_mine)
        quarters.append(along_x(quarters[0], 2))
        pair_away = along_x(pair, 2)
        probs, attended = attend(place, query, pair, pair_away, lengths, offsets, quarters[1:])
        out_mine = gather_x(place, quarters, [pair]).reshape(D, HEADS)
        out_other = other_core(out_mine)
        middle, normed_two, every = branch(
            place, attended, other_core(attended), out_mine, out_other, inputs, gains, got[3:]
        )
    with jax.named_scope("ffn"):
        normed_mine = ring("ring_normed", send_ring(normed_two))
        normed_other = other_core(normed_mine)
        gathered = in_hbm(gathered.reshape(4, 4, 2, ROWS, 3 * HALF))
        rows, grad_mine, grad_other, down_full = ffn_rows(
            normed_mine, normed_other, cotangent_mine, cotangent_other, gathered
        )
        down_full = down_full.reshape(D, HALF)
        shares = scatter_ring("ring_grad", in_hbm(grad_mine), other_core(grad_other))
        wgrad, mark = weight_grads(normed_mine, normed_other, cotangent_mine, cotangent_other, rows, [shares[0]])
        wgrad = pass_on(wgrad, shares[1:])
        summed = lax.psum_scatter(wgrad.reshape(D, 3 * HALF), ("y", "z"), scatter_dimension=0, tiled=True)
    with jax.named_scope("attention_back"):
        middle_grad, two_grad, branch_mine, heads, away = branch_back(
            place, shares, in_hbm(middle), gains, cotangent, in_hbm(out_mine), in_hbm(out_other), [mark]
        )
        received = other_core(away)
        mixed, pair_own, pair_send = attend_back(
            in_hbm(probs),
            in_hbm(query),
            in_hbm(pair),
            in_hbm(pair_away),
            heads,
            received,
            in_hbm(cosine),
            in_hbm(sine),
            [],
        )
        out_grad = out_back(in_hbm(every), branch_mine, received, [mixed])
        one_mine, one_away, attn_shares = project_back(
            place,
            mixed,
            pair_own,
            along_x(pair_send, 2),
            in_hbm(cosine),
            in_hbm(sine),
            in_hbm(projections),
            in_hbm(normed_one),
            inputs,
            inputs_away,
            two_grad,
            out_grad,
            [],
        )
    with jax.named_scope("results"):
        part_other = ffn_back("ffn_out", rows, (2,), [down_full], 1, [one_mine])
        part_mine = ffn_back("ffn_out", rows, (2,), [down_full], 0, [part_other])
        shares, relayed = send_x(attn_shares)
        shares, _ = scatter_b(place, shares)
        output_shares = scatter_ring("ring_output", part_mine, in_hbm(other_core(part_other)), [relayed])
        output = (middle + add(*output_shares)).astype(bf16)
        source = inputs.astype(f32)
        inverse_one = lax.rsqrt(jnp.mean(source * source, axis=1, keepdims=True) + epsilon)
        scaled_one = (one_mine + other_core(one_away)) * gains[:1]
        input_grad = (
            middle_grad
            + inverse_one * scaled_one
            - source * inverse_one**3 * jnp.mean(scaled_one * source, axis=1, keepdims=True)
        )
        keep, gone = part_x_lo(place, in_hbm(summed.reshape(2, ROWS, 3 * HALF)), output_shares[:1])
        *ffn_grads, done = finish_ffn(place, keep, partner_x(gone), output_shares[1:])
        mine, gone = scatter_core(place, scatter_a(place, shares, [*output_shares[:3], keep]), [done])
        qkv_grad, out_grad, extra = finish(place, mine, other_core(gone))
        bias_grad = lax.dynamic_slice(extra, (0, 2 + 16 * place.narrow), (1, 16))[0]
    return (
        output,
        input_grad,
        extra[:, 0],
        qkv_grad,
        bias_grad,
        out_grad,
        extra[:, 1],
        ffn_grads[0],
        ffn_grads[1],
        ffn_grads[2].T,
    )


def solution(mesh):
    split_mesh = Mesh(mesh.devices.reshape(4, 2, 4, 2, 2), BOTH)
    return jax.shard_map(
        per_device,
        mesh=split_mesh,
        in_specs=(
            P(BOTH, None),
            P(BOTH),
            P(BOTH, None),
            P(BOTH),
            P(BOTH, None),
            P(BOTH),
            P(WIDE_AXES, NARROW_AXES),
            P(WIDE_AXES, NARROW_AXES),
            P(NARROW_AXES, WIDE_AXES),
            P(WIDE_AXES, None),
            P(WIDE_AXES, None),
            P(BOTH, None),
        ),
        out_specs=(
            P(BOTH, None),
            P(BOTH, None),
            P(BOTH),
            P(BOTH, None),
            P(BOTH),
            P(BOTH, None),
            P(BOTH),
            P(WIDE_AXES, NARROW_AXES),
            P(WIDE_AXES, NARROW_AXES),
            P(NARROW_AXES, WIDE_AXES),
        ),
        check_vma=False,
    )
```

```python
import math

import jax
import jax.numpy as jnp
from jax import lax
from jax.experimental import pallas as pl
from jax.experimental.pallas import tpu as pltpu
from jax.sharding import Mesh
from jax.sharding import PartitionSpec as P

D = 1536
QH = 12
KVH = 2
HD = 128
FF = 8960
GROUP = QH // KVH
HEADS = GROUP * HD
QKV = HEADS + 2 * HD
HALF = 1152
SPARE = FF // 4 - HALF
EXTRA = 128
WIDE = 32
ROWS = 48
WIDE_AXES = ("y", "x_lo", "z")
NARROW_AXES = ("x_hi", "core")
BOTH = WIDE_AXES + NARROW_AXES
RING = ("x_lo", "x_hi", "core")
epsilon = 1e-06
rope_base = 10000.0
bf16 = jnp.bfloat16
f32 = jnp.float32


def coords(index):
    wide, narrow = divmod(index, 4)
    y, rest = divmod(wide, 8)
    x_lo, z = divmod(rest, 4)
    x_hi, core = divmod(narrow, 2)
    return x_hi * 2 + x_lo, y, z, core


def number_of(x, y, z, core):
    x_hi, x_lo = divmod(x % 4, 2)
    return (((y % 4) * 2 + x_lo) * 4 + z % 4) * 4 + x_hi * 2 + core


def send(value, move):
    pairs = [(i, number_of(*move(*coords(i)))) for i in range(128)]
    return lax.ppermute(value, BOTH, pairs)


def other_core(value):
    return send(value, lambda x, y, z, c: (x, y, z, 1 - c))


def along_x(value, step):
    return send(value, lambda x, y, z, c: (x + step, y, z, c))


def partner_x(value):
    return send(value, lambda x, y, z, c: (x ^ 1, y, z, c))


def along_a(value, step):
    return send(value, lambda x, y, z, c: (x, y, z + step, c) if c == 0 else (x, y + step, z, c))


def along_b(value, step):
    return send(value, lambda x, y, z, c: (x, y + step, z, c) if c == 0 else (x, y, z + step, c))


class Place:
    def __init__(self):
        self.y, self.x_lo, self.z, self.x_hi, self.core = (lax.axis_index(axis) for axis in BOTH)
        self.narrow = self.x_hi * 2 + self.core
        self.x = self.x_hi * 2 + self.x_lo
        first = self.core == 0
        self.a = jnp.where(first, self.z, self.y)
        self.b = jnp.where(first, self.y, self.z)
        self.first = first

    def slot_a(self, x_lo, step):
        at = (self.a + step) % 4
        return jnp.where(self.first, x_lo * 4 + at, at * 2 + x_lo)

    def slot_b(self, j, step):
        at = (self.b + step) % 4
        return jnp.where(self.first, at * 8 + j, j * 4 + at)


STEPS = (0, -1, 1, 2)


def after(value, *others):
    return lax.optimization_barrier((value, *others))[0]


def whole(shape, dtype=bf16):
    return jax.ShapeDtypeStruct(shape, dtype)


def size(*arrays):
    return sum(math.prod(a.shape) * jnp.dtype(a.dtype).itemsize for a in arrays)


def cost(flops, *arrays):
    return pl.CostEstimate(flops=int(flops), bytes_accessed=int(size(*arrays)), transcendentals=0)


SCALARS = pl.BlockSpec(memory_space=pltpu.SMEM)
IN_VMEM = pl.BlockSpec(memory_space=pltpu.VMEM)
TOTAL = QKV + EXTRA + HEADS


def local(name, kernel, scalars, inputs, outs, scratch=(), extra=0, flops=0, wait_for=(), tables=()):
    outs = tuple(outs)
    held = sum(size(s) for s in scratch)
    n, m = len(tables) + len(inputs), len(wait_for)

    def body(at, *refs):
        kernel(at, *refs[:n], *refs[n + m :])

    return pl.pallas_call(
        body,
        out_shape=outs,
        in_specs=[SCALARS] * (1 + len(tables)) + [IN_VMEM] * len(inputs) + [pl.BlockSpec(memory_space=pl.ANY)] * m,
        out_specs=(IN_VMEM,) * len(outs),
        scratch_shapes=list(scratch),
        compiler_params=pltpu.CompilerParams(vmem_limit_bytes=int(size(*inputs, *outs) + held + extra + (2 << 20))),
        cost_estimate=cost(flops, *inputs, *outs),
        name=name,
    )(jnp.stack(scalars).astype(jnp.int32), *tables, *inputs, *wait_for)


def in_hbm(array):
    return pltpu.with_memory_space_constraint(array, pltpu.HBM)


def nothing():
    return [jnp.int32(0)]


PACKED = 2 * ROWS * HEADS // (QKV + EXTRA)


def pack(first, second):
    rows = jnp.concatenate([first, second], axis=0)
    tiles = jnp.concatenate([rows[:, i : i + 128] for i in range(0, HEADS, 128)], axis=0)
    return jnp.concatenate([tiles[i : i + PACKED] for i in range(0, tiles.shape[0], PACKED)], axis=1)


def unpack(packed):
    tiles = jnp.concatenate([packed[:, i : i + 128] for i in range(0, QKV + EXTRA, 128)], axis=0)
    rows = jnp.concatenate([tiles[i : i + 2 * ROWS] for i in range(0, tiles.shape[0], 2 * ROWS)], axis=1)
    return rows[:ROWS], rows[ROWS:]


def gather_a(place, block, wait_for):
    got = [block, *(along_a(block, step) for step in (1, -1, 2))]
    slots = [place.slot_a(x_lo, step) for step in STEPS for x_lo in range(2)]
    width = QKV + EXTRA

    def kernel(at, *refs):
        out, quarter, held = refs[4:]
        for k in range(4):
            for x_lo in range(2):
                slot = at[2 * k + x_lo]
                out[pl.ds(pl.multiple_of(slot * ROWS, ROWS), ROWS), :] = refs[k][x_lo, :, :width]
                held[slot] = refs[k][x_lo, :, width:]
        first, second = held[2 * at[8]], held[2 * at[8] + 1]
        out[8 * ROWS :] = pack(first, second)
        quarter[0], quarter[1] = first, second

    outs = [whole((8 * ROWS + PACKED, width)), whole((2, ROWS, HEADS))]
    scratch = [pltpu.VMEM((8, ROWS, HEADS), bf16)]
    return local("gather_a", kernel, slots + [place.x], got, outs, scratch, 2 << 20, wait_for=wait_for)


def gather_b(place, message, quarter):
    left, right = along_b(message, 1), along_b(message, -1)
    far = along_b(quarter, 2)
    half = 4 * ROWS

    def forward(at, left_ref, right_ref, top, bottom):
        top[...], bottom[...] = left_ref[:half], right_ref[half : 2 * half]

    def collect(at, near_ref, left_ref, right_ref, far_ref, out):
        for k, ref in enumerate((left_ref, right_ref)):
            out[2 * k + 2], out[2 * k + 3] = unpack(ref[2 * half :])
        for i in range(2):
            out[i], out[6 + i] = near_ref[i], far_ref[i]

    top, bottom = local("forward", forward, nothing(), [left, right], [whole((half, QKV + EXTRA))] * 2)
    sent, outs = top, [whole((8, ROWS, HEADS))]
    quarter = local("collect", collect, nothing(), [quarter, left, right, far], outs, (), 2 << 20, wait_for=[top])[0]
    quarters = [quarter, along_x(quarter, 1), along_x(quarter, -1)]
    top, bottom = along_b(top, 1), along_b(bottom, -1)

    def kernel(at, *refs):
        main, extra = refs[5:]
        for k in range(4):
            for j in range(8):
                source, spot = (k, j) if k < 3 else (3 + j // 4, j % 4)
                rows = slice(spot * ROWS, (spot + 1) * ROWS)
                main[at[8 * k + j]] = refs[source][rows, :QKV]
                extra[at[8 * k + j]] = refs[source][rows, QKV:]

    inputs = [message, left, right, top, bottom]
    outs = [whole((WIDE, ROWS, QKV)), whole((WIDE, ROWS, EXTRA))]
    main, extra = local("gather_b", kernel, slots_b(place), inputs, outs, (), 1 << 20)
    return main, extra, quarters, sent


def gather_x(place, quarters, wait_for):
    slots = []
    for back in (0, 1, 3, 2):
        x = (place.x - back) % 4
        slots += [place.slot_b(2 * x + i, step) for step in STEPS for i in range(2)]

    def kernel(at, *refs):
        for n in range(4):
            for k in range(8):
                refs[4][at[8 * n + k]] = refs[n][k]

    return local("gather_x", kernel, slots, quarters, [whole((WIDE, ROWS, HEADS))], wait_for=wait_for)[0]


def add(*terms):
    return sum(t.astype(f32) for t in terms)


def slots_b(place):
    return [place.slot_b(j, step) for step in STEPS for j in range(8)]


def send_x(shares):
    own, left, right, top, bottom = shares
    from_right, from_left = along_x(top, -1), along_x(bottom, 1)

    def kernel(at, left_ref, right_ref, top_ref, bottom_ref, left_out, right_out):
        left_out[:8] = (left_ref[:8].astype(f32) + top_ref[...].astype(f32)).astype(bf16)
        left_out[8:] = left_ref[8:]
        right_out[:8] = right_ref[:8]
        right_out[8:] = (right_ref[8:].astype(f32) + bottom_ref[...].astype(f32)).astype(bf16)

    inputs = [left, right, from_right, from_left]
    left, right = local("relay", kernel, nothing(), inputs, [whole(left.shape)] * 2, (), 4 << 20)
    return [own, along_x(left, -1), along_x(right, 1)], left


def scatter_b(place, shares):
    slots = []
    for step in STEPS:
        at = (place.b + step) % 4
        slots += [jnp.where(place.first, at * 4 + a, a * 4 + at) for a in range(4)]

    def kernel(at, *refs):
        for k in range(4):
            for a in range(4):
                spot = at[4 * k + a]
                total = sum(refs[n][spot].astype(f32) for n in range(3))
                refs[3 + k][a] = total.astype(bf16)

    outs = [whole((4, *shares[0].shape[1:]))] * 4
    own, left, right, opposite = local("scatter_b", kernel, slots, shares, outs, (), 2 << 20)
    return [own, along_b(left, -1), along_b(right, 1), along_b(opposite, 2)], own


def scatter_a(place, shares, wait_for):
    slots = [(place.a + step) % 4 for step in STEPS]

    def kernel(at, *refs):
        for k in range(4):
            total = sum(refs[n][at[k]].astype(f32) for n in range(4))
            refs[4 + k][...] = total.astype(bf16)

    outs = [whole(shares[0].shape[1:])] * 4
    own, left, right, opposite = local("scatter_a", kernel, slots, shares, outs, (), 2 << 20, wait_for=wait_for)
    return [own, along_a(left, -1), along_a(right, 1), along_a(opposite, 2)]


def scatter_core(place, shares, wait_for):
    width = shares[0].shape[1]

    def kernel(at, *refs):
        total = sum(refs[n][...].astype(f32) for n in range(4))
        first, low, high = at[0] == 0, total[:12], total[12:]
        refs[4][...] = jnp.where(first, low, high)
        refs[5][...] = jnp.where(first, high, low).astype(bf16)

    outs = [whole((12, width), f32), whole((12, width))]
    return local("scatter_core", kernel, [place.core], shares, outs, (), 2 << 20, wait_for=wait_for)


def arrange(got, wait_for):
    width = got.shape[2]

    def kernel(at, source, out, rows):
        for x_lo in range(2):
            for k in range(4):
                rows[x_lo, 12 * k : 12 * k + 12, :] = source[x_lo * 4 + k].astype(f32)
        out[...] = rows[...].astype(bf16)

    scratch = [pltpu.VMEM((2, ROWS, width), f32)]
    return local("arrange", kernel, nothing(), [got], [whole((2, ROWS, width))], scratch, wait_for=wait_for)[0]


def finish(place, mine, received):
    def kernel(at, mine_ref, got, qkv, out, extra):
        first, a, b = at[0] == 0, mine_ref[...], got[...].astype(f32)
        low, high = jnp.where(first, a, b), jnp.where(first, b, a)
        qkv[:, :HEADS], qkv[:, HEADS:D] = low[:, :HEADS], high[:, :HEADS]
        for i in range(2):
            cut = slice(HEADS + i * HD, HEADS + (i + 1) * HD)
            at_lane = D + 2 * i * HD
            qkv[:, at_lane : at_lane + HD], qkv[:, at_lane + HD : at_lane + 2 * HD] = low[:, cut], high[:, cut]
        extra[...] = (a + b)[:, QKV : QKV + EXTRA]
        out[:, :HEADS], out[:, HEADS:] = low[:, QKV + EXTRA :], high[:, QKV + EXTRA :]

    outs = (whole((12, 2 * QKV), f32), whole((12, D), f32), whole((12, EXTRA), f32))
    return local("finish", kernel, [place.core], [mine, received], outs)


def send_ring(rows):
    return [rows, along_x(rows, 1), along_x(rows, -1), along_x(rows, 2)]


def ring(name, got, wait_for=()):
    def kernel(at, *refs):
        for k in range(4):
            refs[4][128 * k : 128 * (k + 1)] = refs[k][...]

    return local(name, kernel, nothing(), got, [whole((512, D))], wait_for=wait_for)[0]


def scatter_ring(name, mine, other, wait_for=()):
    def kernel(at, mine_ref, other_ref, own, *rest):
        for k in range(4):
            rows = slice(128 * k, 128 * (k + 1))
            total = mine_ref[rows].astype(f32) + other_ref[rows].astype(f32)
            if k == 0:
                own[...] = total
            else:
                rest[k - 1][...] = total.astype(bf16)

    outs = [whole((128, D), f32)] + [whole((128, D))] * 3
    own, left, right, opposite = local(name, kernel, nothing(), [mine, other], outs, wait_for=wait_for)
    return [own, along_x(left, -1), along_x(right, 1), along_x(opposite, 2)]


def select(first, low, high):
    return jnp.where(first, low.astype(f32), high.astype(f32))


def turn(values, cosine, sine):
    return values * cosine + pltpu.roll(values, HD // 2, 1) * sine


def project(place, inputs, inputs_away, projections, lanes, cosine, sine, wait_for):
    tokens = 256

    def kernel(at, own, away, weight, lane_ref, cos_ref, sin_ref, normed, query, pair, gains):
        first = at[0] == 0
        table = lane_ref[...].astype(f32)
        gains_all = jnp.transpose(table.reshape(D, EXTRA))
        gains[...] = gains_all[:8]
        sums = jnp.sum(table, axis=1)
        left, right = pltpu.roll(sums, EXTRA - 2, 1), pltpu.roll(sums, 62, 1)
        lane = lax.broadcasted_iota(jnp.int32, (1, EXTRA), 1)

        def bias_at(low, high):
            def tile(j):
                return jnp.where(lane < 64, left[2 * j : 2 * j + 1], right[2 * j + 1 : 2 * j + 2])

            return jnp.where(first, tile(low), tile(high))

        for half, ref in enumerate((own, away)):
            rows = slice(128 * half, 128 * (half + 1))
            x = ref[...].astype(f32)
            inverse = lax.rsqrt(jnp.mean(x * x, axis=1, keepdims=True) + epsilon)
            normed[rows] = (x * inverse * gains_all[:1]).astype(bf16)
        cos, sin = cos_ref[...], sin_ref[...]
        mixed = jnp.dot(normed[...], weight[...], preferred_element_type=f32)
        for h in range(GROUP):
            values = mixed[:, h * HD : (h + 1) * HD] + bias_at(h, GROUP + h)
            query[h] = turn(values, cos, sin).astype(bf16)
        key = mixed[:, HEADS : HEADS + HD] + bias_at(12, 13)
        pair[:, :HD] = turn(key, cos, sin).astype(bf16)
        pair[:, HD:] = (mixed[:, HEADS + HD :] + bias_at(14, 15)).astype(bf16)

    outs = [whole((tokens, D)), whole((GROUP, tokens, HD)), whole((tokens, 2 * HD)), whole((8, D), f32)]
    inputs = [inputs, inputs_away, projections, lanes, cosine, sine]
    flops = 2 * tokens * D * QKV
    return local("project", kernel, [place.core], inputs, outs, extra=8 << 20, flops=flops, wait_for=wait_for)


def attend(place, query, pair, pair_away, lengths, offsets, wait_for):
    tokens = 256
    scale = HD**-0.5

    def kernel(at, offset, length, query_ref, own, away, probs, attended):
        core, start = at[0], at[1]
        off_a, off_b, len_a, len_b = offset[0, 0], offset[0, 1], length[0, 0], length[0, 1]

        def slot_of(index, base):
            other = index >= 128
            return base + jnp.where(other, (1 - core) * 128 - 128, core * 128) + index

        def which(slot):
            in_a = (slot >= off_a) & (slot < off_a + len_a)
            in_b = (slot >= off_b) & (slot < off_b + len_b)
            return jnp.where(in_a, 0, jnp.where(in_b, 1, -1))

        rows = slot_of(lax.broadcasted_iota(jnp.int32, (tokens, 1), 0), start)
        lane = lax.broadcasted_iota(jnp.int32, (1, 2 * tokens), 1)
        columns = jnp.where(lane < tokens, slot_of(lane, start), slot_of(lane - tokens, tokens - start))
        number, key_number = which(rows), which(columns)
        allowed = ((number == key_number) & (number >= 0) & (columns <= rows)) | (columns == rows)
        keys = jnp.concatenate([own[:, :HD], away[:, :HD]], axis=0)
        values = jnp.concatenate([own[:, HD:], away[:, HD:]], axis=0)
        for h in range(GROUP):
            scores = lax.dot_general(query_ref[h], keys, (((1,), (1,)), ((), ())), preferred_element_type=f32) * scale
            scores = jnp.where(allowed, scores, -1e30)
            raised = jnp.exp(scores - jnp.max(scores, axis=1, keepdims=True))
            result = raised * (1.0 / jnp.sum(raised, axis=1, keepdims=True))
            probs[h] = result
            attended[:, h * HD : (h + 1) * HD] = jnp.dot(
                result.astype(bf16), values, preferred_element_type=f32
            ).astype(bf16)

    scalars, tables = [place.core, place.x_hi * tokens], [offsets, lengths]
    outs = [whole((GROUP, tokens, 2 * tokens), f32), whole((tokens, HEADS))]
    flops = 8 * GROUP * tokens * tokens * HD
    return local(
        "attend", kernel, scalars, [query, pair, pair_away], outs, (), 6 << 20, flops, wait_for, tables
    )


def branch(place, attended, attended_away, out_mine, out_other, inputs, gains, wait_for):
    def kernel(at, mine, away, weight, weight_away, x_ref, gain, middle, normed, every):
        first = at[0] == 0
        for half, (a, b) in enumerate(((mine[:128], away[128:]), (mine[128:], away[:128]))):
            rows = slice(128 * half, 128 * (half + 1))
            every[rows, :HEADS] = select(first, a, b).astype(bf16)
            every[rows, HEADS:] = select(first, b, a).astype(bf16)
        left = every[:128]
        a = jnp.dot(left, weight[...], preferred_element_type=f32)
        b = jnp.dot(left, weight_away[...], preferred_element_type=f32)
        x = x_ref[...].astype(f32)
        low = x[:, :HEADS] + jnp.where(first, a, b)
        high = x[:, HEADS:] + jnp.where(first, b, a)
        middle[:, :HEADS], middle[:, HEADS:] = low, high
        squares = jnp.sum(low * low, axis=1, keepdims=True) + jnp.sum(high * high, axis=1, keepdims=True)
        inverse = lax.rsqrt(squares * (1.0 / D) + epsilon)
        normed[:, :HEADS] = (low * inverse * gain[1:2, :HEADS]).astype(bf16)
        normed[:, HEADS:] = (high * inverse * gain[1:2, HEADS:]).astype(bf16)

    outs = [whole((128, D), f32), whole((128, D)), whole((256, D))]
    inputs = [attended, attended_away, out_mine, out_other, inputs, gains]
    return local(
        "branch", kernel, [place.core], inputs, outs, extra=6 << 20, flops=2 * 128 * D * D, wait_for=wait_for
    )


def branch_back(place, shares, middle, gains, cotangent, out_mine, out_other, wait_for):
    def kernel(at, own, left, right, opposite, mid_ref, gain, cot, weight, weight_away, grad, gain_grad, mine, heads, away):
        first = at[0] == 0
        total = own[...] + left[...].astype(f32) + right[...].astype(f32) + opposite[...].astype(f32)
        mid = mid_ref[...]
        inverse = lax.rsqrt(jnp.mean(mid * mid, axis=1, keepdims=True) + epsilon)
        scaled = total * gain[1:2]
        mean = jnp.mean(scaled * mid, axis=1, keepdims=True)
        result = cot[...].astype(f32) + inverse * scaled - mid * (inverse * inverse * inverse * mean)
        grad[...] = result
        gain_grad[...] = jnp.sum(total * mid * inverse, axis=0, keepdims=True)
        low, high = result[:, :HEADS], result[:, HEADS:]
        mine[...] = jnp.where(first, low, high).astype(bf16)
        away[:, :HEADS] = jnp.where(first, high, low).astype(bf16)
        back = lax.dot_general(mine[...], weight[...], (((1,), (1,)), ((), ())), preferred_element_type=f32)
        back += lax.dot_general(
            away[:, :HEADS], weight_away[...], (((1,), (1,)), ((), ())), preferred_element_type=f32
        )
        low, high = back[:, :HEADS], back[:, HEADS:]
        heads[...] = jnp.where(first, low, high).astype(bf16)
        away[:, HEADS:] = jnp.where(first, high, low).astype(bf16)

    outs = [whole((128, D), f32), whole((1, D), f32), whole((128, HEADS)), whole((128, HEADS)), whole((128, D))]
    inputs = [*shares, middle, gains, cotangent, out_mine, out_other]
    return local(
        "branch_back", kernel, [place.core], inputs, outs, extra=8 << 20, flops=2 * 128 * D * D, wait_for=wait_for
    )


def attend_back(probs, query, pair, pair_away, heads, received, cosine, sine, wait_for):
    tokens = 256
    scale = HD**-0.5

    def kernel(at, probs_ref, query_ref, own, away, mine, others, cos_ref, sin_ref, mixed, pair_own, pair_send, total):
        keys = jnp.concatenate([own[:, :HD], away[:, :HD]], axis=0)
        values = jnp.concatenate([own[:, HD:], away[:, HD:]], axis=0)
        cos, sin = cos_ref[...], sin_ref[...]
        for h in range(GROUP):
            cut = slice(h * HD, (h + 1) * HD)
            grad = jnp.concatenate([mine[:, cut], others[:, HEADS + h * HD : HEADS + (h + 1) * HD]], axis=0)
            p = probs_ref[h]
            by_prob = lax.dot_general(grad, values, (((1,), (1,)), ((), ())), preferred_element_type=f32)
            row = jnp.sum(p * by_prob, axis=1, keepdims=True)
            by_score = (p * (by_prob - row)).astype(bf16)
            by_query = jnp.dot(by_score, keys, preferred_element_type=f32) * scale
            mixed[:, cut] = turn(by_query, cos, -sin).astype(bf16)
            by_key = lax.dot_general(by_score, query_ref[h], (((0,), (0,)), ((), ())), preferred_element_type=f32)
            by_value = lax.dot_general(p.astype(bf16), grad, (((0,), (0,)), ((), ())), preferred_element_type=f32)
            if h == 0:
                total[:, :HD], total[:, HD:] = by_key * scale, by_value
            else:
                total[:, :HD] += by_key * scale
                total[:, HD:] += by_value
        pair_own[...] = total[:tokens]
        pair_send[...] = total[tokens:].astype(bf16)

    outs = [whole((tokens, HEADS)), whole((tokens, 2 * HD), f32), whole((tokens, 2 * HD))]
    inputs = [probs, query, pair, pair_away, heads, received, cosine, sine]
    scratch = [pltpu.VMEM((2 * tokens, 2 * HD), f32)]
    flops = 20 * GROUP * tokens * tokens * HD
    return local("attend_back", kernel, nothing(), inputs, outs, scratch, 8 << 20, flops, wait_for)


def out_back(every, mine, received, wait_for):
    def kernel(at, every_ref, mine_ref, others, out):
        both = jnp.concatenate([mine_ref[...], others[:, :HEADS]], axis=0)
        for r in range(0, D, 384):
            part = lax.dot_general(
                every_ref[:, r : r + 384], both, (((0,), (0,)), ((), ())), preferred_element_type=f32
            )
            out[r // 24 : r // 24 + 16] = part.reshape(16, 24, HEADS).astype(bf16)

    flops = 2 * 256 * D * HEADS
    inputs = [every, mine, received]
    return local("out_back", kernel, nothing(), inputs, [whole((2 * WIDE, 24, HEADS))], (), 6 << 20, flops, wait_for)[0]


def project_back(place, mixed, pair_own, pair_received, cosine, sine, projections, normed, inputs, inputs_away, two, out,
                 wait_for):
    width = QKV + EXTRA

    def kernel(at, mix, own_ref, got, cos_ref, sin_ref, weight, norm_ref, x_ref, x_away, two_ref, out_ref, mine, away, *rest):
        shares, (held, grads, rows) = rest[:5], rest[5:]
        core = at[4]
        total = own_ref[...] + got[...].astype(f32)
        grads[:, :HEADS] = mix[...]
        grads[:, HEADS : HEADS + HD] = turn(total[:, :HD], cos_ref[...], -sin_ref[...]).astype(bf16)
        grads[:, HEADS + HD :] = total[:, HD:].astype(bf16)
        one = jnp.zeros((1, D), f32)
        for half, (x_from, ref) in enumerate(((x_ref, mine), (x_away, away))):
            part = lax.dot_general(
                grads[128 * half : 128 * (half + 1)],
                weight[...],
                (((1,), (1,)), ((), ())),
                preferred_element_type=f32,
            )
            ref[...] = part
            x = x_from[...].astype(f32)
            inverse = lax.rsqrt(jnp.mean(x * x, axis=1, keepdims=True) + epsilon)
            one += jnp.sum(part * x * inverse, axis=0, keepdims=True)
        for r in range(0, D, 384):
            part = lax.dot_general(
                norm_ref[:, r : r + 384], grads[...], (((0,), (0,)), ((), ())), preferred_element_type=f32
            )
            held[r // 24 : r // 24 + 16, :, :QKV] = part.reshape(16, 24, QKV).astype(bf16)
        rows[...] = jnp.zeros((EXTRA, D), f32)
        rows[0:1], rows[1:2] = one, two_ref[...]
        held[:, :, QKV:] = jnp.transpose(rows[...]).reshape(2 * WIDE, 24, EXTRA).astype(bf16)
        bias = jnp.sum(grads[...].astype(f32), axis=0, keepdims=True)
        lane = lax.broadcasted_iota(jnp.int32, (24, EXTRA), 1)
        row = lax.broadcasted_iota(jnp.int32, (24, EXTRA), 0)
        spot = (lane >= 2) & (lane < 66) & (lax.rem(row, 12) == 0)
        for i in range(8):
            tile = bias[:, i * HD : (i + 1) * HD]
            base = 12 * core + 2 * i if i < GROUP else 24 + 4 * (i - GROUP) + 2 * core
            for odd, shift in ((0, 2), (1, 66)):
                moved = pltpu.roll(tile, shift, 1)
                for half in range(2):
                    at_block = 2 * (base + odd) + half
                    before = held[at_block, :, QKV:].astype(f32)
                    held[at_block, :, QKV:] = jnp.where(spot, moved, before).astype(bf16)
        for k in range(4):
            for n in range(16):
                ref, spot = (shares[k], n) if k < 3 else (shares[3 + n // 8], n % 8)
                source = at[k] + n // 4 * 16 + n % 4 * 2
                ref[spot, :, :width] = held[source]
                ref[spot, :, width:] = out_ref[source]

    outs = [whole((128, D), f32)] * 2 + [whole((n, 24, TOTAL)) for n in (16, 16, 16, 8, 8)]
    scratch = [pltpu.VMEM((2 * WIDE, 24, width), bf16), pltpu.VMEM((256, QKV), bf16), pltpu.VMEM((EXTRA, D), f32)]
    inputs = [mixed, pair_own, pair_received, cosine, sine, projections, normed, inputs, inputs_away, two, out]
    scalars = [x % 2 * 8 + x // 2 for x in ((place.x + step) % 4 for step in STEPS)] + [place.core]
    flops = 4 * 256 * D * QKV
    mine, away, *shares = local("project_back", kernel, scalars, inputs, outs, scratch, 14 << 20, flops, wait_for)
    return mine, away, shares


def prepare_attention(place, qkv_weight, out_weight, norm_one, norm_two, qkv_bias):
    def kernel(at, qkv, out, one, two, bias, result):
        narrow = at[0]
        lane = lax.broadcasted_iota(jnp.int32, (12, EXTRA), 1)
        row = lax.broadcasted_iota(jnp.int32, (12, EXTRA), 0)
        diagonal = lax.broadcasted_iota(jnp.int32, (12, 12), 0) == lax.broadcasted_iota(jnp.int32, (12, 12), 1)

        def column(gain):
            return jnp.sum(jnp.where(diagonal, gain[...].astype(f32), 0.0), axis=1, keepdims=True)

        extra = jnp.where(lane == 0, column(one), 0.0) + jnp.where(lane == 1, column(two), 0.0)
        spread = jnp.concatenate([bias[...].astype(f32)] * 8, axis=1)
        base = 2 + 16 * narrow
        shifted = pltpu.roll(spread, 2, 1)
        extra = extra + jnp.where((row == 0) & (lane >= base) & (lane < base + 16), shifted, 0.0)
        extra = extra.astype(bf16)
        for k in range(8):
            c = k % 2
            result[k, :, :HEADS] = qkv[:, c * HEADS : (c + 1) * HEADS]
            for i in range(2):
                at_lane = D + (2 * i + c) * HD
                result[k, :, HEADS + i * HD : HEADS + (i + 1) * HD] = qkv[:, at_lane : at_lane + HD]
            result[k, :, QKV : QKV + EXTRA] = extra
            result[k, :, QKV + EXTRA :] = out[:, c * HEADS : (c + 1) * HEADS]

    inputs = [
        in_hbm(a)
        for a in (qkv_weight, out_weight, norm_one.reshape(1, 12), norm_two.reshape(1, 12), qkv_bias.reshape(1, 16))
    ]
    return local("prepare_attention", kernel, [place.narrow], inputs, [whole((8, 12, TOTAL))])[0]


def prepare_ffn(place, weights):
    def kernel(at, gate, up, down, mine, other):
        zero = at[0] == 0
        for i, weight in enumerate((gate, up, down)):
            low = weight[:, :HALF].astype(f32)
            high = jnp.concatenate([weight[:, HALF:].astype(f32), jnp.zeros((ROWS, HALF - SPARE), f32)], axis=1)
            mine[:, i * HALF : (i + 1) * HALF] = jnp.where(zero, low, high).astype(bf16)
            other[:, i * HALF : (i + 1) * HALF] = jnp.where(zero, high, low).astype(bf16)

    outs = (whole((ROWS, 3 * HALF)),) * 2
    return local("prepare_ffn", kernel, [place.x_lo], [in_hbm(w) for w in weights], outs)


def by_x_lo(place, mine, other, wait_for):
    def kernel(at, mine_ref, other_ref, out):
        out[at[0]] = mine_ref[...]
        out[1 - at[0]] = other_ref[...]

    return local("by_x_lo", kernel, [place.x_lo], [mine, other], [whole((2, *mine.shape))], wait_for=wait_for)[0]


def part_x_lo(place, both, wait_for):
    def kernel(at, source, mine, other):
        mine[...] = source[at[0]]
        other[...] = source[1 - at[0]]

    return local("part_x_lo", kernel, [place.x_lo], [both], [whole(both.shape[1:])] * 2, wait_for=wait_for)


def finish_ffn(place, keep, gone, wait_for):
    def kernel(at, keep_ref, gone_ref, *outs):
        zero, (*outs, mark) = at[0] == 0, outs
        mark[...] = jnp.zeros((8, 128), f32)
        for i, out in enumerate(outs):
            a = keep_ref[:, i * HALF : (i + 1) * HALF].astype(f32)
            b = gone_ref[:, i * HALF : (i + 1) * HALF].astype(f32)
            out[:, :HALF] = jnp.where(zero, a, b)
            out[:, HALF:] = jnp.where(zero, b, a)[:, :SPARE]

    outs = [whole((ROWS, HALF + SPARE), f32)] * 3 + [whole((8, 128), f32)]
    return local("finish_ffn", kernel, [place.x_lo], [keep, gone], outs, wait_for=wait_for)


def ffn_rows(x_mine, x_other, c_mine, c_other, gathered):
    half, step = x_mine.shape[0], 256
    chunks = 2 * half // step
    tokens = (x_mine, x_other, c_mine, c_other)

    def kernel(*refs):
        far_tokens, source, rows, mine, other, down = refs[:4], *refs[4:9]
        weights, held, near, grads, sems, token_sems, out_sems, row_sems, grad_sems = refs[9:]
        loads = [[] for _ in range(3)]
        token_loads = [pltpu.make_async_copy(far_tokens[i], near.at[i], token_sems.at[i]) for i in range(4)]

        def load_weight(m):
            for y in range(4):
                for x_lo in range(2):
                    load = pltpu.make_async_copy(
                        source.at[y, :, x_lo, :, pl.ds(m * HALF, HALF)],
                        weights.at[m, pl.ds(y * 8 + x_lo * 4, 4)],
                        sems.at[(m * 4 + y) * 2 + x_lo],
                    )
                    load.start()
                    loads[m].append(load)

        token_loads[0].start()
        load_weight(0)
        load_weight(1)
        token_loads[2].start()
        load_weight(2)
        token_loads[1].start()
        token_loads[3].start()
        per_side = half // step

        def store_chunk(n, side, here, start):
            there = pl.ds(pl.multiple_of(n * step, step), step)
            for i in range(3):
                copy = pltpu.make_async_copy(held.at[i, there], rows.at[i, there], row_sems.at[3 * n + i])
                copy.start() if start else copy.wait()
            for k, out in enumerate((mine, other)):

                @pl.when(side == k)
                def _():
                    copy = pltpu.make_async_copy(grads.at[there], out.at[here], grad_sems.at[n])
                    copy.start() if start else copy.wait()

        def chunk(n, _):
            side, here = n // per_side, pl.ds(pl.multiple_of(lax.rem(n, per_side) * step, step), step)
            there = pl.ds(pl.multiple_of(n * step, step), step)
            products = []
            for m in range(3):
                i = side if m < 2 else 2 + side

                @pl.when(n == 0)
                def _():
                    for load in loads[m] + [token_loads[0 if m < 2 else 2]] * (m != 1):
                        load.wait()

                @pl.when(n == per_side)
                def _():
                    for load in [token_loads[1 if m < 2 else 3]] * (m != 1):
                        load.wait()

                products.append(jnp.dot(near[i, here], weights[m].reshape(D, HALF), preferred_element_type=f32))
            gate, upward, grad = products
            sigmoid = 1.0 / (1.0 + jnp.exp(-gate))
            silu = gate * sigmoid
            held[0, there] = (grad * upward * (sigmoid * (1.0 + gate * (1.0 - sigmoid)))).astype(bf16)
            held[1, there] = (grad * silu).astype(bf16)
            held[2, there] = (silu * upward).astype(bf16)
            back = sum(
                lax.dot_general(
                    held[m, there], weights[m].reshape(D, HALF), (((1,), (1,)), ((), ())), preferred_element_type=f32
                )
                for m in range(2)
            )
            grads[there] = back.astype(bf16)
            store_chunk(n, side, here, True)

            @pl.when(n == 0)
            def _():
                down_store.start()

            return 0

        down_store = pltpu.make_async_copy(weights.at[2], down, out_sems.at[0])
        lax.fori_loop(0, chunks, chunk, 0)
        down_store.wait()
        for n in range(chunks):
            store_chunk(n, n // per_side, pl.ds(n % per_side * step, step), False)

    outs = (
        pltpu.HBM((3, 2 * half, HALF), bf16),
        pltpu.HBM((half, D), bf16),
        pltpu.HBM((half, D), bf16),
        pltpu.HBM((WIDE, ROWS, HALF), bf16),
    )
    return pl.pallas_call(
        kernel,
        out_shape=outs,
        in_specs=[pl.BlockSpec(memory_space=pl.ANY)] * 5,
        out_specs=(pl.BlockSpec(memory_space=pl.ANY),) * 4,
        scratch_shapes=[
            pltpu.VMEM((3, WIDE, ROWS, HALF), bf16),
            pltpu.VMEM((3, 2 * half, HALF), bf16),
            pltpu.VMEM((4, half, D), bf16),
            pltpu.VMEM((2 * half, D), bf16),
            pltpu.SemaphoreType.DMA((24,)),
            pltpu.SemaphoreType.DMA((4,)),
            pltpu.SemaphoreType.DMA((1,)),
            pltpu.SemaphoreType.DMA((3 * chunks,)),
            pltpu.SemaphoreType.DMA((chunks,)),
        ],
        compiler_params=pltpu.CompilerParams(vmem_limit_bytes=40 << 20),
        cost_estimate=cost(20 * half * D * HALF, *tokens, gathered),
        name="ffn_rows",
    )(*(in_hbm(t) for t in tokens), gathered)


def ffn_back(name, rows, parts, weights, half, wait_for=()):
    count, pairs = rows.shape[1] // 2, len(parts)
    n, cut = 3, D // 3

    def kernel(*refs):
        out = refs[-1]
        for r in range(0, count, 256):
            out[r : r + 256] = sum(
                lax.dot_general(
                    refs[i][0, r : r + 256], refs[pairs + i][...], (((1,), (1,)), ((), ())), preferred_element_type=f32
                )
                for i in range(pairs)
            ).astype(bf16)

    out = whole((count, D))
    return pl.pallas_call(
        kernel,
        grid=(n,),
        out_shape=out,
        in_specs=[pl.BlockSpec((1, count, HALF), lambda j, m=m: (m, half, 0)) for m in parts]
        + [pl.BlockSpec((cut, HALF), lambda j: (j, 0))] * pairs
        + [pl.BlockSpec(memory_space=pl.ANY)] * len(wait_for),
        out_specs=pl.BlockSpec((count, cut), lambda j: (0, j)),
        compiler_params=pltpu.CompilerParams(vmem_limit_bytes=20 << 20),
        cost_estimate=cost(2 * pairs * count * D * HALF, out, out, out),
        name=name,
    )(*([in_hbm(rows)] * pairs), *(in_hbm(w) for w in weights), *wait_for)


def weight_grads(x_mine, x_other, c_mine, c_other, rows, wait_for):
    count = x_mine.shape[0]

    def kernel(xa, xb, ca, cb, r, *refs):
        out, mark = refs[-2:]
        mark[...] = jnp.zeros((8, 128), f32)

        def products(a, b):
            left = jnp.concatenate([a[...], b[...]], axis=0)
            part = lax.dot_general(left, r[0], (((0,), (0,)), ((), ())), preferred_element_type=f32).astype(bf16)
            for w in range(WIDE):
                y, rest = divmod(w, 8)
                x_lo, z = divmod(rest, 4)
                out[y * 8 + z * 2 + x_lo] = part[w * ROWS : (w + 1) * ROWS]

        @pl.when(pl.program_id(0) < 2)
        def _():
            products(xa, xb)

        @pl.when(pl.program_id(0) == 2)
        def _():
            products(ca, cb)

    left_spec = pl.BlockSpec((count, D), lambda m: (0, 0), pipeline_mode=pl.Buffered(1))
    return pl.pallas_call(
        kernel,
        grid=(3,),
        out_shape=(pltpu.HBM((WIDE, ROWS, 3 * HALF), bf16), whole((8, 128), f32)),
        in_specs=[left_spec] * 4
        + [pl.BlockSpec((1, 2 * count, HALF), lambda m: (m, 0, 0))]
        + [pl.BlockSpec(memory_space=pl.ANY)] * len(wait_for),
        out_specs=(
            pl.BlockSpec((WIDE, ROWS, HALF), lambda m: (0, 0, m)),
            pl.BlockSpec((8, 128), lambda m: (0, 0)),
        ),
        compiler_params=pltpu.CompilerParams(vmem_limit_bytes=46 << 20),
        cost_estimate=cost(12 * count * D * HALF, rows),
        name="weight_grads",
    )(*(in_hbm(v) for v in (x_mine, x_other, c_mine, c_other, rows)), *wait_for)


def pass_on(array, wait_for):
    def kernel(*refs):
        pass

    return pl.pallas_call(
        kernel,
        out_shape=pltpu.HBM(array.shape, array.dtype),
        in_specs=[pl.BlockSpec(memory_space=pl.ANY)] * (1 + len(wait_for)),
        out_specs=pl.BlockSpec(memory_space=pl.ANY),
        input_output_aliases={0: 0},
        compiler_params=pltpu.CompilerParams(vmem_limit_bytes=1 << 20),
        name="pass_on",
    )(in_hbm(array), *wait_for)


def rope_tables(position):
    halfway = HD // 2
    inverse = rope_base ** (-jnp.arange(halfway, dtype=f32) * 2.0 / HD)
    angles = position.astype(f32)[:, None] * inverse[None, :]
    angles = jnp.concatenate([angles, angles], axis=1)
    return jnp.cos(angles), jnp.sin(angles)


def dot(left, right, dims):
    return lax.dot_general(left, right, (dims, ((), ())), preferred_element_type=f32)


def per_device(
    inputs,
    norm_one,
    qkv_weight,
    qkv_bias,
    out_weight,
    norm_two,
    gate_weight,
    up_weight,
    down_weight,
    lengths,
    offsets,
    cotangent,
):
    place = Place()
    own = inputs.shape[0]
    zero = place.x_lo == 0
    with jax.named_scope("weights"):
        mine, other = prepare_ffn(place, (gate_weight, up_weight, down_weight.T))
        other = partner_x(other)
        blocks = prepare_attention(place, qkv_weight, out_weight, norm_one, norm_two, qkv_bias)
        blocks = lax.all_to_all(blocks, RING, 0, 0, tiled=True)
        inputs_away = other_core(inputs)
        got = send_ring(cotangent)
        message, quarter = gather_a(place, arrange(blocks, [inputs_away]), got[1:3])
        projections, lanes, quarters, sent = gather_b(place, message, quarter)
        block = pass_on(by_x_lo(place, mine, other, [message]), [sent])
        gathered = lax.all_gather(block.reshape(2 * ROWS, 3 * HALF), ("y", "z"), axis=0, tiled=True)
        projections = projections.reshape(D, QKV)
    with jax.named_scope("layout"):
        start = place.x_hi * 2 * own
        ramp = jnp.arange(own, dtype=jnp.int32)
        slots = jnp.concatenate([start + place.core * own + ramp, start + (1 - place.core) * own + ramp])
        inside = (slots[:, None] >= offsets[0][None, :]) & (slots[:, None] < (offsets[0] + lengths[0])[None, :])
        position = jnp.sum(jnp.where(inside, slots[:, None] - offsets[0][None, :], 0), axis=1)
        cosine, sine = rope_tables(position)
        sine = jnp.where(jnp.arange(HD)[None, :] < HD // 2, -sine, sine)
    with jax.named_scope("attention"):
        normed_one, query, pair, gains = project(
            place, inputs, inputs_away, projections, lanes, cosine, sine, []
        )
        cotangent_mine = ring("ring_cotangent", got, [pair])
        cotangent_other = other_core(cotangent_mine)
        quarters.append(along_x(quarters[0], 2))
        pair_away = along_x(pair, 2)
        probs, attended = attend(place, query, pair, pair_away, lengths, offsets, quarters[1:])
        out_mine = gather_x(place, quarters, [pair]).reshape(D, HEADS)
        out_other = other_core(out_mine)
        middle, normed_two, every = branch(
            place, attended, other_core(attended), out_mine, out_other, inputs, gains, got[3:]
        )
    with jax.named_scope("ffn"):
        normed_mine = ring("ring_normed", send_ring(normed_two))
        normed_other = other_core(normed_mine)
        gathered = in_hbm(gathered.reshape(4, 4, 2, ROWS, 3 * HALF))
        rows, grad_mine, grad_other, down_full = ffn_rows(
            normed_mine, normed_other, cotangent_mine, cotangent_other, gathered
        )
        down_full = down_full.reshape(D, HALF)
        shares = scatter_ring("ring_grad", in_hbm(grad_mine), other_core(grad_other))
        wgrad, mark = weight_grads(normed_mine, normed_other, cotangent_mine, cotangent_other, rows, [shares[0]])
        wgrad = pass_on(wgrad, shares[1:])
        summed = lax.psum_scatter(wgrad.reshape(D, 3 * HALF), ("y", "z"), scatter_dimension=0, tiled=True)
    with jax.named_scope("attention_back"):
        middle_grad, two_grad, branch_mine, heads, away = branch_back(
            place, shares, in_hbm(middle), gains, cotangent, in_hbm(out_mine), in_hbm(out_other), [mark]
        )
        received = other_core(away)
        mixed, pair_own, pair_send = attend_back(
            in_hbm(probs),
            in_hbm(query),
            in_hbm(pair),
            in_hbm(pair_away),
            heads,
            received,
            in_hbm(cosine),
            in_hbm(sine),
            [],
        )
        out_grad = out_back(in_hbm(every), branch_mine, received, [mixed])
        one_mine, one_away, attn_shares = project_back(
            place,
            mixed,
            pair_own,
            along_x(pair_send, 2),
            in_hbm(cosine),
            in_hbm(sine),
            in_hbm(projections),
            in_hbm(normed_one),
            inputs,
            inputs_away,
            two_grad,
            out_grad,
            [],
        )
    with jax.named_scope("results"):
        part_other = ffn_back("ffn_out", rows, (2,), [down_full], 1, [one_mine])
        part_mine = ffn_back("ffn_out", rows, (2,), [down_full], 0, [part_other])
        shares, relayed = send_x(attn_shares)
        shares, _ = scatter_b(place, shares)
        output_shares = scatter_ring("ring_output", part_mine, in_hbm(other_core(part_other)), [relayed])
        output = (middle + add(*output_shares)).astype(bf16)
        source = inputs.astype(f32)
        inverse_one = lax.rsqrt(jnp.mean(source * source, axis=1, keepdims=True) + epsilon)
        scaled_one = (one_mine + other_core(one_away)) * gains[:1]
        input_grad = (
            middle_grad
            + inverse_one * scaled_one
            - source * inverse_one**3 * jnp.mean(scaled_one * source, axis=1, keepdims=True)
        )
        keep, gone = part_x_lo(place, in_hbm(summed.reshape(2, ROWS, 3 * HALF)), output_shares[:1])
        *ffn_grads, done = finish_ffn(place, keep, partner_x(gone), output_shares[1:])
        mine, gone = scatter_core(place, scatter_a(place, shares, [*output_shares[:2], keep]), [done])
        qkv_grad, out_grad, extra = finish(place, mine, other_core(gone))
        bias_grad = lax.dynamic_slice(extra, (0, 2 + 16 * place.narrow), (1, 16))[0]
    return (
        output,
        input_grad,
        extra[:, 0],
        qkv_grad,
        bias_grad,
        out_grad,
        extra[:, 1],
        ffn_grads[0],
        ffn_grads[1],
        ffn_grads[2].T,
    )


def solution(mesh):
    split_mesh = Mesh(mesh.devices.reshape(4, 2, 4, 2, 2), BOTH)
    return jax.shard_map(
        per_device,
        mesh=split_mesh,
        in_specs=(
            P(BOTH, None),
            P(BOTH),
            P(BOTH, None),
            P(BOTH),
            P(BOTH, None),
            P(BOTH),
            P(WIDE_AXES, NARROW_AXES),
            P(WIDE_AXES, NARROW_AXES),
            P(NARROW_AXES, WIDE_AXES),
            P(WIDE_AXES, None),
            P(WIDE_AXES, None),
            P(BOTH, None),
        ),
        out_specs=(
            P(BOTH, None),
            P(BOTH, None),
            P(BOTH),
            P(BOTH, None),
            P(BOTH),
            P(BOTH, None),
            P(BOTH),
            P(WIDE_AXES, NARROW_AXES),
            P(WIDE_AXES, NARROW_AXES),
            P(NARROW_AXES, WIDE_AXES),
        ),
        check_vma=False,
    )
```
